128 devices in a mesh: ctx: 16 (over z, y_hi, core), tp: 8 (over y_lo, x).
Axes of the slice: x: 4, y: 4 (y_hi: 2, y_lo: 2; y = y_hi * 2 + y_lo), z: 4, core: 2. Of those that a mesh axis runs over, the one named last changes fastest.
Arguments:
- token_ids: int32 [16384], P('ctx'), may hold values from 0 to 16383
- embed_table: bfloat16 [16384, 2048], P(None, 'tp'), may hold values from -10 to 10
- latents: bfloat16 [2048, 2048], P('ctx', 'tp'), may hold values from -60 to 60
- w_query: bfloat16 [2048, 2048], P(None, 'tp'), may hold values from -1 to 1
- w_key: bfloat16 [2048, 2048], P(None, 'tp'), may hold values from -1 to 1
- w_value: bfloat16 [2048, 2048], P(None, 'tp'), may hold values from -0.125 to 0.125
- w_out: bfloat16 [2048, 2048], P('tp'), may hold values from -0.125 to 0.125
- out_grad: bfloat16 [2048, 2048], P('ctx', 'tp'), may hold values from -6 to 6
- offsets: int32 [2048], replicated, may hold values from 0 to 16383, as said below
Outputs:
- cross_out: bfloat16 [2048, 2048], P('ctx', 'tp')
- latent_grad: bfloat16 [2048, 2048], P('ctx', 'tp')
- key_grad: float32 [2048, 2048], P('ctx', 'tp')
- value_grad: float32 [2048, 2048], P('ctx', 'tp')
The draws below stay inside these ranges and needn't reach their ends.
Inputs may be any that keep to these rules, and one draw needn't show every extreme that they name: `offsets`: nondecreasing along the latents; the first latent's offset is 0 and the last one's is 16383.
All inputs are finite; a program needn't handle non-finite values.
Results may differ from the reference program's by a relative error of at most 0.027.
The reference program's roundings to bfloat16 on the way (of `context`, `probs_low`, `attended`, `attended_grad`, `score_grad`, `query_grad`, `key_out_grad` and `value_out_grad`) count: a program that leaves them out, or rounds other values in their place, can miss the bound.
Values may be sent and summed in bfloat16 or wider, within the bound.
No kernel may reach another device: no remote copies, remote signals or barrier semaphores. Data moves between devices by JAX's collectives and lax.ppermute only.
A program may use at most 128 MiB of HBM per device.

```python
import math
import jax
import jax.numpy as jnp
import numpy as np
from jax import lax

HEADS = 16
HEAD_DIM = 128
D = 2048
VOCAB = 16384
LATENTS = 2048
CTX = 16384


def draw_embed_table(key, part):
    key = jax.random.fold_in(key, 3)
    drawn = jnp.clip(jax.random.normal(key, (VOCAB, D), jnp.float32), -4.0, 4.0)
    return drawn.astype(jnp.bfloat16)


def draw_latents(key, part):
    key = jax.random.fold_in(key, 5)
    drawn = 3.0 * jnp.clip(jax.random.normal(key, (LATENTS, D), jnp.float32), -4.0, 4.0)
    return drawn.astype(jnp.bfloat16)


def draw_w_query(key, part):
    key = jax.random.fold_in(key, 7)
    drawn = jnp.clip(jax.random.normal(key, (D, D), jnp.float32), -4.0, 4.0) * D ** (-0.5)
    return drawn.astype(jnp.bfloat16)


def draw_w_key(key, part):
    key = jax.random.fold_in(key, 9)
    drawn = jnp.clip(jax.random.normal(key, (D, D), jnp.float32), -4.0, 4.0) * D ** (-0.5)
    return drawn.astype(jnp.bfloat16)


def draw_offsets(key, part):
    key = jax.random.fold_in(key, 11)
    drawn = jax.random.randint(key, (LATENTS,), 0, CTX, dtype=jnp.int32)
    ordered = jnp.sort(drawn)
    row_index = jnp.arange(LATENTS)
    ordered = jnp.where(row_index == 0, 0, ordered)
    ordered = jnp.where(row_index == LATENTS - 1, CTX - 1, ordered)
    return ordered.astype(jnp.int32)


def with_ends(values, key, low, largest):
    extent = values.shape
    spot = [jax.random.randint(jax.random.fold_in(key, axis), (), 0, extent[axis]) for axis in range(len(extent))]
    values = values.at[tuple(spot)].set(low)
    longest = extent.index(max(extent))
    spot[longest] = (spot[longest] + 1) % extent[longest]
    return values.at[tuple(spot)].set(largest)


def level_of(stream_key, shape, split, least, top_value):
    factor_of = 1.0
    for position, shards_of in split:
        steps = jax.random.uniform(jax.random.fold_in(jax.random.fold_in(stream_key, 6), position), (shards_of,), jnp.float32, least / len(split), top_value / len(split))
        factor_of = factor_of * jnp.repeat(jnp.exp(steps), shape[position] // shards_of).reshape((-1,) + (1,) * (len(shape) - 1 - position))
    return factor_of


def rank_bounds(count, skew):
    loads = [(1 << 20) // math.isqrt(rank ** skew) + 1 for rank in range(1, count + 1)]
    spread = 1 + sum(loads) // (1 << 30)
    return np.cumsum(np.array([max(1, weight // spread) for weight in loads]))


def ranked(rng, dims, amount, slope):
    listing = rank_bounds(amount, slope)
    ticket = jax.random.randint(jax.random.fold_in(rng, 1), dims, 0, int(listing[amount - 1]))
    grade = jnp.searchsorted(jnp.asarray(listing, jnp.int32), ticket, side="right")
    return jax.random.permutation(jax.random.fold_in(rng, 2), amount)[grade].astype(jnp.int32)


def normal_values(own_key, extent, spread, limit, cuts=(), kind=jnp.bfloat16):
    array = spread * jax.random.normal(own_key, extent, jnp.float32)
    if cuts:
        array = array * level_of(own_key, extent, cuts, -0.22, 0.18)
    return jnp.clip(array, -limit, limit).astype(kind)


def setup_inputs(seed: int = 0) -> dict:
    key_of = jax.random.split(jax.random.key(seed), 10)
    token_ids = with_ends(ranked(key_of[0], (CTX,), VOCAB, 2), jax.random.fold_in(key_of[0], 3), 0, VOCAB - 1).astype(jnp.int32)
    embed_table = draw_embed_table(jax.random.fold_in(key_of[9], 71), 0)
    latents = draw_latents(jax.random.fold_in(key_of[9], 71), 0)
    w_query = draw_w_query(jax.random.fold_in(key_of[9], 71), 0)
    w_key = draw_w_key(jax.random.fold_in(key_of[9], 71), 0)
    w_value = normal_values(key_of[5], (D, D), D ** -0.5, 0.125, ((1, 8),))
    w_out = normal_values(key_of[6], (D, D), D ** -0.5, 0.125, ((0, 8),))
    out_grad = normal_values(key_of[7], (LATENTS, D), 1.0, 6.0, ((0, 16), (1, 8)))
    offsets = draw_offsets(jax.random.fold_in(key_of[9], 71), 0)
    return dict(token_ids=token_ids, embed_table=embed_table, latents=latents, w_query=w_query, w_key=w_key, w_value=w_value, w_out=w_out, out_grad=out_grad, offsets=offsets)


masked_value = -1e+30

def by_head(matrix, count):
    return matrix.reshape(count, HEADS, HEAD_DIM).transpose(1, 0, 2)

def reference(token_ids, embed_table, latents, w_query, w_key, w_value, w_out, out_grad, offsets):
    score_scale = 1.0 / math.sqrt(HEAD_DIM)
    context = jnp.take(embed_table, token_ids, axis=0)
    queries = jnp.dot(latents, w_query, preferred_element_type=jnp.float32).astype(jnp.bfloat16)
    key_rows = jnp.dot(context, w_key, preferred_element_type=jnp.float32).astype(jnp.bfloat16)
    value_rows = jnp.dot(context, w_value, preferred_element_type=jnp.float32).astype(jnp.bfloat16)
    block_rows = min(512, LATENTS)
    block_count = LATENTS // block_rows
    positions = jnp.arange(CTX, dtype=jnp.int32)
    query_heads = by_head(queries, LATENTS)
    key_heads = by_head(key_rows, CTX)
    value_heads = by_head(value_rows, CTX)
    offset_blocks = offsets.reshape(block_count, block_rows)

    def head_forward(inputs):
        query_head, key_head, value_head = inputs
        key_wide = key_head.astype(jnp.float32)

        def one_block(pieces):
            query_blk, offset_blk = pieces
            scores = jnp.dot(query_blk.astype(jnp.float32), key_wide.T, precision=lax.Precision.HIGHEST) * score_scale
            visible = positions[None, :] <= offset_blk[:, None]
            peak_score = lax.optimization_barrier(jnp.max(jnp.where(visible, scores, masked_value), axis=1))
            exp_total = lax.optimization_barrier(jnp.sum(jnp.exp(jnp.where(visible, scores - peak_score[:, None], masked_value)), axis=1))
            log_total = peak_score + jnp.log(exp_total)
            probs_low = jnp.exp(jnp.where(visible, scores - log_total[:, None], masked_value)).astype(jnp.bfloat16)
            attended_blk = jnp.dot(probs_low, value_head, preferred_element_type=jnp.float32)
            return (attended_blk, log_total)
        outputs, totals = lax.map(one_block, (query_head.reshape(block_count, block_rows, HEAD_DIM), offset_blocks))
        return (outputs.reshape(LATENTS, HEAD_DIM), totals.reshape(LATENTS))
    head_out, head_total = lax.map(head_forward, (query_heads, key_heads, value_heads))
    attended = head_out.transpose(1, 0, 2).reshape(LATENTS, D).astype(jnp.bfloat16)
    cross_out = jnp.dot(attended, w_out, preferred_element_type=jnp.float32).astype(jnp.bfloat16)
    attended_grad = jnp.dot(out_grad, w_out.T, preferred_element_type=jnp.float32).astype(jnp.bfloat16)
    grad_heads = by_head(attended_grad, LATENTS)
    row_delta = lax.optimization_barrier(jnp.sum(grad_heads.astype(jnp.float32) * by_head(attended, LATENTS).astype(jnp.float32), axis=2))

    def head_backward(inputs):
        query_head, key_head, value_head, grad_head, total_head, delta_head = inputs
        key_wide = key_head.astype(jnp.float32)
        value_wide = value_head.astype(jnp.float32)

        def one_block(carry, pieces):
            key_acc, value_acc = carry
            query_blk, offset_blk, grad_blk, total_blk, delta_blk = pieces
            scores = jnp.dot(query_blk.astype(jnp.float32), key_wide.T, precision=lax.Precision.HIGHEST) * score_scale
            visible = positions[None, :] <= offset_blk[:, None]
            probs = jnp.exp(jnp.where(visible, scores - total_blk[:, None], masked_value))
            prob_grad = jnp.dot(grad_blk.astype(jnp.float32), value_wide.T, precision=lax.Precision.HIGHEST)
            score_grad = (probs * (prob_grad - delta_blk[:, None]) * score_scale).astype(jnp.bfloat16)
            query_part = jnp.dot(score_grad, key_head, preferred_element_type=jnp.float32)
            key_acc = key_acc + jnp.dot(score_grad.T, query_blk, preferred_element_type=jnp.float32)
            value_acc = value_acc + jnp.dot(probs.astype(jnp.bfloat16).T, grad_blk, preferred_element_type=jnp.float32)
            return ((key_acc, value_acc), query_part)
        zero_acc = jnp.zeros((CTX, HEAD_DIM), jnp.float32)
        pieces = (query_head.reshape(block_count, block_rows, HEAD_DIM), offset_blocks, grad_head.reshape(block_count, block_rows, HEAD_DIM), total_head.reshape(block_count, block_rows), delta_head.reshape(block_count, block_rows))
        (key_acc, value_acc), query_parts = lax.scan(one_block, (zero_acc, zero_acc), pieces)
        return (key_acc, value_acc, query_parts.reshape(LATENTS, HEAD_DIM))
    key_acc, value_acc, query_acc = lax.map(head_backward, (query_heads, key_heads, value_heads, grad_heads, head_total, row_delta))
    query_grad = query_acc.transpose(1, 0, 2).reshape(LATENTS, D).astype(jnp.bfloat16)
    latent_grad = jnp.dot(query_grad, w_query.T, preferred_element_type=jnp.float32).astype(jnp.bfloat16)
    key_out_grad = key_acc.transpose(1, 0, 2).reshape(CTX, D).astype(jnp.bfloat16)
    value_out_grad = value_acc.transpose(1, 0, 2).reshape(CTX, D).astype(jnp.bfloat16)
    key_grad = jnp.dot(context.T, key_out_grad, preferred_element_type=jnp.float32)
    value_grad = jnp.dot(context.T, value_out_grad, preferred_element_type=jnp.float32)
    return (cross_out, latent_grad, key_grad, value_grad)
```

```python
import math

import jax
import jax.numpy as jnp
from jax import lax
from jax.experimental import pallas as pl
from jax.experimental.pallas import tpu as pltpu
from jax.sharding import PartitionSpec as P

HEAD_DIM = 128
CTX_DEVICES = 16
TP_DEVICES = 8
FEATURES = 256
HEADS_HERE = FEATURES // HEAD_DIM
ROWS = 128
PAIRS = CTX_DEVICES // 2
PAIR_ROWS = 2 * ROWS
CHUNK = 512
HALF = CHUNK // 2

SCORE_SCALE = 1.0 / math.sqrt(HEAD_DIM)
LOG2_SCALE = SCORE_SCALE * math.log2(math.e)
MASKED = -1e30
FLOOR = -1e29

NN = (((1,), (0,)), ((), ()))
NT = (((1,), (1,)), ((), ()))
TN = (((0,), (0,)), ((), ()))

bf16 = jnp.bfloat16
f32 = jnp.float32


def mm(left, right, dims=NN):
    return lax.dot_general(left, right, dims, preferred_element_type=f32)


def swap(value, axis, bits):
    count = CTX_DEVICES if axis == "ctx" else TP_DEVICES
    return lax.ppermute(value, axis, [(i, i ^ bits) for i in range(count)])


def exchange(value, axis, groups=None):
    return lax.all_to_all(value, axis, 0, 0, axis_index_groups=groups, tiled=True)


def to_all(value, axis):
    count = CTX_DEVICES if axis == "ctx" else TP_DEVICES
    return exchange(jnp.broadcast_to(value[None], (count,) + value.shape), axis)


def whole(shape):
    return pl.BlockSpec(shape, lambda i: (0,) * len(shape), pipeline_mode=pl.Buffered(1))


def kernel_call(body, outs, scalars, arrays, scratch=(), flops=0):
    moved = sum(a.size * a.dtype.itemsize for a in arrays)
    moved += sum(math.prod(shape) * jnp.dtype(kind).itemsize for shape, kind in outs)
    call = pl.pallas_call(
        body,
        grid=(1,),
        out_shape=[jax.ShapeDtypeStruct(shape, kind) for shape, kind in outs],
        in_specs=[pl.BlockSpec(memory_space=pltpu.SMEM)] * len(scalars)
        + [whole(a.shape) for a in arrays],
        out_specs=[whole(shape) for shape, _ in outs],
        scratch_shapes=list(scratch),
        compiler_params=pltpu.CompilerParams(vmem_limit_bytes=40 * 1024 * 1024),
        cost_estimate=pl.CostEstimate(flops=flops, bytes_accessed=moved, transcendentals=0),
    )
    return list(call(*scalars, *arrays))


def gather_tp(block):
    half = block.shape[0] // 2
    near = swap(block, "tp", 1)
    back = swap(block, "tp", 3)
    side = swap(block, "tp", 4)
    far_top = swap(near[:half], "tp", 3)
    far_low = swap(back[half:], "tp", 1)
    side_near = swap(side, "tp", 1)
    side_back = swap(side, "tp", 3)
    side_far_top = swap(far_top, "tp", 4)
    side_far_low = swap(far_low, "tp", 4)
    return [
        block, near, far_top, far_low, back,
        side, side_near, side_far_top, side_far_low, side_back,
    ]


def whole_blocks(refs):
    return [
        refs[0][...],
        refs[1][...],
        jnp.concatenate([refs[2][...], refs[3][...]], axis=0),
        refs[4][...],
        refs[5][...],
        refs[6][...],
        jnp.concatenate([refs[7][...], refs[8][...]], axis=0),
        refs[9][...],
    ]


def shard_start(tp_index, r):
    return pl.multiple_of((tp_index ^ r) * FEATURES, FEATURES)


def head_of(h):
    return slice(h * HEAD_DIM, (h + 1) * HEAD_DIM)


def rows_body(w_query, w_out, blocks, out):
    query = jnp.zeros((ROWS, FEATURES), f32)
    grads = [jnp.zeros((HEAD_DIM, ROWS), f32) for _ in range(HEADS_HERE)]
    for r in range(TP_DEVICES):
        part = slice(r * FEATURES, (r + 1) * FEATURES)
        query += mm(blocks[r, :ROWS, :], w_query[part, :])
        for h in range(HEADS_HERE):
            grads[h] += mm(w_out[head_of(h), part], blocks[r, ROWS:, :], NT)
    out[:ROWS, :] = query.astype(bf16)
    for h in range(HEADS_HERE):
        out[ROWS:, head_of(h)] = grads[h].astype(bf16)


def project_body(info, w_key, w_value, *refs):
    key_out, value_out = refs[-2:]
    tp_index = info[0]
    context = jnp.concatenate(whole_blocks(refs[:-2]), axis=1)
    for weight, out in ((w_key, key_out), (w_value, value_out)):
        ordered = jnp.concatenate(
            [weight[pl.ds(shard_start(tp_index, r), FEATURES), :] for r in range(TP_DEVICES)],
            axis=0,
        )
        out[...] = mm(context, ordered).astype(bf16)


def pair_query(rows, p, h):
    return jnp.concatenate(
        [rows[2 * p, :ROWS, head_of(h)], rows[2 * p + 1, :ROWS, head_of(h)]], axis=0
    )


def pair_grad(rows, p, h):
    return jnp.concatenate(
        [rows[2 * p, ROWS:, head_of(h)], rows[2 * p + 1, ROWS:, head_of(h)]], axis=1
    )


def visible_in(base, offset_row):
    places = base + lax.broadcasted_iota(jnp.int32, (CHUNK, PAIR_ROWS), 0)
    return places <= offset_row


def turned(value):
    return value.astype(f32).T.astype(bf16)


def forward_body(chunk, info, limits, offsets, rows, keys, values, *refs):
    earlier = refs[:2] if chunk else None
    stats, parts = refs[-3:-1]
    values_t = refs[-1]
    base = info[1 + chunk]
    for h in range(HEADS_HERE):
        values_t[head_of(h), :] = turned(values[:, head_of(h)])

    def step(p, carry):
        seen = limits[p] >= base

        @pl.when(seen)
        def _():
            visible = visible_in(base, offsets[p])
            for h in range(HEADS_HERE):
                scores = mm(keys[:, head_of(h)], pair_query(rows, p, h), NT) * LOG2_SCALE
                scores = jnp.where(visible, scores, MASKED)
                peak = jnp.maximum(jnp.max(scores, axis=0, keepdims=True), FLOOR)
                weights = jnp.exp2(scores - peak)
                total = jnp.sum(weights, axis=0, keepdims=True)
                some = total > 0.0
                safe = jnp.where(some, total, 1.0)
                part = mm(values_t[head_of(h), :], weights.astype(bf16))
                part = part * jnp.where(some, 1.0 / safe, 0.0)
                level = jnp.where(some, peak + jnp.log2(safe), MASKED)
                delta = jnp.sum(
                    part * pair_grad(rows, p, h).astype(f32), axis=0, keepdims=True
                )
                if chunk:
                    old = earlier[0][p, h : h + 1, :]
                    old_part = earlier[1][p, head_of(h), :]
                    top = jnp.maximum(level, old)
                    mine, theirs = jnp.exp2(level - top), jnp.exp2(old - top)
                    both = mine + theirs
                    mine, theirs = mine / both, theirs / both
                    level = top + jnp.log2(both)
                    delta = mine * delta + theirs * earlier[0][p, h + 2 : h + 3, :]
                    part = mine * part + theirs * old_part
                stats[p, h : h + 1, :] = level
                stats[p, h + 2 : h + 3, :] = delta
                parts[p, head_of(h), :] = part

        @pl.when(jnp.logical_not(seen))
        def _():
            if chunk:
                stats[p] = earlier[0][p]
                parts[p] = earlier[1][p]
            else:
                stats[p, :2, :] = jnp.full((2, PAIR_ROWS), MASKED, f32)
                stats[p, 2:, :] = jnp.zeros((2, PAIR_ROWS), f32)
                parts[p] = jnp.zeros((FEATURES, PAIR_ROWS), f32)

        return carry

    lax.fori_loop(0, PAIRS, step, 0)


def split_parity(core, value):
    low, high = value[:, :ROWS], value[:, ROWS:]
    return jnp.where(core == 1, high, low), jnp.where(core == 1, low, high)


def join_body(info, everyone, local, parts, stats, own, other):
    core = info[3] & 1
    for p in range(PAIRS):
        pieces = [everyone[i, p] for i in range(CTX_DEVICES)]
        top = pieces[0][:2]
        for piece in pieces[1:]:
            top = jnp.maximum(top, piece[:2])
        total = jnp.zeros((2, PAIR_ROWS), f32)
        delta = jnp.zeros((2, PAIR_ROWS), f32)
        for piece in pieces:
            weight = jnp.exp2(piece[:2] - top)
            total += weight
            delta += weight * piece[2:]
        level = top + jnp.log2(total)
        stats[p, :2, :] = level
        stats[p, 2:, :] = delta / total
        weight = jnp.exp2(local[p][:2] - level)
        for h in range(HEADS_HERE):
            mine, theirs = split_parity(core, parts[p, head_of(h), :] * weight[h : h + 1, :])
            own[p, head_of(h), :] = mine
            other[p, head_of(h), :] = theirs.astype(bf16)


def backward_body(info, limits, offsets, rows, key_a, value_a, key_b, value_b, stats, *refs):
    both, own, other, key_acc, value_acc, keys_t, query_acc = refs
    for h in range(HEADS_HERE):
        backward_head(
            h, info, limits, offsets, rows, key_a, value_a, key_b, value_b, stats,
            both, key_acc, value_acc, keys_t, query_acc,
        )
        for p in range(PAIRS):
            mine, theirs = split_parity(info[3] & 1, query_acc[p])
            own[p, head_of(h), :] = mine
            other[p, head_of(h), :] = theirs.astype(bf16)


def backward_head(
    h, info, limits, offsets, rows, key_a, value_a, key_b, value_b, stats,
    both, key_acc, value_acc, keys_t, query_acc,
):
    query_acc[...] = jnp.zeros(query_acc.shape, f32)
    for chunk, keys, values in ((0, key_a, value_a), (1, key_b, value_b)):
        base = info[1 + chunk]
        key_acc[...] = jnp.zeros(key_acc.shape, f32)
        value_acc[...] = jnp.zeros(value_acc.shape, f32)
        keys_t[...] = turned(keys[:, head_of(h)])

        def step(p, carry):
            @pl.when(limits[p] >= base)
            def _():
                visible = visible_in(base, offsets[p])
                query = pair_query(rows, p, h)
                grad_t = pair_grad(rows, p, h)
                scores = mm(keys[:, head_of(h)], query, NT) * LOG2_SCALE
                probs = jnp.exp2(jnp.where(visible, scores - stats[p, h : h + 1, :], MASKED))
                prob_grad = mm(values[:, head_of(h)], grad_t)
                score_grad = (
                    probs * (prob_grad - stats[p, h + 2 : h + 3, :]) * SCORE_SCALE
                ).astype(bf16)
                value_acc[...] += mm(probs.astype(bf16), grad_t, NT)
                key_acc[...] += mm(score_grad, query)
                query_acc[p] += mm(keys_t[...], score_grad)

            return carry

        lax.fori_loop(0, PAIRS, step, 0)
        span = slice(chunk * CHUNK, (chunk + 1) * CHUNK)
        both[span, head_of(h)] = key_acc[...].astype(bf16)
        both[span, head_of(HEADS_HERE + h)] = value_acc[...].astype(bf16)


def weight_body(info, both, *refs):
    own, other = refs[-2:]
    tp_index = info[0]
    flipped = (info[3] & 1) == 1
    first = whole_blocks(refs[:10])
    second = whole_blocks(refs[10:20])
    for r in range(TP_DEVICES):
        terms = mm(first[r], both[:CHUNK, :], TN) + mm(second[r], both[CHUNK:, :], TN)
        place = tp_index ^ r
        low, high = terms[:ROWS], terms[ROWS:]
        own[place] = jnp.where(flipped, high, low)
        other[place] = jnp.where(flipped, low, high).astype(bf16)


def add_body(own, received, out):
    out[...] = (own[...] + received[...].astype(f32)).astype(bf16)


def sum_ctx(own, other):
    received = swap(other, "ctx", 1)
    added = kernel_call(add_body, [(own.shape, bf16)], [], [own, received])[0]
    groups = [list(range(core, CTX_DEVICES, 2)) for core in range(2)]
    return exchange(added, "ctx", groups)


def total_of(terms):
    total = terms[0].astype(f32)
    for i in range(1, terms.shape[0]):
        total = total + terms[i].astype(f32)
    return total


def cross_body(w_out, terms, out):
    attended = total_of(terms).T.astype(bf16)
    for r in range(TP_DEVICES):
        out[r] = mm(attended, w_out[:, r * FEATURES : (r + 1) * FEATURES]).astype(bf16)


def latent_body(w_query, terms, out):
    query_grad = total_of(terms).T.astype(bf16)
    for r in range(TP_DEVICES):
        part = w_query[r * FEATURES : (r + 1) * FEATURES, :]
        out[r] = mm(query_grad, part, NT).astype(bf16)


def sum_tp(body, weight, terms):
    flops = 2 * ROWS * FEATURES * FEATURES * TP_DEVICES
    shape = (TP_DEVICES, ROWS, FEATURES)
    blocks = kernel_call(body, [(shape, bf16)], [], [weight, terms], flops=flops)[0]
    return total_of(exchange(blocks, "tp")).astype(bf16)


def shards(token_ids, embed_table, latents, w_query, w_key, w_value, w_out, out_grad, offsets):
    ctx_index = lax.axis_index("ctx").astype(jnp.int32)
    tp_index = lax.axis_index("tp").astype(jnp.int32)
    key_count = token_ids.shape[0]

    mirror_ids = swap(token_ids[CHUNK:], "ctx", CTX_DEVICES - 1)
    base_a = ctx_index * key_count
    base_b = (CTX_DEVICES - 1 - ctx_index) * key_count + CHUNK
    info = jnp.stack([tp_index, base_a, base_b, ctx_index])
    limits = jnp.max(offsets.reshape(PAIRS, PAIR_ROWS), axis=1)
    near_offsets = offsets.reshape(PAIRS, 1, PAIR_ROWS)

    blocks = to_all(jnp.concatenate([latents, out_grad], axis=0), "tp")
    own = kernel_call(
        rows_body,
        [((2 * ROWS, FEATURES), bf16)],
        [],
        [w_query, w_out, blocks],
        flops=2 * 2 * ROWS * 2048 * FEATURES,
    )[0]
    rows = to_all(own, "ctx")

    contexts, keys, values = [], [], []
    for ids in (token_ids[:CHUNK], mirror_ids):
        local = embed_table.at[ids].get(mode="promise_in_bounds")
        blocks = gather_tp(local)
        key, value = kernel_call(
            project_body,
            [((CHUNK, FEATURES), bf16)] * 2,
            [info],
            [w_key, w_value] + blocks,
            flops=2 * 2 * CHUNK * 2048 * FEATURES,
        )
        contexts.append(blocks)
        keys.append(key)
        values.append(value)

    unit = 2 * CHUNK * 2048 * FEATURES // 2
    part_shape = (PAIRS, FEATURES, ROWS)
    stats_shape = (PAIRS, 4, PAIR_ROWS)
    state = []
    for chunk in range(2):
        state = kernel_call(
            lambda *refs, chunk=chunk: forward_body(chunk, *refs),
            [(stats_shape, f32), ((PAIRS, FEATURES, PAIR_ROWS), f32)],
            [info, limits],
            [near_offsets, rows, keys[chunk], values[chunk]] + state,
            scratch=[pltpu.VMEM((FEATURES, CHUNK), bf16)],
            flops=4 * unit,
        )
    local, parts = state

    stats, own_out, other_out = kernel_call(
        join_body,
        [(stats_shape, f32), (part_shape, f32), (part_shape, bf16)],
        [info],
        [to_all(local, "ctx"), local, parts],
    )

    attended_terms = sum_ctx(own_out, other_out)
    cross_out = sum_tp(cross_body, w_out, attended_terms)

    both, own_query, other_query = kernel_call(
        backward_body,
        [((2 * CHUNK, 2 * FEATURES), bf16), (part_shape, f32), (part_shape, bf16)],
        [info, limits],
        [near_offsets, rows, keys[0], values[0], keys[1], values[1], stats],
        scratch=[
            pltpu.VMEM((CHUNK, HEAD_DIM), f32),
            pltpu.VMEM((CHUNK, HEAD_DIM), f32),
            pltpu.VMEM((HEAD_DIM, CHUNK), bf16),
            pltpu.VMEM((PAIRS, HEAD_DIM, PAIR_ROWS), f32),
        ],
        flops=20 * unit,
    )
    query_terms = sum_ctx(own_query, other_query)
    block_shape = (PAIRS, ROWS, 2 * FEATURES)
    own_weight, other_weight = kernel_call(
        weight_body,
        [(block_shape, f32), (block_shape, bf16)],
        [info],
        [both] + contexts[0] + contexts[1],
        flops=4 * 2 * CHUNK * 2048 * FEATURES,
    )
    weight_grad = total_of(sum_ctx(own_weight, other_weight))
    latent_grad = sum_tp(latent_body, w_query, query_terms)
    return (cross_out, latent_grad, weight_grad[:, :FEATURES], weight_grad[:, FEATURES:])


def solution(mesh):
    placed = (
        P("ctx"),
        P(None, "tp"),
        P("ctx", "tp"),
        P(None, "tp"),
        P(None, "tp"),
        P(None, "tp"),
        P("tp", None),
        P("ctx", "tp"),
        P(),
    )
    return jax.shard_map(
        shards,
        mesh=mesh,
        in_specs=placed,
        out_specs=(P("ctx", "tp"), P("ctx", "tp"), P("ctx", "tp"), P("ctx", "tp")),
        check_vma=False,
    )
```

```python
import math

import jax
import jax.numpy as jnp
from jax import lax
from jax.experimental import pallas as pl
from jax.experimental.pallas import tpu as pltpu
from jax.sharding import PartitionSpec as P

HEAD_DIM = 128
CTX_DEVICES = 16
TP_DEVICES = 8
FEATURES = 256
HEADS_HERE = FEATURES // HEAD_DIM
ROWS = 128
CHIPS = CTX_DEVICES // 2
GROUPS = 4
GROUP_ROWS = 4 * ROWS
SPAN = 512

SCORE_SCALE = 1.0 / math.sqrt(HEAD_DIM)
LOG2_SCALE = SCORE_SCALE * math.log2(math.e)
MASKED = -1e30
FLOOR = -1e29

NN = (((1,), (0,)), ((), ()))
NT = (((1,), (1,)), ((), ()))
TN = (((0,), (0,)), ((), ()))

bf16 = jnp.bfloat16
f32 = jnp.float32


def mm(left, right, dims=NN):
    return lax.dot_general(left, right, dims, preferred_element_type=f32)


def swap(value, axis, bits):
    count = CTX_DEVICES if axis == "ctx" else TP_DEVICES
    return lax.ppermute(value, axis, [(i, i ^ bits) for i in range(count)])


def exchange(value, axis, groups=None):
    return lax.all_to_all(value, axis, 0, 0, axis_index_groups=groups, tiled=True)


def whole(shape):
    return pl.BlockSpec(shape, lambda i: (0,) * len(shape), pipeline_mode=pl.Buffered(1))


def kernel_call(body, outs, scalars, arrays, unfetched=(), scratch=(), flops=0, room=60):
    moved = sum(a.size * a.dtype.itemsize for a in [*unfetched, *arrays])
    moved += sum(math.prod(shape) * jnp.dtype(kind).itemsize for shape, kind in outs)
    call = pl.pallas_call(
        body,
        grid=(1,),
        out_shape=[jax.ShapeDtypeStruct(shape, kind) for shape, kind in outs],
        in_specs=[pl.BlockSpec(memory_space=pltpu.SMEM)] * len(scalars)
        + [pl.BlockSpec(memory_space=pl.ANY)] * len(unfetched)
        + [whole(a.shape) for a in arrays],
        out_specs=[whole(shape) for shape, _ in outs],
        scratch_shapes=list(scratch),
        compiler_params=pltpu.CompilerParams(vmem_limit_bytes=room * 1024 * 1024),
        cost_estimate=pl.CostEstimate(flops=flops, bytes_accessed=moved, transcendentals=0),
    )
    return list(call(*scalars, *unfetched, *arrays))


def gather_tp_first(block):
    return swap(block, "tp", 1), swap(block, "tp", 3), swap(block, "tp", 4)


def gather_tp_rest(block, first):
    near, back, side = first
    side_near = swap(near, "tp", 4)
    side_back = swap(side, "tp", 3)
    far = swap(back, "tp", 1)
    side_far = swap(side_near, "tp", 3)
    return [block, near, far, back, side, side_near, side_far, side_back]


def gather_ctx(block):
    two = jnp.stack([block, swap(block, "ctx", 2)])
    even = jnp.concatenate([two] + [swap(two, "ctx", code) for code in (4, 8, 12)], axis=0)
    return [even, swap(even, "ctx", 1)]


def shard_start(tp_index, r):
    return pl.multiple_of((tp_index ^ r) * FEATURES, FEATURES)


def head_of(h):
    return slice(h * HEAD_DIM, (h + 1) * HEAD_DIM)


def rows_body(info, w_query, w_out, *refs):
    blocks, out = refs[:-1], refs[-1]
    query = jnp.zeros((ROWS, FEATURES), f32)
    grads = [jnp.zeros((HEAD_DIM, ROWS), f32) for _ in range(HEADS_HERE)]
    for r in range(TP_DEVICES):
        part = pl.ds(shard_start(info[0], r), FEATURES)
        query += mm(blocks[r][:ROWS, :], w_query[part, :])
        for h in range(HEADS_HERE):
            grads[h] += mm(w_out[head_of(h), part], blocks[r][ROWS:, :], NT)
    out[:ROWS, :] = query.astype(bf16)
    for h in range(HEADS_HERE):
        out[ROWS:, head_of(h)] = grads[h].astype(bf16)


def row_copies(even, odd, rows, arrived):
    return [
        pltpu.make_async_copy(even, rows.at[0], arrived.at[0]),
        pltpu.make_async_copy(odd, rows.at[1], arrived.at[1]),
    ]


def row_block(rows, ctx_index, block):
    return rows.at[(ctx_index ^ block) & 1, (ctx_index ^ block) >> 1]


def group_query(rows, ctx_index, group, h):
    blocks = [row_block(rows, ctx_index, GROUPS * group + i) for i in range(GROUPS)]
    return jnp.concatenate([block[:ROWS, head_of(h)] for block in blocks], axis=0)


def group_grad(rows, ctx_index, group, h):
    blocks = [row_block(rows, ctx_index, GROUPS * group + i) for i in range(GROUPS)]
    return jnp.concatenate([block[ROWS:, head_of(h)] for block in blocks], axis=1)


def visible_in(base, offset_row):
    places = base + lax.broadcasted_iota(jnp.int32, (SPAN, GROUP_ROWS), 0)
    return places <= offset_row


def turned(value):
    return value.astype(f32).T.astype(bf16)


def span_of(i):
    return slice(i * SPAN, (i + 1) * SPAN)


def forward_body(info, limits, even, odd, offsets, w_key, w_value, *refs):
    keys, values, stats, parts, values_t, rows, arrived = refs[TP_DEVICES:]
    copies = row_copies(even, odd, rows, arrived)
    for copy in copies:
        copy.start()
    ctx_index = info[1]
    context = jnp.concatenate([ref[...] for ref in refs[:TP_DEVICES]], axis=1)
    for weight, out in ((w_key, keys), (w_value, values)):
        ordered = jnp.concatenate(
            [weight[pl.ds(shard_start(info[0], r), FEATURES), :] for r in range(TP_DEVICES)],
            axis=0,
        )
        out[...] = mm(context, ordered).astype(bf16)
    for h in range(HEADS_HERE):
        values_t[head_of(h), :] = turned(values[:, head_of(h)])
    for copy in copies:
        copy.wait()

    def step(group, carry):
        stats[group, :2, :] = jnp.full((2, GROUP_ROWS), MASKED, f32)
        stats[group, 2:, :] = jnp.zeros((2, GROUP_ROWS), f32)
        parts[group] = jnp.zeros((FEATURES, GROUP_ROWS), f32)
        for i in range(2):
            base = info[2 + i]

            @pl.when(limits[group] >= base)
            def _():
                visible = visible_in(base, offsets[group])
                for h in range(HEADS_HERE):
                    query = group_query(rows, ctx_index, group, h)
                    scores = mm(keys[span_of(i), head_of(h)], query, NT) * LOG2_SCALE
                    scores = jnp.where(visible, scores, MASKED)
                    old = stats[group, h : h + 1, :]
                    peak = jnp.maximum(jnp.max(scores, axis=0, keepdims=True), FLOOR)
                    peak = jnp.maximum(peak, old)
                    weights = jnp.exp2(scores - peak)
                    keep = jnp.exp2(old - peak)
                    total = keep * stats[group, h + 2 : h + 3, :]
                    total += jnp.sum(weights, axis=0, keepdims=True)
                    part = mm(values_t[head_of(h), span_of(i)], weights.astype(bf16))
                    parts[group, head_of(h), :] = keep * parts[group, head_of(h), :] + part
                    stats[group, h : h + 1, :] = peak
                    stats[group, h + 2 : h + 3, :] = total

        for h in range(HEADS_HERE):
            total = stats[group, h + 2 : h + 3, :]
            some = total > 0.0
            safe = jnp.where(some, total, 1.0)
            part = parts[group, head_of(h), :] * jnp.where(some, 1.0 / safe, 0.0)
            grad_t = group_grad(rows, ctx_index, group, h).astype(f32)
            level = jnp.where(some, stats[group, h : h + 1, :] + jnp.log2(safe), MASKED)
            stats[group, h : h + 1, :] = level
            stats[group, h + 2 : h + 3, :] = jnp.sum(part * grad_t, axis=0, keepdims=True)
            parts[group, head_of(h), :] = part
        return carry

    lax.fori_loop(0, GROUPS, step, 0)


def joined(refs, group):
    pieces = [ref[group] for ref in refs]
    top = pieces[0][:2]
    for piece in pieces[1:]:
        top = jnp.maximum(top, piece[:2])
    total = jnp.zeros((2, GROUP_ROWS), f32)
    delta = jnp.zeros((2, GROUP_ROWS), f32)
    for piece in pieces:
        weight = jnp.exp2(piece[:2] - top)
        total += weight
        delta += weight * piece[2:]
    return top + jnp.log2(total), delta / total


def join_body(own, one, two, three, stats):
    for group in range(GROUPS):
        level, delta = joined((own, one, two, three), group)
        stats[group, :2, :] = level
        stats[group, 2:, :] = delta


def split_parity(core, group, value, mine, other):
    for i in range(GROUPS // 2):
        low = value[:, 2 * i * ROWS : (2 * i + 1) * ROWS]
        high = value[:, (2 * i + 1) * ROWS : (2 * i + 2) * ROWS]
        chip = group * (GROUPS // 2) + i
        mine[chip] = jnp.where(core == 1, high, low)
        other[chip] = jnp.where(core == 1, low, high).astype(bf16)


def join_scale_body(own, one, two, three, local, parts, stats, blocks):
    for group in range(GROUPS):
        level, delta = joined((own, one, two, three), group)
        stats[group, :2, :] = level
        stats[group, 2:, :] = delta
        weight = jnp.exp2(local[group][:2] - level)
        for h in range(HEADS_HERE):
            scaled = (parts[group, head_of(h), :] * weight[h : h + 1, :]).astype(bf16)
            for i in range(GROUPS):
                place = GROUPS * group + i
                blocks[place, head_of(h), :] = scaled[:, i * ROWS : (i + 1) * ROWS]


def backward_body(info, limits, even, odd, offsets, keys, values, stats, *refs):
    both, mine, other, key_acc, value_acc, keys_t, query_acc, rows, arrived = refs
    copies = row_copies(even, odd, rows, arrived)
    for copy in copies:
        copy.start()
    ctx_index = info[1]
    query_acc[...] = jnp.zeros(query_acc.shape, f32)
    key_acc[...] = jnp.zeros(key_acc.shape, f32)
    value_acc[...] = jnp.zeros(value_acc.shape, f32)
    for h in range(HEADS_HERE):
        keys_t[head_of(h), :] = turned(keys[:, head_of(h)])
    for copy in copies:
        copy.wait()

    def step(group, carry):
        for i in range(2):
            base = info[2 + i]
            span = span_of(i)

            @pl.when(limits[group] >= base)
            def _():
                visible = visible_in(base, offsets[group])
                for h in range(HEADS_HERE):
                    query = group_query(rows, ctx_index, group, h)
                    grad_t = group_grad(rows, ctx_index, group, h)
                    scores = mm(keys[span, head_of(h)], query, NT) * LOG2_SCALE
                    scores = jnp.where(visible, scores - stats[group, h : h + 1, :], MASKED)
                    probs = jnp.exp2(scores)
                    prob_grad = mm(values[span, head_of(h)], grad_t)
                    delta = stats[group, h + 2 : h + 3, :]
                    score_grad = (probs * (prob_grad - delta) * SCORE_SCALE).astype(bf16)
                    value_acc[span, head_of(h)] += mm(probs.astype(bf16), grad_t, NT)
                    key_acc[span, head_of(h)] += mm(score_grad, query)
                    query_acc[group, head_of(h), :] += mm(keys_t[head_of(h), span], score_grad)

        return carry

    lax.fori_loop(0, GROUPS, step, 0)
    both[:, :FEATURES] = key_acc[...].astype(bf16)
    both[:, FEATURES:] = value_acc[...].astype(bf16)
    for group in range(GROUPS):
        split_parity(ctx_index & 1, group, query_acc[group], mine, other)


def weight_body(info, both, *refs):
    mine, other = refs[-2:]
    flipped = (info[1] & 1) == 1
    for r in range(TP_DEVICES):
        terms = mm(refs[r][...], both[...], TN)
        place = info[0] ^ r
        low, high = terms[:ROWS], terms[ROWS:]
        mine[place] = jnp.where(flipped, high, low)
        other[place] = jnp.where(flipped, low, high).astype(bf16)


def add_body(own, received, out):
    out[...] = (own[...] + received[...].astype(f32)).astype(bf16)


def sum_ctx(own, other):
    received = swap(other, "ctx", 1)
    added = kernel_call(add_body, [(own.shape, bf16)], [], [own, received], room=16)[0]
    groups = [list(range(core, CTX_DEVICES, 2)) for core in range(2)]
    return exchange(added, "ctx", groups)


def spread_z_body(info, own, received, kept, one, two, three):
    z = info[1] >> 2
    for y in range(2):
        place = 2 * z + y
        kept[y] = own[place] + received[place].astype(f32)
        for code, out in ((1, one), (2, two), (3, three)):
            place = 2 * (z ^ code) + y
            out[y] = (own[place] + received[place].astype(f32)).astype(bf16)


def spread_y_body(info, own, one, two, three, kept, sent):
    y = (info[1] >> 1) & 1
    for place, out in ((y, kept), (1 - y, sent)):
        total = own[place]
        for term in (one, two, three):
            total += term[place].astype(f32)
        out[...] = total.astype(out.dtype)


def sum_ctx_staged(info, own, other):
    shape = own.shape[1:]
    kept, *sent = kernel_call(
        spread_z_body,
        [((2,) + shape, f32)] + [((2,) + shape, bf16)] * 3,
        [info],
        [own, swap(other, "ctx", 1)],
        room=16,
    )
    terms = [swap(block, "ctx", 4 * code) for code, block in zip((1, 2, 3), sent)]
    kept, sent = kernel_call(
        spread_y_body, [(shape, f32), (shape, bf16)], [info], [kept] + terms, room=16
    )
    return kept, swap(sent, "ctx", 2)


def total_of(terms):
    total = terms[0].astype(f32)
    for i in range(1, terms.shape[0]):
        total = total + terms[i].astype(f32)
    return total


def close_body(info, w_out, w_query, attended_terms, query_kept, query_rest, *outs):
    attended = total_of(attended_terms).T.astype(bf16)
    query_grad = (query_kept[...] + query_rest[...].astype(f32)).T.astype(bf16)
    for r in range(TP_DEVICES):
        part = pl.ds(shard_start(info[0], r), FEATURES)
        cross = mm(attended, w_out[:, part])
        latent = mm(query_grad, w_query[part, :], NT)
        outs[r][:, :FEATURES] = cross.astype(outs[r].dtype)
        outs[r][:, FEATURES:] = latent.astype(outs[r].dtype)


def shards(token_ids, embed_table, latents, w_query, w_key, w_value, w_out, out_grad, offsets):
    ctx_index = lax.axis_index("ctx").astype(jnp.int32)
    tp_index = lax.axis_index("tp").astype(jnp.int32)
    key_count = token_ids.shape[0]

    mirror_ids = swap(token_ids[SPAN:], "ctx", CTX_DEVICES - 1)
    info = jnp.stack(
        [
            tp_index,
            ctx_index,
            ctx_index * key_count,
            (CTX_DEVICES - 1 - ctx_index) * key_count + SPAN,
        ]
    )
    limits = jnp.max(offsets.reshape(GROUPS, GROUP_ROWS), axis=1)
    offset_rows = offsets.reshape(GROUPS, 1, GROUP_ROWS)

    row_part = jnp.concatenate([latents, out_grad], axis=0)
    row_first = gather_tp_first(row_part)
    ids = jnp.concatenate([token_ids[:SPAN], mirror_ids])
    context_part = embed_table.at[ids].get(mode="promise_in_bounds")
    row_first, context_part = lax.optimization_barrier((row_first, context_part))
    row_blocks = gather_tp_rest(row_part, row_first)
    context = gather_tp_rest(context_part, gather_tp_first(context_part))

    own = kernel_call(
        rows_body,
        [((2 * ROWS, FEATURES), bf16)],
        [info],
        [w_query, w_out] + row_blocks,
        flops=2 * 2 * ROWS * 2048 * FEATURES,
    )[0]
    rows = gather_ctx(own)

    unit = 2 * SPAN * 2048 * FEATURES
    part_shape = (CHIPS, FEATURES, ROWS)
    stats_shape = (GROUPS, 4, GROUP_ROWS)
    rows_scratch = [
        pltpu.VMEM((2, CHIPS, 2 * ROWS, FEATURES), bf16),
        pltpu.SemaphoreType.DMA((2,)),
    ]
    keys, values, local, parts = kernel_call(
        forward_body,
        [
            ((2 * SPAN, FEATURES), bf16),
            ((2 * SPAN, FEATURES), bf16),
            (stats_shape, f32),
            ((GROUPS, FEATURES, GROUP_ROWS), f32),
        ],
        [info, limits],
        [offset_rows, w_key, w_value] + context,
        unfetched=rows,
        scratch=[pltpu.VMEM((FEATURES, 2 * SPAN), bf16)] + rows_scratch,
        flops=8 * unit,
    )

    chip = kernel_call(
        join_body,
        [(stats_shape, f32)],
        [],
        [local] + [swap(local, "ctx", code) for code in (1, 2, 3)],
        room=8,
    )[0]
    stats, out_blocks = kernel_call(
        join_scale_body,
        [(stats_shape, f32), ((CTX_DEVICES, FEATURES, ROWS), bf16)],
        [],
        [chip] + [swap(chip, "ctx", code) for code in (4, 8, 12)] + [local, parts],
        room=16,
    )
    attended_terms = exchange(out_blocks, "ctx")

    both, own_query, other_query = kernel_call(
        backward_body,
        [((2 * SPAN, 2 * FEATURES), bf16), (part_shape, f32), (part_shape, bf16)],
        [info, limits],
        [offset_rows, keys, values, stats],
        unfetched=rows,
        scratch=[
            pltpu.VMEM((2 * SPAN, FEATURES), f32),
            pltpu.VMEM((2 * SPAN, FEATURES), f32),
            pltpu.VMEM((FEATURES, 2 * SPAN), bf16),
            pltpu.VMEM((GROUPS, FEATURES, GROUP_ROWS), f32),
        ]
        + rows_scratch,
        flops=10 * unit,
    )
    query_kept, query_rest = sum_ctx_staged(info, own_query, other_query)
    block_shape = (CHIPS, ROWS, 2 * FEATURES)
    own_weight, other_weight = kernel_call(
        weight_body,
        [(block_shape, f32), (block_shape, bf16)],
        [info],
        [both] + context,
        flops=4 * unit,
    )
    weight_grad = total_of(sum_ctx(own_weight, other_weight))

    terms = kernel_call(
        close_body,
        [((ROWS, 2 * FEATURES), f32)] + [((ROWS, 2 * FEATURES), bf16)] * (TP_DEVICES - 1),
        [info],
        [w_out, w_query, attended_terms, query_kept, query_rest],
        flops=2 * 2 * ROWS * FEATURES * FEATURES * TP_DEVICES,
        room=16,
    )
    total = terms[0]
    for r in range(1, TP_DEVICES):
        total = total + swap(terms[r], "tp", r).astype(f32)
    total = total.astype(bf16)
    return (
        total[:, :FEATURES],
        total[:, FEATURES:],
        weight_grad[:, :FEATURES],
        weight_grad[:, FEATURES:],
    )


def solution(mesh):
    placed = (
        P("ctx"),
        P(None, "tp"),
        P("ctx", "tp"),
        P(None, "tp"),
        P(None, "tp"),
        P(None, "tp"),
        P("tp", None),
        P("ctx", "tp"),
        P(),
    )
    return jax.shard_map(
        shards,
        mesh=mesh,
        in_specs=placed,
        out_specs=(P("ctx", "tp"), P("ctx", "tp"), P("ctx", "tp"), P("ctx", "tp")),
        check_vma=False,
    )
```

```python
import math

import jax
import jax.numpy as jnp
from jax import lax
from jax.experimental import pallas as pl
from jax.experimental.pallas import tpu as pltpu
from jax.sharding import PartitionSpec as P

HEAD_DIM = 128
CTX_DEVICES = 16
TP_DEVICES = 8
FEATURES = 256
HEADS_HERE = FEATURES // HEAD_DIM
ROWS = 128
LAST_PEER = 6
FIRST_PEERS = (0, 1, 2, 3, 4, 5, 7)
CHIPS = CTX_DEVICES // 2
GROUPS = 4
GROUP_ROWS = 4 * ROWS
SPAN = 512

SCORE_SCALE = 1.0 / math.sqrt(HEAD_DIM)
LOG2_SCALE = SCORE_SCALE * math.log2(math.e)
MASKED = -1e30
FLOOR = -1e29

NN = (((1,), (0,)), ((), ()))
NT = (((1,), (1,)), ((), ()))
TN = (((0,), (0,)), ((), ()))

bf16 = jnp.bfloat16
f32 = jnp.float32


def mm(left, right, dims=NN):
    return lax.dot_general(left, right, dims, preferred_element_type=f32)


def swap(value, axis, bits):
    count = CTX_DEVICES if axis == "ctx" else TP_DEVICES
    return lax.ppermute(value, axis, [(i, i ^ bits) for i in range(count)])


def exchange(value, axis, groups=None):
    return lax.all_to_all(value, axis, 0, 0, axis_index_groups=groups, tiled=True)


def whole(shape):
    return pl.BlockSpec(shape, lambda i: (0,) * len(shape), pipeline_mode=pl.Buffered(1))


def kernel_call(body, outs, scalars, arrays, unfetched=(), scratch=(), room=60):
    call = pl.pallas_call(
        body,
        grid=(1,),
        out_shape=[jax.ShapeDtypeStruct(shape, kind) for shape, kind in outs],
        in_specs=[pl.BlockSpec(memory_space=pltpu.SMEM)] * len(scalars)
        + [pl.BlockSpec(memory_space=pl.ANY)] * len(unfetched)
        + [whole(a.shape) for a in arrays],
        out_specs=[whole(shape) for shape, _ in outs],
        scratch_shapes=list(scratch),
        compiler_params=pltpu.CompilerParams(vmem_limit_bytes=room * 1024 * 1024),
        cost_estimate=pl.CostEstimate(flops=0, bytes_accessed=0, transcendentals=0),
    )
    return list(call(*scalars, *unfetched, *arrays))


def gather_tp_first(block):
    return swap(block, "tp", 1), swap(block, "tp", 3), swap(block, "tp", 4)


def gather_tp_rest(block, first):
    near, back, side = first
    side_near = swap(near, "tp", 4)
    side_back = swap(side, "tp", 3)
    far = swap(back, "tp", 1)
    side_far = swap(side_near, "tp", 3)
    return [block, near, far, back, side, side_near, side_far, side_back]


def gather_ctx(block, beside):
    two = jnp.stack([block, beside])
    one, other, last = [swap(two, "ctx", code) for code in (4, 8, 12)]
    even = [jnp.concatenate([two, one], axis=0), jnp.concatenate([other, last], axis=0)]
    return even + [swap(half, "ctx", 1) for half in even]


def shard_start(tp_index, r):
    return pl.multiple_of((tp_index ^ r) * FEATURES, FEATURES)


def head_of(h):
    return slice(h * HEAD_DIM, (h + 1) * HEAD_DIM)


def rows_body(info, w_query, w_out, *refs):
    blocks, out = refs[:-1], refs[-1]
    query = jnp.zeros((ROWS, FEATURES), f32)
    grads = [jnp.zeros((HEAD_DIM, ROWS), f32) for _ in range(HEADS_HERE)]
    for r in range(TP_DEVICES):
        part = pl.ds(shard_start(info[0], r), FEATURES)
        query += mm(blocks[r][:ROWS, :], w_query[part, :])
        for h in range(HEADS_HERE):
            grads[h] += mm(w_out[head_of(h), part], blocks[r][ROWS:, :], NT)
    out[:ROWS, :] = query.astype(bf16)
    for h in range(HEADS_HERE):
        out[ROWS:, head_of(h)] = grads[h].astype(bf16)


def row_copies(sources, rows, arrived):
    return [
        pltpu.make_async_copy(
            source, rows.at[i // 2, pl.ds(i % 2 * (CHIPS // 2), CHIPS // 2)], arrived.at[i]
        )
        for i, source in enumerate(sources)
    ]


def row_block(rows, ctx_index, block):
    return rows.at[(ctx_index ^ block) & 1, (ctx_index ^ block) >> 1]


def group_query(rows, ctx_index, group, h):
    blocks = [row_block(rows, ctx_index, GROUPS * group + i) for i in range(GROUPS)]
    return jnp.concatenate([block[:ROWS, head_of(h)] for block in blocks], axis=0)


def group_grad(rows, ctx_index, group, h):
    blocks = [row_block(rows, ctx_index, GROUPS * group + i) for i in range(GROUPS)]
    return jnp.concatenate([block[ROWS:, head_of(h)] for block in blocks], axis=1)


def visible_in(base, offset_row):
    places = base + lax.broadcasted_iota(jnp.int32, (SPAN, GROUP_ROWS), 0)
    return places <= offset_row


def turned(value):
    return value.astype(f32).T.astype(bf16)


def span_of(i):
    return slice(i * SPAN, (i + 1) * SPAN)


def ordered_rows(weight, tp_index, order):
    return jnp.concatenate(
        [weight[pl.ds(shard_start(tp_index, r), FEATURES), :] for r in order], axis=0
    )


def project_body(info, w_key, w_value, *refs):
    context = jnp.concatenate([ref[...] for ref in refs[:-1]], axis=1)
    out = refs[-1]
    out[:, :FEATURES] = mm(context, ordered_rows(w_key, info[0], FIRST_PEERS))
    out[:, FEATURES:] = mm(context, ordered_rows(w_value, info[0], FIRST_PEERS))


def forward_body(info, limits, *refs):
    sources, refs = refs[:4], refs[4:]
    offsets, w_key, w_value, begun, last = refs[:5]
    keys, values, stats, parts, values_t, rows, arrived = refs[5:]
    copies = row_copies(sources, rows, arrived)
    for copy in copies:
        copy.start()
    ctx_index = info[1]
    start = shard_start(info[0], LAST_PEER)
    for i, (weight, out) in enumerate(((w_key, keys), (w_value, values))):
        rest = mm(last[...], weight[pl.ds(start, FEATURES), :])
        out[...] = (begun[:, i * FEATURES : (i + 1) * FEATURES] + rest).astype(bf16)
    for h in range(HEADS_HERE):
        values_t[head_of(h), :] = turned(values[:, head_of(h)])
    for copy in copies:
        copy.wait()

    def step(group, carry):
        stats[group, :2, :] = jnp.full((2, GROUP_ROWS), MASKED, f32)
        stats[group, 2:, :] = jnp.zeros((2, GROUP_ROWS), f32)
        parts[group] = jnp.zeros((FEATURES, GROUP_ROWS), f32)
        for i in range(2):
            base = info[2 + i]

            @pl.when(limits[group] >= base)
            def _():
                visible = visible_in(base, offsets[group])
                for h in range(HEADS_HERE):
                    query = group_query(rows, ctx_index, group, h)
                    scores = mm(keys[span_of(i), head_of(h)], query, NT) * LOG2_SCALE
                    scores = jnp.where(visible, scores, MASKED)
                    old = stats[group, h : h + 1, :]
                    peak = jnp.maximum(jnp.max(scores, axis=0, keepdims=True), FLOOR)
                    peak = jnp.maximum(peak, old)
                    weights = jnp.exp2(scores - peak)
                    keep = jnp.exp2(old - peak)
                    total = keep * stats[group, h + 2 : h + 3, :]
                    total += jnp.sum(weights, axis=0, keepdims=True)
                    part = mm(values_t[head_of(h), span_of(i)], weights.astype(bf16))
                    parts[group, head_of(h), :] = keep * parts[group, head_of(h), :] + part
                    stats[group, h : h + 1, :] = peak
                    stats[group, h + 2 : h + 3, :] = total

        for h in range(HEADS_HERE):
            total = stats[group, h + 2 : h + 3, :]
            some = total > 0.0
            safe = jnp.where(some, total, 1.0)
            part = parts[group, head_of(h), :] * jnp.where(some, 1.0 / safe, 0.0)
            grad_t = group_grad(rows, ctx_index, group, h).astype(f32)
            level = jnp.where(some, stats[group, h : h + 1, :] + jnp.log2(safe), MASKED)
            stats[group, h : h + 1, :] = level
            stats[group, h + 2 : h + 3, :] = jnp.sum(part * grad_t, axis=0, keepdims=True)
            parts[group, head_of(h), :] = part
        return carry

    lax.fori_loop(0, GROUPS, step, 0)


def joined(refs, group):
    pieces = [ref[group] for ref in refs]
    top = pieces[0][:2]
    for piece in pieces[1:]:
        top = jnp.maximum(top, piece[:2])
    total = jnp.zeros((2, GROUP_ROWS), f32)
    delta = jnp.zeros((2, GROUP_ROWS), f32)
    for piece in pieces:
        weight = jnp.exp2(piece[:2] - top)
        total += weight
        delta += weight * piece[2:]
    return top + jnp.log2(total), delta / total


def join_body(own, one, two, three, stats):
    for group in range(GROUPS):
        level, delta = joined((own, one, two, three), group)
        stats[group, :2, :] = level
        stats[group, 2:, :] = delta


def split_parity(core, group, value, mine, other):
    for i in range(GROUPS // 2):
        low = value[:, 2 * i * ROWS : (2 * i + 1) * ROWS]
        high = value[:, (2 * i + 1) * ROWS : (2 * i + 2) * ROWS]
        chip = group * (GROUPS // 2) + i
        mine[chip] = jnp.where(core == 1, high, low)
        other[chip] = jnp.where(core == 1, low, high).astype(bf16)


def scale_body(own, one, two, three, local, parts, blocks):
    for group in range(GROUPS):
        level, _ = joined((own, one, two, three), group)
        weight = jnp.exp2(local[group][:2] - level)
        for h in range(HEADS_HERE):
            scaled = (parts[group, head_of(h), :] * weight[h : h + 1, :]).astype(bf16)
            for i in range(GROUPS):
                place = GROUPS * group + i
                blocks[place, head_of(h), :] = scaled[:, i * ROWS : (i + 1) * ROWS]


def backward_body(info, limits, *refs):
    sources, refs = refs[:4], refs[4:]
    offsets, keys, values, own, one, two, three = refs[:7]
    both, mine, other, stats, key_acc, value_acc, keys_t, query_acc, rows, arrived = refs[7:]
    copies = row_copies(sources, rows, arrived)
    for copy in copies:
        copy.start()
    for group in range(GROUPS):
        level, delta = joined((own, one, two, three), group)
        stats[group, :2, :] = level
        stats[group, 2:, :] = delta
    ctx_index = info[1]
    query_acc[...] = jnp.zeros(query_acc.shape, f32)
    key_acc[...] = jnp.zeros(key_acc.shape, f32)
    value_acc[...] = jnp.zeros(value_acc.shape, f32)
    for h in range(HEADS_HERE):
        keys_t[head_of(h), :] = turned(keys[:, head_of(h)])
    for copy in copies:
        copy.wait()

    def step(group, carry):
        for i in range(2):
            base = info[2 + i]
            span = span_of(i)

            @pl.when(limits[group] >= base)
            def _():
                visible = visible_in(base, offsets[group])
                for h in range(HEADS_HERE):
                    query = group_query(rows, ctx_index, group, h)
                    grad_t = group_grad(rows, ctx_index, group, h)
                    scores = mm(keys[span, head_of(h)], query, NT) * LOG2_SCALE
                    scores = jnp.where(visible, scores - stats[group, h : h + 1, :], MASKED)
                    probs = jnp.exp2(scores)
                    prob_grad = mm(values[span, head_of(h)], grad_t)
                    delta = stats[group, h + 2 : h + 3, :]
                    score_grad = (probs * (prob_grad - delta) * SCORE_SCALE).astype(bf16)
                    value_acc[span, head_of(h)] += mm(probs.astype(bf16), grad_t, NT)
                    key_acc[span, head_of(h)] += mm(score_grad, query)
                    query_acc[group, head_of(h), :] += mm(keys_t[head_of(h), span], score_grad)

        return carry

    lax.fori_loop(0, GROUPS, step, 0)
    both[:, :FEATURES] = key_acc[...].astype(bf16)
    both[:, FEATURES:] = value_acc[...].astype(bf16)
    for group in range(GROUPS):
        split_parity(ctx_index & 1, group, query_acc[group], mine, other)


def weight_body(info, both, *refs):
    mine, other = refs[-2:]
    flipped = (info[1] & 1) == 1
    for r in range(TP_DEVICES):
        terms = mm(refs[r][...], both[...], TN)
        place = info[0] ^ r
        low, high = terms[:ROWS], terms[ROWS:]
        mine[place] = jnp.where(flipped, high, low)
        other[place] = jnp.where(flipped, low, high).astype(bf16)


def add_body(own, received, out):
    out[...] = (own[...] + received[...].astype(f32)).astype(bf16)


def sum_ctx(own, other):
    received = swap(other, "ctx", 1)
    added = kernel_call(add_body, [(own.shape, bf16)], [], [own, received], room=16)[0]
    groups = [list(range(core, CTX_DEVICES, 2)) for core in range(2)]
    return exchange(added, "ctx", groups)


def spread_z_body(info, own, received, kept, one, two, three):
    z = info[1] >> 2
    for y in range(2):
        place = 2 * z + y
        kept[y] = own[place] + received[place].astype(f32)
        for code, out in ((1, one), (2, two), (3, three)):
            place = 2 * (z ^ code) + y
            out[y] = (own[place] + received[place].astype(f32)).astype(bf16)


def spread_y_body(info, own, one, two, three, kept, sent):
    y = (info[1] >> 1) & 1
    for place, out in ((y, kept), (1 - y, sent)):
        total = own[place]
        for term in (one, two, three):
            total += term[place].astype(f32)
        out[...] = total.astype(out.dtype)


def sum_ctx_staged(info, own, other):
    shape = own.shape[1:]
    kept, *sent = kernel_call(
        spread_z_body,
        [((2,) + shape, f32)] + [((2,) + shape, bf16)] * 3,
        [info],
        [own, swap(other, "ctx", 1)],
        room=16,
    )
    terms = [swap(block, "ctx", 4 * code) for code, block in zip((1, 2, 3), sent)]
    kept, sent = kernel_call(
        spread_y_body, [(shape, f32), (shape, bf16)], [info], [kept] + terms, room=16
    )
    return kept, swap(sent, "ctx", 2)


def total_of(terms):
    total = terms[0].astype(f32)
    for i in range(1, terms.shape[0]):
        total = total + terms[i].astype(f32)
    return total


def close_body(info, w_out, w_query, attended_terms, query_kept, query_rest, *outs):
    attended = total_of(attended_terms).T.astype(bf16)
    query_grad = (query_kept[...] + query_rest[...].astype(f32)).T.astype(bf16)
    for r in range(TP_DEVICES):
        part = pl.ds(shard_start(info[0], r), FEATURES)
        cross = mm(attended, w_out[:, part])
        latent = mm(query_grad, w_query[part, :], NT)
        outs[r][:, :FEATURES] = cross.astype(outs[r].dtype)
        outs[r][:, FEATURES:] = latent.astype(outs[r].dtype)


def shards(token_ids, embed_table, latents, w_query, w_key, w_value, w_out, out_grad, offsets):
    ctx_index = lax.axis_index("ctx").astype(jnp.int32)
    tp_index = lax.axis_index("tp").astype(jnp.int32)
    key_count = token_ids.shape[0]

    mirror_ids = swap(token_ids[SPAN:], "ctx", CTX_DEVICES - 1)
    info = jnp.stack(
        [
            tp_index,
            ctx_index,
            ctx_index * key_count,
            (CTX_DEVICES - 1 - ctx_index) * key_count + SPAN,
        ]
    )
    limits = jnp.max(offsets.reshape(GROUPS, GROUP_ROWS), axis=1)
    offset_rows = offsets.reshape(GROUPS, 1, GROUP_ROWS)

    row_part = jnp.concatenate([latents, out_grad], axis=0)
    row_first = gather_tp_first(row_part)
    ids = jnp.concatenate([token_ids[:SPAN], mirror_ids])
    context_part = embed_table.at[ids].get(mode="promise_in_bounds")
    row_first, context_part = lax.optimization_barrier((row_first, context_part))
    row_blocks = gather_tp_rest(row_part, row_first)
    context_first = gather_tp_first(context_part)

    own = kernel_call(
        rows_body,
        [((2 * ROWS, FEATURES), bf16)],
        [info],
        [w_query, w_out] + row_blocks,
    )[0]
    beside, context_first = lax.optimization_barrier((swap(own, "ctx", 2), context_first))
    rows = gather_ctx(own, beside)
    context = gather_tp_rest(context_part, context_first)
    begun = kernel_call(
        project_body,
        [((2 * SPAN, 2 * FEATURES), f32)],
        [info],
        [w_key, w_value] + [context[r] for r in FIRST_PEERS],
    )[0]

    part_shape = (CHIPS, FEATURES, ROWS)
    stats_shape = (GROUPS, 4, GROUP_ROWS)
    rows_scratch = [
        pltpu.VMEM((2, CHIPS, 2 * ROWS, FEATURES), bf16),
        pltpu.SemaphoreType.DMA((4,)),
    ]
    keys, values, local, parts = kernel_call(
        forward_body,
        [
            ((2 * SPAN, FEATURES), bf16),
            ((2 * SPAN, FEATURES), bf16),
            (stats_shape, f32),
            ((GROUPS, FEATURES, GROUP_ROWS), f32),
        ],
        [info, limits],
        [offset_rows, w_key, w_value, begun, context[LAST_PEER]],
        unfetched=rows,
        scratch=[pltpu.VMEM((FEATURES, 2 * SPAN), bf16)] + rows_scratch,
    )

    chip = kernel_call(
        join_body,
        [(stats_shape, f32)],
        [],
        [local] + [swap(local, "ctx", code) for code in (1, 2, 3)],
        room=8,
    )[0]
    chips = [chip] + [swap(chip, "ctx", code) for code in (4, 8, 12)]
    out_blocks = kernel_call(
        scale_body,
        [((CTX_DEVICES, FEATURES, ROWS), bf16)],
        [],
        chips + [local, parts],
    )[0]
    out_blocks, chips = lax.optimization_barrier((out_blocks, chips))
    attended_terms = exchange(out_blocks, "ctx")

    both, own_query, other_query = kernel_call(
        backward_body,
        [((2 * SPAN, 2 * FEATURES), bf16), (part_shape, f32), (part_shape, bf16)],
        [info, limits],
        [offset_rows, keys, values] + chips,
        unfetched=rows,
        scratch=[
            pltpu.VMEM(stats_shape, f32),
            pltpu.VMEM((2 * SPAN, FEATURES), f32),
            pltpu.VMEM((2 * SPAN, FEATURES), f32),
            pltpu.VMEM((FEATURES, 2 * SPAN), bf16),
            pltpu.VMEM((GROUPS, FEATURES, GROUP_ROWS), f32),
        ]
        + rows_scratch,
    )
    query_kept, query_rest = sum_ctx_staged(info, own_query, other_query)
    block_shape = (CHIPS, ROWS, 2 * FEATURES)
    own_weight, other_weight = kernel_call(
        weight_body,
        [(block_shape, f32), (block_shape, bf16)],
        [info],
        [both] + context,
    )
    own_weight, other_weight, attended_terms = lax.optimization_barrier(
        (own_weight, other_weight, attended_terms)
    )
    weight_grad = total_of(sum_ctx(own_weight, other_weight))

    terms = kernel_call(
        close_body,
        [((ROWS, 2 * FEATURES), f32)] + [((ROWS, 2 * FEATURES), bf16)] * (TP_DEVICES - 1),
        [info],
        [w_out, w_query, attended_terms, query_kept, query_rest],
        room=16,
    )
    total = terms[0]
    for r in range(1, TP_DEVICES):
        total = total + swap(terms[r], "tp", r).astype(f32)
    total = total.astype(bf16)
    return (
        total[:, :FEATURES],
        total[:, FEATURES:],
        weight_grad[:, :FEATURES],
        weight_grad[:, FEATURES:],
    )


def solution(mesh):
    placed = (
        P("ctx"),
        P(None, "tp"),
        P("ctx", "tp"),
        P(None, "tp"),
        P(None, "tp"),
        P(None, "tp"),
        P("tp", None),
        P("ctx", "tp"),
        P(),
    )
    return jax.shard_map(
        shards,
        mesh=mesh,
        in_specs=placed,
        out_specs=(P("ctx", "tp"), P("ctx", "tp"), P("ctx", "tp"), P("ctx", "tp")),
        check_vma=False,
    )
```

```python
import math

import jax
import jax.numpy as jnp
from jax import lax
from jax.experimental import pallas as pl
from jax.experimental.pallas import tpu as pltpu
from jax.sharding import PartitionSpec as P

HEAD_DIM = 128
CTX_DEVICES = 16
TP_DEVICES = 8
FEATURES = 256
HEADS_HERE = FEATURES // HEAD_DIM
ROWS = 128
LAST_PEER = 6
FIRST_PEERS = (0, 1, 2, 3, 4, 5, 7)
CHIPS = CTX_DEVICES // 2
GROUPS = 4
GROUP_ROWS = 4 * ROWS
SPAN = 512

SCORE_SCALE = 1.0 / math.sqrt(HEAD_DIM)
LOG2_SCALE = SCORE_SCALE * math.log2(math.e)
MASKED = -1e30
FLOOR = -1e29

NN = (((1,), (0,)), ((), ()))
NT = (((1,), (1,)), ((), ()))
TN = (((0,), (0,)), ((), ()))

bf16 = jnp.bfloat16
f32 = jnp.float32


def mm(left, right, dims=NN):
    return lax.dot_general(left, right, dims, preferred_element_type=f32)


def swap(value, axis, bits):
    count = CTX_DEVICES if axis == "ctx" else TP_DEVICES
    return lax.ppermute(value, axis, [(i, i ^ bits) for i in range(count)])


def exchange(value, axis, groups=None):
    return lax.all_to_all(value, axis, 0, 0, axis_index_groups=groups, tiled=True)


def whole(shape):
    return pl.BlockSpec(shape, lambda i: (0,) * len(shape), pipeline_mode=pl.Buffered(1))


def kernel_call(body, outs, scalars, arrays, unfetched=(), scratch=(), room=60):
    call = pl.pallas_call(
        body,
        grid=(1,),
        out_shape=[jax.ShapeDtypeStruct(shape, kind) for shape, kind in outs],
        in_specs=[pl.BlockSpec(memory_space=pltpu.SMEM)] * len(scalars)
        + [pl.BlockSpec(memory_space=pl.ANY)] * len(unfetched)
        + [whole(a.shape) for a in arrays],
        out_specs=[whole(shape) for shape, _ in outs],
        scratch_shapes=list(scratch),
        compiler_params=pltpu.CompilerParams(vmem_limit_bytes=room * 1024 * 1024),
        cost_estimate=pl.CostEstimate(flops=0, bytes_accessed=0, transcendentals=0),
    )
    return list(call(*scalars, *unfetched, *arrays))


def far_blocks(near, back, side):
    return swap(back, "tp", 1), swap(near, "tp", 4), swap(side, "tp", 3)


def gather_ctx(block, beside):
    two = jnp.stack([block, beside])
    one, other, last = [swap(two, "ctx", code) for code in (4, 8, 12)]
    even = [jnp.concatenate([two, one], axis=0), jnp.concatenate([other, last], axis=0)]
    return even + [swap(half, "ctx", 1) for half in even]


def shard_start(tp_index, r):
    return pl.multiple_of((tp_index ^ r) * FEATURES, FEATURES)


def head_of(h):
    return slice(h * HEAD_DIM, (h + 1) * HEAD_DIM)


def rows_body(info, w_query, w_out, *refs):
    blocks, out = refs[:-1], refs[-1]
    query = jnp.zeros((ROWS, FEATURES), f32)
    grads = [jnp.zeros((HEAD_DIM, ROWS), f32) for _ in range(HEADS_HERE)]
    for r in range(TP_DEVICES):
        part = pl.ds(shard_start(info[0], r), FEATURES)
        query += mm(blocks[r][:ROWS, :], w_query[part, :])
        for h in range(HEADS_HERE):
            grads[h] += mm(w_out[head_of(h), part], blocks[r][ROWS:, :], NT)
    out[:ROWS, :] = query.astype(bf16)
    for h in range(HEADS_HERE):
        out[ROWS:, head_of(h)] = grads[h].astype(bf16)


def row_copies(sources, rows, arrived):
    return [
        pltpu.make_async_copy(
            source, rows.at[i // 2, pl.ds(i % 2 * (CHIPS // 2), CHIPS // 2)], arrived.at[i]
        )
        for i, source in enumerate(sources)
    ]


def row_block(rows, ctx_index, block):
    return rows.at[(ctx_index ^ block) & 1, (ctx_index ^ block) >> 1]


def group_query(rows, ctx_index, group, h):
    blocks = [row_block(rows, ctx_index, GROUPS * group + i) for i in range(GROUPS)]
    return jnp.concatenate([block[:ROWS, head_of(h)] for block in blocks], axis=0)


def group_grad(rows, ctx_index, group, h):
    blocks = [row_block(rows, ctx_index, GROUPS * group + i) for i in range(GROUPS)]
    return jnp.concatenate([block[ROWS:, head_of(h)] for block in blocks], axis=1)


def visible_in(base, offset_row):
    places = base + lax.broadcasted_iota(jnp.int32, (SPAN, GROUP_ROWS), 0)
    return places <= offset_row


def turned(value):
    return value.astype(f32).T.astype(bf16)


def span_of(i):
    return slice(i * SPAN, (i + 1) * SPAN)


def ordered_rows(weight, tp_index, order):
    return jnp.concatenate(
        [weight[pl.ds(shard_start(tp_index, r), FEATURES), :] for r in order], axis=0
    )


def project_body(info, w_key, w_value, *refs):
    context = jnp.concatenate([ref[...] for ref in refs[:-1]], axis=1)
    out = refs[-1]
    out[:, :FEATURES] = mm(context, ordered_rows(w_key, info[0], FIRST_PEERS))
    out[:, FEATURES:] = mm(context, ordered_rows(w_value, info[0], FIRST_PEERS))


def forward_body(info, limits, *refs):
    sources, refs = refs[:4], refs[4:]
    offsets, w_key, w_value, begun, last = refs[:5]
    keys, values, stats, parts, values_t, rows, arrived = refs[5:]
    copies = row_copies(sources, rows, arrived)
    for copy in copies:
        copy.start()
    ctx_index = info[1]
    start = shard_start(info[0], LAST_PEER)
    for i, (weight, out) in enumerate(((w_key, keys), (w_value, values))):
        rest = mm(last[...], weight[pl.ds(start, FEATURES), :])
        out[...] = (begun[:, i * FEATURES : (i + 1) * FEATURES] + rest).astype(bf16)
    for h in range(HEADS_HERE):
        values_t[head_of(h), :] = turned(values[:, head_of(h)])
    for copy in copies:
        copy.wait()

    def step(group, carry):
        stats[group, :2, :] = jnp.full((2, GROUP_ROWS), MASKED, f32)
        stats[group, 2:, :] = jnp.zeros((2, GROUP_ROWS), f32)
        parts[group] = jnp.zeros((FEATURES, GROUP_ROWS), f32)
        for i in range(2):
            base = info[2 + i]

            @pl.when(limits[group] >= base)
            def _():
                visible = visible_in(base, offsets[group])
                for h in range(HEADS_HERE):
                    query = group_query(rows, ctx_index, group, h)
                    scores = mm(keys[span_of(i), head_of(h)], query, NT) * LOG2_SCALE
                    scores = jnp.where(visible, scores, MASKED)
                    old = stats[group, h : h + 1, :]
                    peak = jnp.maximum(jnp.max(scores, axis=0, keepdims=True), FLOOR)
                    peak = jnp.maximum(peak, old)
                    weights = jnp.exp2(scores - peak)
                    keep = jnp.exp2(old - peak)
                    total = keep * stats[group, h + 2 : h + 3, :]
                    total += jnp.sum(weights, axis=0, keepdims=True)
                    part = mm(values_t[head_of(h), span_of(i)], weights.astype(bf16))
                    parts[group, head_of(h), :] = keep * parts[group, head_of(h), :] + part
                    stats[group, h : h + 1, :] = peak
                    stats[group, h + 2 : h + 3, :] = total

        for h in range(HEADS_HERE):
            total = stats[group, h + 2 : h + 3, :]
            some = total > 0.0
            safe = jnp.where(some, total, 1.0)
            part = parts[group, head_of(h), :] * jnp.where(some, 1.0 / safe, 0.0)
            grad_t = group_grad(rows, ctx_index, group, h).astype(f32)
            level = jnp.where(some, stats[group, h : h + 1, :] + jnp.log2(safe), MASKED)
            stats[group, h : h + 1, :] = level
            stats[group, h + 2 : h + 3, :] = jnp.sum(part * grad_t, axis=0, keepdims=True)
            parts[group, head_of(h), :] = part
        return carry

    lax.fori_loop(0, GROUPS, step, 0)


def joined(refs, group):
    pieces = [ref[group] for ref in refs]
    top = pieces[0][:2]
    for piece in pieces[1:]:
        top = jnp.maximum(top, piece[:2])
    total = jnp.zeros((2, GROUP_ROWS), f32)
    delta = jnp.zeros((2, GROUP_ROWS), f32)
    for piece in pieces:
        weight = jnp.exp2(piece[:2] - top)
        total += weight
        delta += weight * piece[2:]
    return top + jnp.log2(total), delta / total


def join_body(own, one, two, three, stats):
    for group in range(GROUPS):
        level, delta = joined((own, one, two, three), group)
        stats[group, :2, :] = level
        stats[group, 2:, :] = delta


def split_parity(core, group, value, mine, other):
    for i in range(GROUPS // 2):
        low = value[:, 2 * i * ROWS : (2 * i + 1) * ROWS]
        high = value[:, (2 * i + 1) * ROWS : (2 * i + 2) * ROWS]
        chip = group * (GROUPS // 2) + i
        mine[chip] = jnp.where(core == 1, high, low)
        other[chip] = jnp.where(core == 1, low, high).astype(bf16)


def scale_body(own, one, two, three, local, parts, blocks):
    for group in range(GROUPS):
        level, _ = joined((own, one, two, three), group)
        weight = jnp.exp2(local[group][:2] - level)
        for h in range(HEADS_HERE):
            scaled = (parts[group, head_of(h), :] * weight[h : h + 1, :]).astype(bf16)
            for i in range(GROUPS):
                place = GROUPS * group + i
                blocks[place, head_of(h), :] = scaled[:, i * ROWS : (i + 1) * ROWS]


def backward_body(info, limits, *refs):
    sources, refs = refs[:4], refs[4:]
    offsets, keys, values, own, one, two, three = refs[:7]
    both, mine, other, stats, key_acc, value_acc, keys_t, query_acc, rows, arrived = refs[7:]
    copies = row_copies(sources, rows, arrived)
    for copy in copies:
        copy.start()
    for group in range(GROUPS):
        level, delta = joined((own, one, two, three), group)
        stats[group, :2, :] = level
        stats[group, 2:, :] = delta
    ctx_index = info[1]
    query_acc[...] = jnp.zeros(query_acc.shape, f32)
    key_acc[...] = jnp.zeros(key_acc.shape, f32)
    value_acc[...] = jnp.zeros(value_acc.shape, f32)
    for h in range(HEADS_HERE):
        keys_t[head_of(h), :] = turned(keys[:, head_of(h)])
    for copy in copies:
        copy.wait()

    def step(group, carry):
        for i in range(2):
            base = info[2 + i]
            span = span_of(i)

            @pl.when(limits[group] >= base)
            def _():
                visible = visible_in(base, offsets[group])
                for h in range(HEADS_HERE):
                    query = group_query(rows, ctx_index, group, h)
                    grad_t = group_grad(rows, ctx_index, group, h)
                    scores = mm(keys[span, head_of(h)], query, NT) * LOG2_SCALE
                    scores = jnp.where(visible, scores - stats[group, h : h + 1, :], MASKED)
                    probs = jnp.exp2(scores)
                    prob_grad = mm(values[span, head_of(h)], grad_t)
                    delta = stats[group, h + 2 : h + 3, :]
                    score_grad = (probs * (prob_grad - delta) * SCORE_SCALE).astype(bf16)
                    value_acc[span, head_of(h)] += mm(probs.astype(bf16), grad_t, NT)
                    key_acc[span, head_of(h)] += mm(score_grad, query)
                    query_acc[group, head_of(h), :] += mm(keys_t[head_of(h), span], score_grad)

        return carry

    lax.fori_loop(0, GROUPS, step, 0)
    both[:, :FEATURES] = key_acc[...].astype(bf16)
    both[:, FEATURES:] = value_acc[...].astype(bf16)
    for group in range(GROUPS):
        split_parity(ctx_index & 1, group, query_acc[group], mine, other)


def weight_body(info, *refs):
    sources, (both, mine, other, blocks, arrived) = refs[:TP_DEVICES], refs[TP_DEVICES:]
    flipped = (info[1] & 1) == 1
    copies = [
        pltpu.make_async_copy(source, blocks.at[r], arrived.at[r])
        for r, source in enumerate(sources)
    ]
    for copy in copies:
        copy.start()
    for r in range(TP_DEVICES):
        copies[r].wait()
        terms = mm(blocks[r], both[...], TN)
        place = info[0] ^ r
        low, high = terms[:ROWS], terms[ROWS:]
        mine[place] = jnp.where(flipped, high, low)
        other[place] = jnp.where(flipped, low, high).astype(bf16)


def add_body(own, received, out):
    out[...] = (own[...] + received[...].astype(f32)).astype(bf16)


def spread_z_body(info, own, received, kept, one, two, three):
    z = info[1] >> 2
    for y in range(2):
        place = 2 * z + y
        kept[y] = own[place] + received[place].astype(f32)
        for code, out in ((1, one), (2, two), (3, three)):
            place = 2 * (z ^ code) + y
            out[y] = (own[place] + received[place].astype(f32)).astype(bf16)


def spread_y_body(info, own, one, two, three, kept, sent):
    y = (info[1] >> 1) & 1
    for place, out in ((y, kept), (1 - y, sent)):
        total = own[place]
        for term in (one, two, three):
            total += term[place].astype(f32)
        out[...] = total.astype(out.dtype)


def total_of(terms):
    total = terms[0].astype(f32)
    for i in range(1, terms.shape[0]):
        total = total + terms[i].astype(f32)
    return total


def close_body(info, w_out, w_query, attended_terms, query_kept, query_rest, *outs):
    attended = total_of(attended_terms).T.astype(bf16)
    query_grad = (query_kept[...] + query_rest[...].astype(f32)).T.astype(bf16)
    for r in range(TP_DEVICES):
        part = pl.ds(shard_start(info[0], r), FEATURES)
        cross = mm(attended, w_out[:, part])
        latent = mm(query_grad, w_query[part, :], NT)
        outs[r][:, :FEATURES] = cross.astype(outs[r].dtype)
        outs[r][:, FEATURES:] = latent.astype(outs[r].dtype)


def shards(token_ids, embed_table, latents, w_query, w_key, w_value, w_out, out_grad, offsets):
    ctx_index = lax.axis_index("ctx").astype(jnp.int32)
    tp_index = lax.axis_index("tp").astype(jnp.int32)
    key_count = token_ids.shape[0]

    mirror_ids = swap(token_ids[SPAN:], "ctx", CTX_DEVICES - 1)
    info = jnp.stack(
        [
            tp_index,
            ctx_index,
            ctx_index * key_count,
            (CTX_DEVICES - 1 - ctx_index) * key_count + SPAN,
        ]
    )
    limits = jnp.max(offsets.reshape(GROUPS, GROUP_ROWS), axis=1)
    offset_rows = offsets.reshape(GROUPS, 1, GROUP_ROWS)

    row_part = jnp.concatenate([latents, out_grad], axis=0)
    near, back, side = (swap(row_part, "tp", bits) for bits in (1, 3, 4))
    far, side_near, side_back = far_blocks(near, back, side)
    ids = jnp.concatenate([token_ids[:SPAN], mirror_ids])
    context_part = embed_table.at[ids].get(mode="promise_in_bounds")
    far, side_near, side_back, context_part = lax.optimization_barrier(
        (far, side_near, side_back, context_part)
    )
    side_far = swap(side_back, "tp", 1)
    context_back, context_side = swap(context_part, "tp", 3), swap(context_part, "tp", 4)
    side_far, context_late = lax.optimization_barrier((side_far, context_part))
    context_first = (swap(context_late, "tp", 1), context_back, context_side)
    row_blocks = [row_part, near, far, back, side, side_near, side_far, side_back]

    own = kernel_call(
        rows_body,
        [((2 * ROWS, FEATURES), bf16)],
        [info],
        [w_query, w_out] + row_blocks,
    )[0]
    beside, context_first = lax.optimization_barrier((swap(own, "ctx", 2), context_first))
    rows = gather_ctx(own, beside)
    near, back, side = context_first
    far, side_near, side_back = far_blocks(near, back, side)
    side_far = swap(side_back, "tp", 1)
    context = [context_part, near, far, back, side, side_near, side_far, side_back]
    begun = kernel_call(
        project_body,
        [((2 * SPAN, 2 * FEATURES), f32)],
        [info],
        [w_key, w_value] + [context[r] for r in FIRST_PEERS],
    )[0]

    part_shape = (CHIPS, FEATURES, ROWS)
    stats_shape = (GROUPS, 4, GROUP_ROWS)
    rows_scratch = [
        pltpu.VMEM((2, CHIPS, 2 * ROWS, FEATURES), bf16),
        pltpu.SemaphoreType.DMA((4,)),
    ]
    keys, values, local, parts = kernel_call(
        forward_body,
        [
            ((2 * SPAN, FEATURES), bf16),
            ((2 * SPAN, FEATURES), bf16),
            (stats_shape, f32),
            ((GROUPS, FEATURES, GROUP_ROWS), f32),
        ],
        [info, limits],
        [offset_rows, w_key, w_value, begun, context[LAST_PEER]],
        unfetched=rows,
        scratch=[pltpu.VMEM((FEATURES, 2 * SPAN), bf16)] + rows_scratch,
    )

    chip = kernel_call(
        join_body,
        [(stats_shape, f32)],
        [],
        [local] + [swap(local, "ctx", code) for code in (1, 2, 3)],
        room=8,
    )[0]
    chips = [chip] + [swap(chip, "ctx", code) for code in (4, 8, 12)]
    out_blocks = kernel_call(
        scale_body,
        [((CTX_DEVICES, FEATURES, ROWS), bf16)],
        [],
        chips + [local, parts],
    )[0]
    out_blocks, chips = lax.optimization_barrier((out_blocks, chips))
    attended_terms = exchange(out_blocks, "ctx")

    both, own_query, other_query = kernel_call(
        backward_body,
        [((2 * SPAN, 2 * FEATURES), bf16), (part_shape, f32), (part_shape, bf16)],
        [info, limits],
        [offset_rows, keys, values] + chips,
        unfetched=rows,
        scratch=[
            pltpu.VMEM(stats_shape, f32),
            pltpu.VMEM((2 * SPAN, FEATURES), f32),
            pltpu.VMEM((2 * SPAN, FEATURES), f32),
            pltpu.VMEM((FEATURES, 2 * SPAN), bf16),
            pltpu.VMEM((GROUPS, FEATURES, GROUP_ROWS), f32),
        ]
        + rows_scratch,
    )
    query_shape = (FEATURES, ROWS)
    kept, *sent = kernel_call(
        spread_z_body,
        [((2,) + query_shape, f32)] + [((2,) + query_shape, bf16)] * 3,
        [info],
        [own_query, swap(other_query, "ctx", 1)],
        room=16,
    )
    both, sent = lax.optimization_barrier((both, sent))
    arriving = [swap(block, "ctx", 4 * code) for code, block in zip((1, 2, 3), sent)]
    block_shape = (CHIPS, ROWS, 2 * FEATURES)
    own_weight, other_weight = kernel_call(
        weight_body,
        [(block_shape, f32), (block_shape, bf16)],
        [info],
        [both],
        unfetched=context,
        scratch=[
            pltpu.VMEM((TP_DEVICES, 2 * SPAN, FEATURES), bf16),
            pltpu.SemaphoreType.DMA((TP_DEVICES,)),
        ],
    )
    own_weight, other_weight, attended_terms, arriving = lax.optimization_barrier(
        (own_weight, other_weight, attended_terms, arriving)
    )
    query_kept, sent = kernel_call(
        spread_y_body,
        [(query_shape, f32), (query_shape, bf16)],
        [info],
        [kept] + arriving,
        room=16,
    )
    weight_blocks = kernel_call(
        add_body,
        [(block_shape, bf16)],
        [],
        [own_weight, swap(other_weight, "ctx", 1)],
        room=16,
    )[0]
    sent, weight_blocks = lax.optimization_barrier((sent, weight_blocks))
    query_rest = swap(sent, "ctx", 2)
    same_core = [list(range(core, CTX_DEVICES, 2)) for core in range(2)]
    weight_grad = total_of(exchange(weight_blocks, "ctx", same_core))

    terms = kernel_call(
        close_body,
        [((ROWS, 2 * FEATURES), f32)] + [((ROWS, 2 * FEATURES), bf16)] * (TP_DEVICES - 1),
        [info],
        [w_out, w_query, attended_terms, query_kept, query_rest],
        room=16,
    )
    total = terms[0]
    for r in range(1, TP_DEVICES):
        total = total + swap(terms[r], "tp", r).astype(f32)
    total = total.astype(bf16)
    return (
        total[:, :FEATURES],
        total[:, FEATURES:],
        weight_grad[:, :FEATURES],
        weight_grad[:, FEATURES:],
    )


def solution(mesh):
    placed = (
        P("ctx"),
        P(None, "tp"),
        P("ctx", "tp"),
        P(None, "tp"),
        P(None, "tp"),
        P(None, "tp"),
        P("tp", None),
        P("ctx", "tp"),
        P(),
    )
    return jax.shard_map(
        shards,
        mesh=mesh,
        in_specs=placed,
        out_specs=(P("ctx", "tp"), P("ctx", "tp"), P("ctx", "tp"), P("ctx", "tp")),
        check_vma=False,
    )
```

```python
import math

import jax
import jax.numpy as jnp
from jax import lax
from jax.experimental import pallas as pl
from jax.experimental.pallas import tpu as pltpu
from jax.sharding import PartitionSpec as P

HEAD_DIM = 128
CTX_DEVICES = 16
TP_DEVICES = 8
FEATURES = 256
HEADS_HERE = FEATURES // HEAD_DIM
ROWS = 128
LAST_PEER = 6
FIRST_PEERS = (0, 1, 2, 3, 4, 5, 7)
CHIPS = CTX_DEVICES // 2
GROUPS = 4
LEVEL_ROWS = 16
GROUP_ROWS = 4 * ROWS
SPAN = 512

SCORE_SCALE = 1.0 / math.sqrt(HEAD_DIM)
LOG2_SCALE = SCORE_SCALE * math.log2(math.e)
MASKED = -1e30
FLOOR = -1e29

NN = (((1,), (0,)), ((), ()))
NT = (((1,), (1,)), ((), ()))
TN = (((0,), (0,)), ((), ()))

bf16 = jnp.bfloat16
f32 = jnp.float32


def mm(left, right, dims=NN):
    return lax.dot_general(left, right, dims, preferred_element_type=f32)


def swap(value, axis, bits):
    count = CTX_DEVICES if axis == "ctx" else TP_DEVICES
    return lax.ppermute(value, axis, [(i, i ^ bits) for i in range(count)])


def exchange(value, axis, groups=None):
    return lax.all_to_all(value, axis, 0, 0, axis_index_groups=groups, tiled=True)


def whole(shape):
    return pl.BlockSpec(shape, lambda i: (0,) * len(shape), pipeline_mode=pl.Buffered(1))


def kernel_call(body, outs, scalars, arrays, unfetched=(), scratch=(), room=60, flops=0):
    call = pl.pallas_call(
        body,
        grid=(1,),
        out_shape=[jax.ShapeDtypeStruct(shape, kind) for shape, kind in outs],
        in_specs=[pl.BlockSpec(memory_space=pltpu.SMEM)] * len(scalars)
        + [pl.BlockSpec(memory_space=pl.ANY)] * len(unfetched)
        + [whole(a.shape) for a in arrays],
        out_specs=[whole(shape) for shape, _ in outs],
        scratch_shapes=list(scratch),
        compiler_params=pltpu.CompilerParams(vmem_limit_bytes=room * 1024 * 1024),
        cost_estimate=pl.CostEstimate(flops=flops, bytes_accessed=0, transcendentals=0),
    )
    return list(call(*scalars, *unfetched, *arrays))


def far_blocks(near, back, side):
    return swap(back, "tp", 1), swap(near, "tp", 4), swap(side, "tp", 3)


def gather_ctx(block, beside):
    two = jnp.stack([block, beside])
    one, other, last = [swap(two, "ctx", code) for code in (4, 8, 12)]
    even = [jnp.concatenate([two, one], axis=0), jnp.concatenate([other, last], axis=0)]
    return even + [swap(half, "ctx", 1) for half in even]


def shard_start(tp_index, r):
    return pl.multiple_of((tp_index ^ r) * FEATURES, FEATURES)


def head_of(h):
    return slice(h * HEAD_DIM, (h + 1) * HEAD_DIM)


def rows_body(info, w_query, w_out, *refs):
    blocks, out = refs[:-1], refs[-1]
    query = jnp.zeros((ROWS, FEATURES), f32)
    grads = [jnp.zeros((HEAD_DIM, ROWS), f32) for _ in range(HEADS_HERE)]
    for r in range(TP_DEVICES):
        part = pl.ds(shard_start(info[0], r), FEATURES)
        query += mm(blocks[r][:ROWS, :], w_query[part, :])
        for h in range(HEADS_HERE):
            grads[h] += mm(w_out[head_of(h), part], blocks[r][ROWS:, :], NT)
    out[:ROWS, :] = query.astype(bf16)
    for h in range(HEADS_HERE):
        out[ROWS:, head_of(h)] = grads[h].astype(bf16)


def row_copies(sources, rows, arrived):
    return [
        pltpu.make_async_copy(
            source, rows.at[i // 2, pl.ds(i % 2 * (CHIPS // 2), CHIPS // 2)], arrived.at[i]
        )
        for i, source in enumerate(sources)
    ]


def row_block(rows, ctx_index, block):
    return rows.at[(ctx_index ^ block) & 1, (ctx_index ^ block) >> 1]


def group_query(rows, ctx_index, group, h):
    blocks = [row_block(rows, ctx_index, GROUPS * group + i) for i in range(GROUPS)]
    return jnp.concatenate([block[:ROWS, head_of(h)] for block in blocks], axis=0)


def group_grad(rows, ctx_index, group, h):
    blocks = [row_block(rows, ctx_index, GROUPS * group + i) for i in range(GROUPS)]
    return jnp.concatenate([block[ROWS:, head_of(h)] for block in blocks], axis=1)


def masked(scores, base, offset_row):
    if offset_row is None:
        return scores
    places = base + lax.broadcasted_iota(jnp.int32, (SPAN, GROUP_ROWS), 0)
    return jnp.where(places <= offset_row, scores, MASKED)


def visit(bounds, base, offsets, group, block):
    whole_seen = bounds[1, group] >= base + (SPAN - 1)

    @pl.when(whole_seen)
    def _():
        block(None)

    @pl.when(jnp.logical_and(bounds[0, group] >= base, jnp.logical_not(whole_seen)))
    def _():
        block(offsets[group])


def pieces_of(level):
    pieces = []
    for _ in range(3):
        piece = level.astype(bf16).astype(f32)
        pieces.append(piece)
        level = level - piece
    return pieces


def turned(value):
    return value.astype(f32).T.astype(bf16)


def span_of(i):
    return slice(i * SPAN, (i + 1) * SPAN)


def ordered_rows(weight, tp_index, order):
    return jnp.concatenate(
        [weight[pl.ds(shard_start(tp_index, r), FEATURES), :] for r in order], axis=0
    )


def project_body(info, w_key, w_value, *refs):
    context = jnp.concatenate([ref[...] for ref in refs[:-1]], axis=1)
    out = refs[-1]
    out[:, :FEATURES] = mm(context, ordered_rows(w_key, info[0], FIRST_PEERS))
    out[:, FEATURES:] = mm(context, ordered_rows(w_value, info[0], FIRST_PEERS))


def forward_body(info, limits, *refs):
    sources, refs = refs[:4], refs[4:]
    offsets, w_key, w_value, begun, last = refs[:5]
    keys, values, stats, blocks, values_t, parts, rows, arrived = refs[5:]
    copies = row_copies(sources, rows, arrived)
    for copy in copies:
        copy.start()
    ctx_index = info[1]
    start = shard_start(info[0], LAST_PEER)
    for i, (weight, out) in enumerate(((w_key, keys), (w_value, values))):
        rest = mm(last[...], weight[pl.ds(start, FEATURES), :])
        out[...] = (begun[:, i * FEATURES : (i + 1) * FEATURES] + rest).astype(bf16)
    for h in range(HEADS_HERE):
        values_t[head_of(h), :] = turned(values[:, head_of(h)])
    for copy in copies:
        copy.wait()

    def step(group, carry):
        stats[group, :2, :] = jnp.full((2, GROUP_ROWS), MASKED, f32)
        stats[group, 2:, :] = jnp.zeros((2, GROUP_ROWS), f32)
        parts[...] = jnp.zeros((FEATURES, GROUP_ROWS), f32)
        for i in range(2):
            base = info[2 + i]

            def block(offset_row, i=i, base=base):
                for h in range(HEADS_HERE):
                    query = group_query(rows, ctx_index, group, h)
                    scores = mm(keys[span_of(i), head_of(h)], query, NT) * LOG2_SCALE
                    scores = masked(scores, base, offset_row)
                    old = stats[group, h : h + 1, :]
                    peak = jnp.maximum(jnp.max(scores, axis=0, keepdims=True), FLOOR)
                    peak = jnp.maximum(peak, old)
                    weights = jnp.exp2(scores - peak)
                    keep = jnp.exp2(old - peak)
                    total = keep * stats[group, h + 2 : h + 3, :]
                    total += jnp.sum(weights, axis=0, keepdims=True)
                    part = mm(values_t[head_of(h), span_of(i)], weights.astype(bf16))
                    parts[head_of(h), :] = keep * parts[head_of(h), :] + part
                    stats[group, h : h + 1, :] = peak
                    stats[group, h + 2 : h + 3, :] = total

            visit(limits, base, offsets, group, block)

        levels = []
        for h in range(HEADS_HERE):
            total = stats[group, h + 2 : h + 3, :]
            some = total > 0.0
            safe = jnp.where(some, total, 1.0)
            part = parts[head_of(h), :] * jnp.where(some, 1.0 / safe, 0.0)
            grad_t = group_grad(rows, ctx_index, group, h).astype(f32)
            level = jnp.where(some, stats[group, h : h + 1, :] + jnp.log2(safe), MASKED)
            stats[group, h : h + 1, :] = level
            stats[group, h + 2 : h + 3, :] = jnp.sum(part * grad_t, axis=0, keepdims=True)
            levels += pieces_of(level)
            for i in range(GROUPS):
                place = GROUPS * group + i
                lanes = slice(i * ROWS, (i + 1) * ROWS)
                blocks[place, head_of(h), :] = part[:, lanes].astype(bf16)
        levels.append(jnp.zeros((LEVEL_ROWS - len(levels), GROUP_ROWS), f32))
        levels = jnp.concatenate(levels, axis=0).astype(bf16)
        for i in range(GROUPS):
            place = GROUPS * group + i
            blocks[place, FEATURES:, :] = levels[:, i * ROWS : (i + 1) * ROWS]
        return carry

    lax.fori_loop(0, GROUPS, step, 0)


def joined(refs, group):
    pieces = [ref[group] for ref in refs]
    top = pieces[0][:2]
    for piece in pieces[1:]:
        top = jnp.maximum(top, piece[:2])
    total = jnp.zeros((2, GROUP_ROWS), f32)
    delta = jnp.zeros((2, GROUP_ROWS), f32)
    for piece in pieces:
        weight = jnp.exp2(piece[:2] - top)
        total += weight
        delta += weight * piece[2:]
    return top + jnp.log2(total), delta / total


def join_body(own, one, two, three, stats):
    for group in range(GROUPS):
        level, delta = joined((own, one, two, three), group)
        stats[group, :2, :] = level
        stats[group, 2:, :] = delta


def split_parity(core, group, value, mine, other):
    for i in range(GROUPS // 2):
        low = value[:, 2 * i * ROWS : (2 * i + 1) * ROWS]
        high = value[:, (2 * i + 1) * ROWS : (2 * i + 2) * ROWS]
        chip = group * (GROUPS // 2) + i
        mine[chip] = jnp.where(core == 1, high, low)
        other[chip] = jnp.where(core == 1, low, high).astype(bf16)


def backward_body(info, limits, *refs):
    sources, refs = refs[:4], refs[4:]
    offsets, keys, values, own, one, two, three = refs[:7]
    both, mine, other, stats, key_acc, value_acc, keys_t, query_acc, rows, arrived = refs[7:]
    copies = row_copies(sources, rows, arrived)
    for copy in copies:
        copy.start()
    for group in range(GROUPS):
        level, delta = joined((own, one, two, three), group)
        stats[group, :2, :] = level
        stats[group, 2:, :] = delta
    ctx_index = info[1]
    query_acc[...] = jnp.zeros(query_acc.shape, f32)
    key_acc[...] = jnp.zeros(key_acc.shape, f32)
    value_acc[...] = jnp.zeros(value_acc.shape, f32)
    for h in range(HEADS_HERE):
        keys_t[head_of(h), :] = turned(keys[:, head_of(h)])
    for copy in copies:
        copy.wait()

    def step(group, carry):
        for i in range(2):
            base = info[2 + i]
            span = span_of(i)

            def block(offset_row, span=span, base=base):
                for h in range(HEADS_HERE):
                    query = group_query(rows, ctx_index, group, h)
                    grad_t = group_grad(rows, ctx_index, group, h)
                    scores = mm(keys[span, head_of(h)], query, NT) * LOG2_SCALE
                    scores = masked(scores - stats[group, h : h + 1, :], base, offset_row)
                    probs = jnp.exp2(scores)
                    prob_grad = mm(values[span, head_of(h)], grad_t)
                    delta = stats[group, h + 2 : h + 3, :]
                    score_grad = (probs * (prob_grad - delta) * SCORE_SCALE).astype(bf16)
                    value_acc[span, head_of(h)] += mm(probs.astype(bf16), grad_t, NT)
                    key_acc[span, head_of(h)] += mm(score_grad, query)
                    query_acc[group, head_of(h), :] += mm(keys_t[head_of(h), span], score_grad)

            visit(limits, base, offsets, group, block)

        return carry

    lax.fori_loop(0, GROUPS, step, 0)
    both[:FEATURES, :] = turned(key_acc[...])
    both[FEATURES:, :] = turned(value_acc[...])
    for group in range(GROUPS):
        split_parity(ctx_index & 1, group, query_acc[group], mine, other)


def weight_body(info, *refs):
    sources, (both, mine, other, blocks, arrived) = refs[:TP_DEVICES], refs[TP_DEVICES:]
    flipped = (info[1] & 1) == 1
    copies = [
        pltpu.make_async_copy(source, blocks.at[r], arrived.at[r])
        for r, source in enumerate(sources)
    ]
    for copy in copies:
        copy.start()
    for r in range(TP_DEVICES):
        copies[r].wait()
        terms = mm(both[...], blocks[r])
        place = info[0] ^ r
        low, high = terms[:, :ROWS], terms[:, ROWS:]
        mine[place] = jnp.where(flipped, high, low)
        other[place] = jnp.where(flipped, low, high).astype(bf16)


def add_body(own, received, out):
    out[...] = (own[...] + received[...].astype(f32)).astype(bf16)


def spread_z_body(info, own, received, kept, one, two, three):
    z = info[1] >> 2
    for y in range(2):
        place = 2 * z + y
        kept[y] = own[place] + received[place].astype(f32)
        for code, out in ((1, one), (2, two), (3, three)):
            place = 2 * (z ^ code) + y
            out[y] = (own[place] + received[place].astype(f32)).astype(bf16)


def spread_y_body(info, own, one, two, three, kept, sent):
    y = (info[1] >> 1) & 1
    for place, out in ((y, kept), (1 - y, sent)):
        total = own[place]
        for term in (one, two, three):
            total += term[place].astype(f32)
        out[...] = total.astype(out.dtype)


def finish_body(terms, key_grad, value_grad):
    total = total_of(terms).T
    key_grad[...] = total[:, :FEATURES]
    value_grad[...] = total[:, FEATURES:]


def weighted_sum(blocks):
    heads = []
    for h in range(HEADS_HERE):
        levels = []
        for i in range(CTX_DEVICES):
            pieces = blocks[i, FEATURES:, :].astype(f32)[3 * h : 3 * h + 3]
            levels.append(pieces[0:1] + pieces[1:2] + pieces[2:3])
        top = levels[0]
        for level in levels[1:]:
            top = jnp.maximum(top, level)
        weights = [jnp.exp2(level - top) for level in levels]
        scale = 1.0 / sum(weights)
        total = jnp.zeros((HEAD_DIM, ROWS), f32)
        for i in range(CTX_DEVICES):
            total += weights[i] * blocks[i, head_of(h), :].astype(f32)
        heads.append(total * scale)
    return jnp.concatenate(heads, axis=0)


def total_of(terms):
    total = terms[0].astype(f32)
    for i in range(1, terms.shape[0]):
        total = total + terms[i].astype(f32)
    return total


def close_body(info, w_out, w_query, attended_terms, query_kept, query_rest, *outs):
    attended = weighted_sum(attended_terms).T.astype(bf16)
    query_grad = (query_kept[...] + query_rest[...].astype(f32)).T.astype(bf16)
    for r in range(TP_DEVICES):
        part = pl.ds(shard_start(info[0], r), FEATURES)
        cross = mm(attended, w_out[:, part])
        latent = mm(query_grad, w_query[part, :], NT)
        outs[r][:, :FEATURES] = cross.astype(outs[r].dtype)
        outs[r][:, FEATURES:] = latent.astype(outs[r].dtype)


def shards(token_ids, embed_table, latents, w_query, w_key, w_value, w_out, out_grad, offsets):
    ctx_index = lax.axis_index("ctx").astype(jnp.int32)
    tp_index = lax.axis_index("tp").astype(jnp.int32)
    key_count = token_ids.shape[0]

    mirror_ids = swap(token_ids[SPAN:], "ctx", CTX_DEVICES - 1)
    info = jnp.stack(
        [
            tp_index,
            ctx_index,
            ctx_index * key_count,
            (CTX_DEVICES - 1 - ctx_index) * key_count + SPAN,
        ]
    )
    grouped = offsets.reshape(GROUPS, GROUP_ROWS)
    limits = jnp.stack([jnp.max(grouped, axis=1), jnp.min(grouped, axis=1)])
    offset_rows = offsets.reshape(GROUPS, 1, GROUP_ROWS)

    row_part = jnp.concatenate([latents, out_grad], axis=0)
    row_part, mirror_ids = lax.optimization_barrier((row_part, mirror_ids))
    near, back, side = (swap(row_part, "tp", bits) for bits in (1, 3, 4))
    far, side_near, side_back = far_blocks(near, back, side)
    ids = jnp.concatenate([token_ids[:SPAN], mirror_ids])
    context_part = embed_table.at[ids].get(mode="promise_in_bounds")
    far, side_near, side_back, context_part = lax.optimization_barrier(
        (far, side_near, side_back, context_part)
    )
    side_far = swap(side_back, "tp", 1)
    context_back, context_side = swap(context_part, "tp", 3), swap(context_part, "tp", 4)
    side_far, context_late = lax.optimization_barrier((side_far, context_part))
    context_first = (swap(context_late, "tp", 1), context_back, context_side)
    row_blocks = [row_part, near, far, back, side, side_near, side_far, side_back]

    own = kernel_call(
        rows_body,
        [((2 * ROWS, FEATURES), bf16)],
        [info],
        [w_query, w_out] + row_blocks,
    )[0]
    beside, context_first = lax.optimization_barrier((swap(own, "ctx", 2), context_first))
    rows = gather_ctx(own, beside)
    near, back, side = context_first
    far, side_near, side_back = far_blocks(near, back, side)
    side_far = swap(side_back, "tp", 1)
    context = [context_part, near, far, back, side, side_near, side_far, side_back]
    begun = kernel_call(
        project_body,
        [((2 * SPAN, 2 * FEATURES), f32)],
        [info],
        [w_key, w_value] + [context[r] for r in FIRST_PEERS],
        flops=20_000_000_000,
    )[0]

    part_shape = (CHIPS, FEATURES, ROWS)
    stats_shape = (GROUPS, 4, GROUP_ROWS)
    rows_scratch = [
        pltpu.VMEM((2, CHIPS, 2 * ROWS, FEATURES), bf16),
        pltpu.SemaphoreType.DMA((4,)),
    ]
    keys, values, local, out_blocks = kernel_call(
        forward_body,
        [
            ((2 * SPAN, FEATURES), bf16),
            ((2 * SPAN, FEATURES), bf16),
            (stats_shape, f32),
            ((CTX_DEVICES, FEATURES + LEVEL_ROWS, ROWS), bf16),
        ],
        [info, limits],
        [offset_rows, w_key, w_value, begun, context[LAST_PEER]],
        unfetched=rows,
        scratch=[
            pltpu.VMEM((FEATURES, 2 * SPAN), bf16),
            pltpu.VMEM((FEATURES, GROUP_ROWS), f32),
        ]
        + rows_scratch,
    )

    chip = kernel_call(
        join_body,
        [(stats_shape, f32)],
        [],
        [local] + [swap(local, "ctx", code) for code in (1, 2, 3)],
        room=8,
    )[0]
    chips = [chip] + [swap(chip, "ctx", code) for code in (4, 8, 12)]
    out_blocks, chips = lax.optimization_barrier((out_blocks, chips))
    attended_terms = exchange(out_blocks, "ctx")

    both, own_query, other_query = kernel_call(
        backward_body,
        [((2 * FEATURES, 2 * SPAN), bf16), (part_shape, f32), (part_shape, bf16)],
        [info, limits],
        [offset_rows, keys, values] + chips,
        unfetched=rows,
        scratch=[
            pltpu.VMEM(stats_shape, f32),
            pltpu.VMEM((2 * SPAN, FEATURES), f32),
            pltpu.VMEM((2 * SPAN, FEATURES), f32),
            pltpu.VMEM((FEATURES, 2 * SPAN), bf16),
            pltpu.VMEM((GROUPS, FEATURES, GROUP_ROWS), f32),
        ]
        + rows_scratch,
    )
    query_shape = (FEATURES, ROWS)
    kept, *sent = kernel_call(
        spread_z_body,
        [((2,) + query_shape, f32)] + [((2,) + query_shape, bf16)] * 3,
        [info],
        [own_query, swap(other_query, "ctx", 1)],
        room=16,
    )
    both, sent = lax.optimization_barrier((both, sent))
    arriving = [swap(block, "ctx", 4 * code) for code, block in zip((1, 2, 3), sent)]
    block_shape = (CHIPS, 2 * FEATURES, ROWS)
    own_weight, other_weight = kernel_call(
        weight_body,
        [(block_shape, f32), (block_shape, bf16)],
        [info],
        [both],
        unfetched=context,
        scratch=[
            pltpu.VMEM((TP_DEVICES, 2 * SPAN, FEATURES), bf16),
            pltpu.SemaphoreType.DMA((TP_DEVICES,)),
        ],
    )
    own_weight, other_weight, attended_terms, arriving = lax.optimization_barrier(
        (own_weight, other_weight, attended_terms, arriving)
    )
    query_kept, sent = kernel_call(
        spread_y_body,
        [(query_shape, f32), (query_shape, bf16)],
        [info],
        [kept] + arriving,
        room=16,
    )
    weight_blocks = kernel_call(
        add_body,
        [(block_shape, bf16)],
        [],
        [own_weight, swap(other_weight, "ctx", 1)],
        room=16,
    )[0]
    query_rest, weight_blocks = lax.optimization_barrier((swap(sent, "ctx", 2), weight_blocks))
    same_core = [list(range(core, CTX_DEVICES, 2)) for core in range(2)]
    key_grad, value_grad = kernel_call(
        finish_body,
        [((ROWS, FEATURES), f32)] * 2,
        [],
        [exchange(weight_blocks, "ctx", same_core)],
        room=16,
    )

    terms = kernel_call(
        close_body,
        [((ROWS, 2 * FEATURES), f32)] + [((ROWS, 2 * FEATURES), bf16)] * (TP_DEVICES - 1),
        [info],
        [w_out, w_query, attended_terms, query_kept, query_rest],
        room=16,
    )
    total = terms[0]
    for r in range(1, TP_DEVICES):
        total = total + swap(terms[r], "tp", r).astype(f32)
    total = total.astype(bf16)
    return (
        total[:, :FEATURES],
        total[:, FEATURES:],
        key_grad,
        value_grad,
    )


def solution(mesh):
    placed = (
        P("ctx"),
        P(None, "tp"),
        P("ctx", "tp"),
        P(None, "tp"),
        P(None, "tp"),
        P(None, "tp"),
        P("tp", None),
        P("ctx", "tp"),
        P(),
    )
    return jax.shard_map(
        shards,
        mesh=mesh,
        in_specs=placed,
        out_specs=(P("ctx", "tp"), P("ctx", "tp"), P("ctx", "tp"), P("ctx", "tp")),
        check_vma=False,
    )
```

```python
import math

import jax
import jax.numpy as jnp
from jax import lax
from jax.experimental import pallas as pl
from jax.experimental.pallas import tpu as pltpu
from jax.sharding import PartitionSpec as P

HEAD_DIM = 128
CTX_DEVICES = 16
TP_DEVICES = 8
FEATURES = 256
HEADS_HERE = FEATURES // HEAD_DIM
ROWS = 128
LAST_PEER = 6
FIRST_PEERS = (0, 1, 2, 3, 4, 5, 7)
CHIPS = CTX_DEVICES // 2
GROUPS = 4
LEVEL_ROWS = 16
GROUP_ROWS = 4 * ROWS
SPAN = 512

SCORE_SCALE = 1.0 / math.sqrt(HEAD_DIM)
LOG2_SCALE = SCORE_SCALE * math.log2(math.e)
MASKED = -1e30
FLOOR = -1e29

NN = (((1,), (0,)), ((), ()))
NT = (((1,), (1,)), ((), ()))
TN = (((0,), (0,)), ((), ()))

bf16 = jnp.bfloat16
f32 = jnp.float32


def mm(left, right, dims=NN):
    return lax.dot_general(left, right, dims, preferred_element_type=f32)


def swap(value, axis, bits):
    count = CTX_DEVICES if axis == "ctx" else TP_DEVICES
    return lax.ppermute(value, axis, [(i, i ^ bits) for i in range(count)])


def exchange(value, axis, groups=None):
    return lax.all_to_all(value, axis, 0, 0, axis_index_groups=groups, tiled=True)


def kernel_call(body, outs, scalars, arrays, scratch=(), room=16, flops=0):
    call = pl.pallas_call(
        body,
        out_shape=[jax.ShapeDtypeStruct(shape, kind) for shape, kind in outs],
        in_specs=[pl.BlockSpec(memory_space=pltpu.SMEM)] * len(scalars)
        + [pl.BlockSpec(memory_space=pltpu.VMEM)] * len(arrays),
        out_specs=[pl.BlockSpec(memory_space=pltpu.VMEM)] * len(outs),
        scratch_shapes=list(scratch),
        compiler_params=pltpu.CompilerParams(vmem_limit_bytes=room * 1024 * 1024),
        cost_estimate=pl.CostEstimate(flops=flops, bytes_accessed=0, transcendentals=0),
    )
    return list(call(*scalars, *arrays))


def far_blocks(near, back, side):
    return swap(back, "tp", 1), swap(near, "tp", 4), swap(side, "tp", 3)


def gather_ctx(block, beside):
    two = jnp.stack([block, beside])
    one, other, last = [swap(two, "ctx", code) for code in (4, 8, 12)]
    even = [jnp.concatenate([two, one], axis=0), jnp.concatenate([other, last], axis=0)]
    return jnp.concatenate(even + [swap(half, "ctx", 1) for half in even], axis=0)


def shard_start(tp_index, r):
    return pl.multiple_of((tp_index ^ r) * FEATURES, FEATURES)


def head_of(h):
    return slice(h * HEAD_DIM, (h + 1) * HEAD_DIM)


def rows_body(info, w_query, w_out, *refs):
    blocks, out = refs[:-1], refs[-1]
    query = jnp.zeros((ROWS, FEATURES), f32)
    grads = [jnp.zeros((HEAD_DIM, ROWS), f32) for _ in range(HEADS_HERE)]
    for r in range(TP_DEVICES):
        part = pl.ds(shard_start(info[0], r), FEATURES)
        query += mm(blocks[r][:ROWS, :], w_query[part, :])
        for h in range(HEADS_HERE):
            grads[h] += mm(w_out[head_of(h), part], blocks[r][ROWS:, :], NT)
    out[:ROWS, :] = query.astype(bf16)
    for h in range(HEADS_HERE):
        out[ROWS:, head_of(h)] = grads[h].astype(bf16)


def row_block(rows, ctx_index, block):
    distance = ctx_index ^ block
    return rows.at[(distance & 1) * CHIPS + (distance >> 1)]


def group_query(rows, ctx_index, group, h):
    blocks = [row_block(rows, ctx_index, GROUPS * group + i) for i in range(GROUPS)]
    return jnp.concatenate([block[:ROWS, head_of(h)] for block in blocks], axis=0)


def group_grad(rows, ctx_index, group, h):
    blocks = [row_block(rows, ctx_index, GROUPS * group + i) for i in range(GROUPS)]
    return jnp.concatenate([block[ROWS:, head_of(h)] for block in blocks], axis=1)


def masked(scores, base, offset_row):
    if offset_row is None:
        return scores
    places = base + lax.broadcasted_iota(jnp.int32, (SPAN, GROUP_ROWS), 0)
    return jnp.where(places <= offset_row, scores, MASKED)


def visit(bounds, base, offsets, group, block):
    whole_seen = bounds[1, group] >= base + (SPAN - 1)

    @pl.when(whole_seen)
    def _():
        block(None)

    @pl.when(jnp.logical_and(bounds[0, group] >= base, jnp.logical_not(whole_seen)))
    def _():
        block(offsets[group])


def pieces_of(level):
    pieces = []
    for _ in range(3):
        piece = level.astype(bf16).astype(f32)
        pieces.append(piece)
        level = level - piece
    return pieces


def turned(value):
    return value.astype(f32).T.astype(bf16)


def span_of(i):
    return slice(i * SPAN, (i + 1) * SPAN)


def ordered_rows(weight, tp_index, order):
    return jnp.concatenate(
        [weight[pl.ds(shard_start(tp_index, r), FEATURES), :] for r in order], axis=0
    )


def project_body(info, w_key, w_value, *refs):
    context = jnp.concatenate([ref[...] for ref in refs[:-1]], axis=1)
    out = refs[-1]
    out[:, :FEATURES] = mm(context, ordered_rows(w_key, info[0], FIRST_PEERS))
    out[:, FEATURES:] = mm(context, ordered_rows(w_value, info[0], FIRST_PEERS))


def forward_body(info, limits, *refs):
    offsets, rows, w_key, w_value, begun, last = refs[:6]
    keys, values, stats, blocks, values_t, parts = refs[6:]
    ctx_index = info[1]
    start = shard_start(info[0], LAST_PEER)
    for i, (weight, out) in enumerate(((w_key, keys), (w_value, values))):
        rest = mm(last[...], weight[pl.ds(start, FEATURES), :])
        out[...] = (begun[:, i * FEATURES : (i + 1) * FEATURES] + rest).astype(bf16)
    for h in range(HEADS_HERE):
        values_t[head_of(h), :] = turned(values[:, head_of(h)])

    def step(group, carry):
        stats[group, :2, :] = jnp.full((2, GROUP_ROWS), MASKED, f32)
        stats[group, 2:, :] = jnp.zeros((2, GROUP_ROWS), f32)
        parts[...] = jnp.zeros((FEATURES, GROUP_ROWS), f32)
        for i in range(2):
            base = info[2 + i]

            def block(offset_row, i=i, base=base):
                for h in range(HEADS_HERE):
                    query = group_query(rows, ctx_index, group, h)
                    scores = mm(keys[span_of(i), head_of(h)], query, NT) * LOG2_SCALE
                    scores = masked(scores, base, offset_row)
                    old = stats[group, h : h + 1, :]
                    peak = jnp.maximum(jnp.max(scores, axis=0, keepdims=True), FLOOR)
                    peak = jnp.maximum(peak, old)
                    weights = jnp.exp2(scores - peak)
                    keep = jnp.exp2(old - peak)
                    total = keep * stats[group, h + 2 : h + 3, :]
                    total += jnp.sum(weights, axis=0, keepdims=True)
                    part = mm(values_t[head_of(h), span_of(i)], weights.astype(bf16))
                    parts[head_of(h), :] = keep * parts[head_of(h), :] + part
                    stats[group, h : h + 1, :] = peak
                    stats[group, h + 2 : h + 3, :] = total

            visit(limits, base, offsets, group, block)

        levels = []
        for h in range(HEADS_HERE):
            total = stats[group, h + 2 : h + 3, :]
            some = total > 0.0
            safe = jnp.where(some, total, 1.0)
            part = parts[head_of(h), :] * jnp.where(some, 1.0 / safe, 0.0)
            grad_t = group_grad(rows, ctx_index, group, h).astype(f32)
            level = jnp.where(some, stats[group, h : h + 1, :] + jnp.log2(safe), MASKED)
            stats[group, h : h + 1, :] = level
            stats[group, h + 2 : h + 3, :] = jnp.sum(part * grad_t, axis=0, keepdims=True)
            levels += pieces_of(level)
            for i in range(GROUPS):
                place = GROUPS * group + i
                lanes = slice(i * ROWS, (i + 1) * ROWS)
                blocks[place, head_of(h), :] = part[:, lanes].astype(bf16)
        levels.append(jnp.zeros((LEVEL_ROWS - len(levels), GROUP_ROWS), f32))
        levels = jnp.concatenate(levels, axis=0).astype(bf16)
        for i in range(GROUPS):
            place = GROUPS * group + i
            blocks[place, FEATURES:, :] = levels[:, i * ROWS : (i + 1) * ROWS]
        return carry

    lax.fori_loop(0, GROUPS, step, 0)


def joined(refs, group):
    pieces = [ref[group] for ref in refs]
    top = pieces[0][:2]
    for piece in pieces[1:]:
        top = jnp.maximum(top, piece[:2])
    total = jnp.zeros((2, GROUP_ROWS), f32)
    delta = jnp.zeros((2, GROUP_ROWS), f32)
    for piece in pieces:
        weight = jnp.exp2(piece[:2] - top)
        total += weight
        delta += weight * piece[2:]
    return top + jnp.log2(total), delta / total


def join_body(own, one, two, three, stats):
    for group in range(GROUPS):
        level, delta = joined((own, one, two, three), group)
        stats[group, :2, :] = level
        stats[group, 2:, :] = delta


def split_parity(core, group, value, mine, other):
    for i in range(GROUPS // 2):
        low = value[:, 2 * i * ROWS : (2 * i + 1) * ROWS]
        high = value[:, (2 * i + 1) * ROWS : (2 * i + 2) * ROWS]
        chip = group * (GROUPS // 2) + i
        mine[chip] = jnp.where(core == 1, high, low)
        other[chip] = jnp.where(core == 1, low, high).astype(bf16)


def backward_body(info, limits, *refs):
    offsets, rows, keys, values, own, one, two, three = refs[:8]
    both, mine, other, stats, key_acc, value_acc, keys_t, query_acc = refs[8:]
    for group in range(GROUPS):
        level, delta = joined((own, one, two, three), group)
        stats[group, :2, :] = level
        stats[group, 2:, :] = delta
    ctx_index = info[1]
    query_acc[...] = jnp.zeros(query_acc.shape, f32)
    key_acc[...] = jnp.zeros(key_acc.shape, f32)
    value_acc[...] = jnp.zeros(value_acc.shape, f32)
    for h in range(HEADS_HERE):
        keys_t[head_of(h), :] = turned(keys[:, head_of(h)])

    def step(group, carry):
        for i in range(2):
            base = info[2 + i]
            span = span_of(i)

            def block(offset_row, span=span, base=base):
                for h in range(HEADS_HERE):
                    query = group_query(rows, ctx_index, group, h)
                    grad_t = group_grad(rows, ctx_index, group, h)
                    scores = mm(keys[span, head_of(h)], query, NT) * LOG2_SCALE
                    scores = masked(scores - stats[group, h : h + 1, :], base, offset_row)
                    probs = jnp.exp2(scores)
                    prob_grad = mm(values[span, head_of(h)], grad_t)
                    delta = stats[group, h + 2 : h + 3, :]
                    score_grad = (probs * (prob_grad - delta) * SCORE_SCALE).astype(bf16)
                    value_acc[span, head_of(h)] += mm(probs.astype(bf16), grad_t, NT)
                    key_acc[span, head_of(h)] += mm(score_grad, query)
                    query_acc[group, head_of(h), :] += mm(keys_t[head_of(h), span], score_grad)

            visit(limits, base, offsets, group, block)

        return carry

    lax.fori_loop(0, GROUPS, step, 0)
    both[:FEATURES, :] = turned(key_acc[...])
    both[FEATURES:, :] = turned(value_acc[...])
    for group in range(GROUPS):
        split_parity(ctx_index & 1, group, query_acc[group], mine, other)


def weight_body(info, *refs):
    both, mine, other = refs[TP_DEVICES:]
    flipped = (info[1] & 1) == 1
    for r in range(TP_DEVICES):
        terms = mm(both[...], refs[r][...])
        place = info[0] ^ r
        low, high = terms[:, :ROWS], terms[:, ROWS:]
        mine[place] = jnp.where(flipped, high, low)
        other[place] = jnp.where(flipped, low, high).astype(bf16)


def add_body(own, received, out):
    out[...] = (own[...] + received[...].astype(f32)).astype(bf16)


def spread_z_body(info, own, received, kept, one, two, three):
    z = info[1] >> 2
    for y in range(2):
        place = 2 * z + y
        kept[y] = own[place] + received[place].astype(f32)
        for code, out in ((1, one), (2, two), (3, three)):
            place = 2 * (z ^ code) + y
            out[y] = (own[place] + received[place].astype(f32)).astype(bf16)


def spread_y_body(info, own, one, two, three, kept, sent):
    y = (info[1] >> 1) & 1
    for place, out in ((y, kept), (1 - y, sent)):
        total = own[place]
        for term in (one, two, three):
            total += term[place].astype(f32)
        out[...] = total.astype(out.dtype)


def finish_body(terms, key_grad, value_grad):
    total = total_of(terms).T
    key_grad[...] = total[:, :FEATURES]
    value_grad[...] = total[:, FEATURES:]


def weighted_sum(blocks):
    heads = []
    for h in range(HEADS_HERE):
        levels = []
        for i in range(CTX_DEVICES):
            pieces = blocks[i, FEATURES:, :].astype(f32)[3 * h : 3 * h + 3]
            levels.append(pieces[0:1] + pieces[1:2] + pieces[2:3])
        top = levels[0]
        for level in levels[1:]:
            top = jnp.maximum(top, level)
        weights = [jnp.exp2(level - top) for level in levels]
        scale = 1.0 / sum(weights)
        total = jnp.zeros((HEAD_DIM, ROWS), f32)
        for i in range(CTX_DEVICES):
            total += weights[i] * blocks[i, head_of(h), :].astype(f32)
        heads.append(total * scale)
    return jnp.concatenate(heads, axis=0)


def total_of(terms):
    total = terms[0].astype(f32)
    for i in range(1, terms.shape[0]):
        total = total + terms[i].astype(f32)
    return total


def close_body(info, w_out, w_query, attended_terms, query_kept, query_rest, *outs):
    attended = weighted_sum(attended_terms).T.astype(bf16)
    query_grad = (query_kept[...] + query_rest[...].astype(f32)).T.astype(bf16)
    for r in range(TP_DEVICES):
        part = pl.ds(shard_start(info[0], r), FEATURES)
        out = outs[r % 4]
        out[r // 4, :, :FEATURES] = mm(attended, w_out[:, part]).astype(out.dtype)
        out[r // 4, :, FEATURES:] = mm(query_grad, w_query[part, :], NT).astype(out.dtype)


def fold_body(own, one, two, three, kept, sent):
    for i, out in ((0, kept), (1, sent)):
        total = own[i]
        for term in (one, two, three):
            total += term[i].astype(f32)
        out[...] = total.astype(out.dtype)


def last_body(kept, rest, cross_out, latent_grad):
    total = (kept[...] + rest[...].astype(f32)).astype(bf16)
    cross_out[...] = total[:, :FEATURES]
    latent_grad[...] = total[:, FEATURES:]


def shards(token_ids, embed_table, latents, w_query, w_key, w_value, w_out, out_grad, offsets):
    ctx_index = lax.axis_index("ctx").astype(jnp.int32)
    tp_index = lax.axis_index("tp").astype(jnp.int32)
    key_count = token_ids.shape[0]

    mirror_ids = swap(token_ids[SPAN:], "ctx", CTX_DEVICES - 1)
    info = jnp.stack(
        [
            tp_index,
            ctx_index,
            ctx_index * key_count,
            (CTX_DEVICES - 1 - ctx_index) * key_count + SPAN,
        ]
    )
    grouped = offsets.reshape(GROUPS, GROUP_ROWS)
    limits = jnp.stack([jnp.max(grouped, axis=1), jnp.min(grouped, axis=1)])
    offset_rows = offsets.reshape(GROUPS, 1, GROUP_ROWS)

    row_part = jnp.concatenate([latents, out_grad], axis=0)
    row_part, mirror_ids = lax.optimization_barrier((row_part, mirror_ids))
    near, back, side = (swap(row_part, "tp", bits) for bits in (1, 3, 4))
    far, side_near, side_back = far_blocks(near, back, side)
    ids = jnp.concatenate([token_ids[:SPAN], mirror_ids])
    context_part = embed_table.at[ids].get(mode="promise_in_bounds")
    far, side_near, side_back, context_part = lax.optimization_barrier(
        (far, side_near, side_back, context_part)
    )
    side_far = swap(side_back, "tp", 1)
    context_back, context_side = swap(context_part, "tp", 3), swap(context_part, "tp", 4)
    side_far, context_late = lax.optimization_barrier((side_far, context_part))
    context_first = (swap(context_late, "tp", 1), context_back, context_side)
    row_blocks = [row_part, near, far, back, side, side_near, side_far, side_back]

    own = kernel_call(
        rows_body,
        [((2 * ROWS, FEATURES), bf16)],
        [info],
        [w_query, w_out] + row_blocks,
    )[0]
    beside, context_first = lax.optimization_barrier((swap(own, "ctx", 2), context_first))
    rows = gather_ctx(own, beside)
    near, back, side = context_first
    far, side_near, side_back = far_blocks(near, back, side)
    side_far = swap(side_back, "tp", 1)
    context = [context_part, near, far, back, side, side_near, side_far, side_back]
    begun = kernel_call(
        project_body,
        [((2 * SPAN, 2 * FEATURES), f32)],
        [info],
        [w_key, w_value] + [context[r] for r in FIRST_PEERS],
        flops=20_000_000_000,
    )[0]

    part_shape = (CHIPS, FEATURES, ROWS)
    stats_shape = (GROUPS, 4, GROUP_ROWS)
    keys, values, local, out_blocks = kernel_call(
        forward_body,
        [
            ((2 * SPAN, FEATURES), bf16),
            ((2 * SPAN, FEATURES), bf16),
            (stats_shape, f32),
            ((CTX_DEVICES, FEATURES + LEVEL_ROWS, ROWS), bf16),
        ],
        [info, limits],
        [offset_rows, rows, w_key, w_value, begun, context[LAST_PEER]],
        scratch=[
            pltpu.VMEM((FEATURES, 2 * SPAN), bf16),
            pltpu.VMEM((FEATURES, GROUP_ROWS), f32),
        ],
        room=24,
    )

    chip = kernel_call(
        join_body,
        [(stats_shape, f32)],
        [],
        [local] + [swap(local, "ctx", code) for code in (1, 2, 3)],
    )[0]
    chips = [chip] + [swap(chip, "ctx", code) for code in (4, 8, 12)]
    out_blocks, chips = lax.optimization_barrier((out_blocks, chips))
    attended_terms = exchange(out_blocks, "ctx")

    both, own_query, other_query = kernel_call(
        backward_body,
        [((2 * FEATURES, 2 * SPAN), bf16), (part_shape, f32), (part_shape, bf16)],
        [info, limits],
        [offset_rows, rows, keys, values] + chips,
        scratch=[
            pltpu.VMEM(stats_shape, f32),
            pltpu.VMEM((2 * SPAN, FEATURES), f32),
            pltpu.VMEM((2 * SPAN, FEATURES), f32),
            pltpu.VMEM((FEATURES, 2 * SPAN), bf16),
            pltpu.VMEM((GROUPS, FEATURES, GROUP_ROWS), f32),
        ],
        room=28,
    )
    query_shape = (FEATURES, ROWS)
    kept, *sent = kernel_call(
        spread_z_body,
        [((2,) + query_shape, f32)] + [((2,) + query_shape, bf16)] * 3,
        [info],
        [own_query, swap(other_query, "ctx", 1)],
    )
    both, sent = lax.optimization_barrier((both, sent))
    arriving = [swap(block, "ctx", 4 * code) for code, block in zip((1, 2, 3), sent)]
    block_shape = (CHIPS, 2 * FEATURES, ROWS)
    own_weight, other_weight = kernel_call(
        weight_body,
        [(block_shape, f32), (block_shape, bf16)],
        [info],
        context + [both],
    )
    own_weight, other_weight, attended_terms, arriving = lax.optimization_barrier(
        (own_weight, other_weight, attended_terms, arriving)
    )
    query_kept, sent = kernel_call(
        spread_y_body,
        [(query_shape, f32), (query_shape, bf16)],
        [info],
        [kept] + arriving,
    )
    weight_blocks = kernel_call(
        add_body,
        [(block_shape, bf16)],
        [],
        [own_weight, swap(other_weight, "ctx", 1)],
    )[0]
    query_rest, weight_blocks = lax.optimization_barrier((swap(sent, "ctx", 2), weight_blocks))
    same_core = [list(range(core, CTX_DEVICES, 2)) for core in range(2)]
    key_grad, value_grad = kernel_call(
        finish_body,
        [((ROWS, FEATURES), f32)] * 2,
        [],
        [exchange(weight_blocks, "ctx", same_core)],
    )

    pair_shape = (2, ROWS, 2 * FEATURES)
    own_terms, *terms = kernel_call(
        close_body,
        [(pair_shape, f32)] + [(pair_shape, bf16)] * 3,
        [info],
        [w_out, w_query, attended_terms, query_kept, query_rest],
    )
    kept, sent = kernel_call(
        fold_body,
        [(pair_shape[1:], f32), (pair_shape[1:], bf16)],
        [],
        [own_terms] + [swap(block, "tp", bits) for bits, block in zip((1, 2, 3), terms)],
    )
    cross_out, latent_grad = kernel_call(
        last_body, [((ROWS, FEATURES), bf16)] * 2, [], [kept, swap(sent, "tp", 4)]
    )
    return (
        cross_out,
        latent_grad,
        key_grad,
        value_grad,
    )


def solution(mesh):
    placed = (
        P("ctx"),
        P(None, "tp"),
        P("ctx", "tp"),
        P(None, "tp"),
        P(None, "tp"),
        P(None, "tp"),
        P("tp", None),
        P("ctx", "tp"),
        P(),
    )
    return jax.shard_map(
        shards,
        mesh=mesh,
        in_specs=placed,
        out_specs=(P("ctx", "tp"), P("ctx", "tp"), P("ctx", "tp"), P("ctx", "tp")),
        check_vma=False,
    )
```

```python
import math

import jax
import jax.numpy as jnp
from jax import lax
from jax.experimental import pallas as pl
from jax.experimental.pallas import tpu as pltpu
from jax.sharding import PartitionSpec as P

HEAD_DIM = 128
CTX_DEVICES = 16
TP_DEVICES = 8
FEATURES = 256
HEADS_HERE = FEATURES // HEAD_DIM
ROWS = 128
LAST_PEER = 6
FIRST_PEERS = (0, 1, 2, 3, 4, 5, 7)
CHIPS = CTX_DEVICES // 2
GROUPS = 4
LEVEL_ROWS = 16
GROUP_ROWS = 4 * ROWS
SPAN = 512

SCORE_SCALE = 1.0 / math.sqrt(HEAD_DIM)
LOG2_SCALE = SCORE_SCALE * math.log2(math.e)
MASKED = -1e30
FLOOR = -1e29

NN = (((1,), (0,)), ((), ()))
NT = (((1,), (1,)), ((), ()))
TN = (((0,), (0,)), ((), ()))

bf16 = jnp.bfloat16
f32 = jnp.float32


def mm(left, right, dims=NN):
    return lax.dot_general(left, right, dims, preferred_element_type=f32)


def swap(value, axis, bits):
    count = CTX_DEVICES if axis == "ctx" else TP_DEVICES
    return lax.ppermute(value, axis, [(i, i ^ bits) for i in range(count)])


def exchange(value, axis, groups=None):
    return lax.all_to_all(value, axis, 0, 0, axis_index_groups=groups, tiled=True)


def whole(shape):
    return pl.BlockSpec(shape, lambda i: (0,) * len(shape), pipeline_mode=pl.Buffered(1))


def kernel_call(body, outs, scalars, arrays, room=16):
    call = pl.pallas_call(
        body,
        grid=(1,),
        out_shape=[jax.ShapeDtypeStruct(shape, kind) for shape, kind in outs],
        in_specs=[pl.BlockSpec(memory_space=pltpu.SMEM)] * len(scalars)
        + [whole(a.shape) for a in arrays],
        out_specs=[whole(shape) for shape, _ in outs],
        compiler_params=pltpu.CompilerParams(vmem_limit_bytes=room * 1024 * 1024),
        cost_estimate=pl.CostEstimate(flops=0, bytes_accessed=0, transcendentals=0),
    )
    return list(call(*scalars, *arrays))


def resident_call(body, outs, scalars, arrays, far_in=(), far_out=(), scratch=(), room=16, flops=0):
    near, far = pl.BlockSpec(memory_space=pltpu.VMEM), pl.BlockSpec(memory_space=pltpu.HBM)
    call = pl.pallas_call(
        body,
        out_shape=[jax.ShapeDtypeStruct(shape, kind) for shape, kind in [*far_out, *outs]],
        in_specs=[pl.BlockSpec(memory_space=pltpu.SMEM)] * len(scalars)
        + [far] * len(far_in)
        + [near] * len(arrays),
        out_specs=[far] * len(far_out) + [near] * len(outs),
        scratch_shapes=list(scratch),
        compiler_params=pltpu.CompilerParams(vmem_limit_bytes=room * 1024 * 1024),
        cost_estimate=pl.CostEstimate(flops=flops, bytes_accessed=0, transcendentals=0),
    )
    return list(call(*scalars, *far_in, *arrays))


def far_blocks(near, back, side):
    return swap(back, "tp", 1), swap(near, "tp", 4), swap(side, "tp", 3)


def both_cores(chips):
    even = [jnp.concatenate(chips[i : i + 2], axis=0) for i in (0, 2)]
    return jnp.concatenate(even + [swap(half, "ctx", 1) for half in even], axis=0)


def shard_start(tp_index, r):
    return pl.multiple_of((tp_index ^ r) * FEATURES, FEATURES)


def head_of(h):
    return slice(h * HEAD_DIM, (h + 1) * HEAD_DIM)


def rows_body(info, w_query, w_out, *refs):
    blocks, out = refs[:-1], refs[-1]
    query = jnp.zeros((ROWS, FEATURES), f32)
    grads = [jnp.zeros((HEAD_DIM, ROWS), f32) for _ in range(HEADS_HERE)]
    for r in range(TP_DEVICES):
        part = pl.ds(shard_start(info[0], r), FEATURES)
        query += mm(blocks[r][:ROWS, :], w_query[part, :])
        for h in range(HEADS_HERE):
            grads[h] += mm(w_out[head_of(h), part], blocks[r][ROWS:, :], NT)
    out[:ROWS, :] = query.astype(bf16)
    for h in range(HEADS_HERE):
        out[ROWS:, head_of(h)] = grads[h].astype(bf16)


def row_block(rows, ctx_index, block):
    distance = ctx_index ^ block
    return rows.at[(distance & 1) * CHIPS + (distance >> 1)]


def group_query(rows, ctx_index, group, h):
    blocks = [row_block(rows, ctx_index, GROUPS * group + i) for i in range(GROUPS)]
    return jnp.concatenate([block[:ROWS, head_of(h)] for block in blocks], axis=0)


def group_grad(rows, ctx_index, group, h):
    blocks = [row_block(rows, ctx_index, GROUPS * group + i) for i in range(GROUPS)]
    return jnp.concatenate([block[ROWS:, head_of(h)] for block in blocks], axis=1)


def masked(scores, base, offset_row):
    if offset_row is None:
        return scores
    places = base + lax.broadcasted_iota(jnp.int32, (SPAN, GROUP_ROWS), 0)
    return jnp.where(places <= offset_row, scores, MASKED)


def visit(bounds, base, offsets, group, block):
    whole_seen = bounds[1, group] >= base + (SPAN - 1)

    @pl.when(whole_seen)
    def _():
        block(None)

    @pl.when(jnp.logical_and(bounds[0, group] >= base, jnp.logical_not(whole_seen)))
    def _():
        block(offsets[group])


def pieces_of(level):
    pieces = []
    for _ in range(3):
        piece = level.astype(bf16).astype(f32)
        pieces.append(piece)
        level = level - piece
    return pieces


def turned(value):
    return value.astype(f32).T.astype(bf16)


def span_of(i):
    return slice(i * SPAN, (i + 1) * SPAN)


def ordered_rows(weight, tp_index, order):
    return jnp.concatenate(
        [weight[pl.ds(shard_start(tp_index, r), FEATURES), :] for r in order], axis=0
    )


def project_body(info, w_key, w_value, *refs):
    context = jnp.concatenate([ref[...] for ref in refs[:-1]], axis=1)
    out = refs[-1]
    out[:, :FEATURES] = mm(context, ordered_rows(w_key, info[0], FIRST_PEERS))
    out[:, FEATURES:] = mm(context, ordered_rows(w_value, info[0], FIRST_PEERS))


def forward_body(info, limits, *refs):
    offsets, rows, w_key, w_value, begun, last, key_out, value_out = refs[:8]
    stats, blocks, keys, values, values_t, parts, copied = refs[8:]
    ctx_index = info[1]
    start = shard_start(info[0], LAST_PEER)
    for i, (weight, out) in enumerate(((w_key, keys), (w_value, values))):
        rest = mm(last[...], weight[pl.ds(start, FEATURES), :])
        out[...] = (begun[:, i * FEATURES : (i + 1) * FEATURES] + rest).astype(bf16)
    copies = [
        pltpu.make_async_copy(keys, key_out, copied.at[0]),
        pltpu.make_async_copy(values, value_out, copied.at[1]),
    ]
    for copy in copies:
        copy.start()
    for h in range(HEADS_HERE):
        values_t[head_of(h), :] = turned(values[:, head_of(h)])

    def step(group, carry):
        stats[group, :2, :] = jnp.full((2, GROUP_ROWS), MASKED, f32)
        stats[group, 2:, :] = jnp.zeros((2, GROUP_ROWS), f32)
        parts[...] = jnp.zeros((FEATURES, GROUP_ROWS), f32)
        for i in range(2):
            base = info[2 + i]

            def block(offset_row, i=i, base=base):
                for h in range(HEADS_HERE):
                    query = group_query(rows, ctx_index, group, h)
                    scores = mm(keys[span_of(i), head_of(h)], query, NT) * LOG2_SCALE
                    scores = masked(scores, base, offset_row)
                    old = stats[group, h : h + 1, :]
                    peak = jnp.maximum(jnp.max(scores, axis=0, keepdims=True), FLOOR)
                    peak = jnp.maximum(peak, old)
                    weights = jnp.exp2(scores - peak)
                    keep = jnp.exp2(old - peak)
                    total = keep * stats[group, h + 2 : h + 3, :]
                    total += jnp.sum(weights, axis=0, keepdims=True)
                    part = mm(values_t[head_of(h), span_of(i)], weights.astype(bf16))
                    parts[head_of(h), :] = keep * parts[head_of(h), :] + part
                    stats[group, h : h + 1, :] = peak
                    stats[group, h + 2 : h + 3, :] = total

            visit(limits, base, offsets, group, block)

        levels = []
        for h in range(HEADS_HERE):
            total = stats[group, h + 2 : h + 3, :]
            some = total > 0.0
            safe = jnp.where(some, total, 1.0)
            part = parts[head_of(h), :] * jnp.where(some, 1.0 / safe, 0.0)
            grad_t = group_grad(rows, ctx_index, group, h).astype(f32)
            level = jnp.where(some, stats[group, h : h + 1, :] + jnp.log2(safe), MASKED)
            stats[group, h : h + 1, :] = level
            stats[group, h + 2 : h + 3, :] = jnp.sum(part * grad_t, axis=0, keepdims=True)
            levels += pieces_of(level)
            for i in range(GROUPS):
                place = GROUPS * group + i
                lanes = slice(i * ROWS, (i + 1) * ROWS)
                blocks[place, head_of(h), :] = part[:, lanes].astype(bf16)
        levels.append(jnp.zeros((LEVEL_ROWS - len(levels), GROUP_ROWS), f32))
        levels = jnp.concatenate(levels, axis=0).astype(bf16)
        for i in range(GROUPS):
            place = GROUPS * group + i
            blocks[place, FEATURES:, :] = levels[:, i * ROWS : (i + 1) * ROWS]
        return carry

    lax.fori_loop(0, GROUPS, step, 0)
    for copy in copies:
        copy.wait()


def joined(refs, group):
    pieces = [ref[group] for ref in refs]
    top = pieces[0][:2]
    for piece in pieces[1:]:
        top = jnp.maximum(top, piece[:2])
    total = jnp.zeros((2, GROUP_ROWS), f32)
    delta = jnp.zeros((2, GROUP_ROWS), f32)
    for piece in pieces:
        weight = jnp.exp2(piece[:2] - top)
        total += weight
        delta += weight * piece[2:]
    return top + jnp.log2(total), delta / total


def join_body(own, one, two, three, stats):
    for group in range(GROUPS):
        level, delta = joined((own, one, two, three), group)
        stats[group, :2, :] = level
        stats[group, 2:, :] = delta


def split_parity(core, group, value, mine, other):
    for i in range(GROUPS // 2):
        low = value[:, 2 * i * ROWS : (2 * i + 1) * ROWS]
        high = value[:, (2 * i + 1) * ROWS : (2 * i + 2) * ROWS]
        chip = group * (GROUPS // 2) + i
        mine[chip] = jnp.where(core == 1, high, low)
        other[chip] = jnp.where(core == 1, low, high).astype(bf16)


def backward_body(info, limits, *refs):
    key_in, value_in, offsets, rows, own, one, two, three, both, mine, other = refs[:11]
    keys, values, stats, key_acc, value_acc, keys_t, query_acc, copied = refs[11:]
    copies = [
        pltpu.make_async_copy(key_in, keys, copied.at[0]),
        pltpu.make_async_copy(value_in, values, copied.at[1]),
    ]
    for copy in copies:
        copy.start()
    for group in range(GROUPS):
        level, delta = joined((own, one, two, three), group)
        stats[group, :2, :] = level
        stats[group, 2:, :] = delta
    ctx_index = info[1]
    query_acc[...] = jnp.zeros(query_acc.shape, f32)
    key_acc[...] = jnp.zeros(key_acc.shape, f32)
    value_acc[...] = jnp.zeros(value_acc.shape, f32)
    for copy in copies:
        copy.wait()
    for h in range(HEADS_HERE):
        keys_t[head_of(h), :] = turned(keys[:, head_of(h)])

    def step(group, carry):
        for i in range(2):
            base = info[2 + i]
            span = span_of(i)

            def block(offset_row, span=span, base=base):
                for h in range(HEADS_HERE):
                    query = group_query(rows, ctx_index, group, h)
                    grad_t = group_grad(rows, ctx_index, group, h)
                    scores = mm(keys[span, head_of(h)], query, NT) * LOG2_SCALE
                    scores = masked(scores - stats[group, h : h + 1, :], base, offset_row)
                    probs = jnp.exp2(scores)
                    prob_grad = mm(values[span, head_of(h)], grad_t)
                    delta = stats[group, h + 2 : h + 3, :]
                    score_grad = (probs * (prob_grad - delta) * SCORE_SCALE).astype(bf16)
                    value_acc[span, head_of(h)] += mm(probs.astype(bf16), grad_t, NT)
                    key_acc[span, head_of(h)] += mm(score_grad, query)
                    query_acc[group, head_of(h), :] += mm(keys_t[head_of(h), span], score_grad)

            visit(limits, base, offsets, group, block)

        return carry

    lax.fori_loop(0, GROUPS, step, 0)
    both[:FEATURES, :] = turned(key_acc[...])
    both[FEATURES:, :] = turned(value_acc[...])
    for group in range(GROUPS):
        split_parity(ctx_index & 1, group, query_acc[group], mine, other)


def weight_body(info, *refs):
    both, mine, other = refs[TP_DEVICES:]
    flipped = (info[1] & 1) == 1
    for r in range(TP_DEVICES):
        terms = mm(both[...], refs[r][...])
        place = info[0] ^ r
        low, high = terms[:, :ROWS], terms[:, ROWS:]
        mine[place] = jnp.where(flipped, high, low)
        other[place] = jnp.where(flipped, low, high).astype(bf16)


def add_body(own, received, out):
    out[...] = (own[...] + received[...].astype(f32)).astype(bf16)


def spread_z_body(info, own, received, kept, one, two, three):
    z = info[1] >> 2
    for y in range(2):
        place = 2 * z + y
        kept[y] = own[place] + received[place].astype(f32)
        for code, out in ((1, one), (2, two), (3, three)):
            place = 2 * (z ^ code) + y
            out[y] = (own[place] + received[place].astype(f32)).astype(bf16)


def spread_y_body(info, own, one, two, three, kept, sent):
    y = (info[1] >> 1) & 1
    for place, out in ((y, kept), (1 - y, sent)):
        total = own[place]
        for term in (one, two, three):
            total += term[place].astype(f32)
        out[...] = total.astype(out.dtype)


def finish_body(terms, key_grad, value_grad):
    total = total_of(terms).T
    key_grad[...] = total[:, :FEATURES]
    value_grad[...] = total[:, FEATURES:]


def weighted_sum(blocks):
    heads = []
    for h in range(HEADS_HERE):
        levels = []
        for i in range(CTX_DEVICES):
            pieces = blocks[i, FEATURES:, :].astype(f32)[3 * h : 3 * h + 3]
            levels.append(pieces[0:1] + pieces[1:2] + pieces[2:3])
        top = levels[0]
        for level in levels[1:]:
            top = jnp.maximum(top, level)
        weights = [jnp.exp2(level - top) for level in levels]
        scale = 1.0 / sum(weights)
        total = jnp.zeros((HEAD_DIM, ROWS), f32)
        for i in range(CTX_DEVICES):
            total += weights[i] * blocks[i, head_of(h), :].astype(f32)
        heads.append(total * scale)
    return jnp.concatenate(heads, axis=0)


def total_of(terms):
    total = terms[0].astype(f32)
    for i in range(1, terms.shape[0]):
        total = total + terms[i].astype(f32)
    return total


def cross_body(info, w_out, attended_terms, *outs):
    attended = weighted_sum(attended_terms).T.astype(bf16)
    for r in range(TP_DEVICES):
        terms = mm(attended, w_out[:, pl.ds(shard_start(info[0], r), FEATURES)])
        outs[r % 4][r // 4] = terms.astype(outs[r % 4].dtype)


def latent_body(info, w_query, query_kept, query_rest, *outs):
    query_grad = (query_kept[...] + query_rest[...].astype(f32)).T.astype(bf16)
    for r in range(TP_DEVICES):
        terms = mm(query_grad, w_query[pl.ds(shard_start(info[0], r), FEATURES), :], NT)
        outs[r % 4][r // 4] = terms.astype(outs[r % 4].dtype)


def fold_body(*refs):
    kept, sent = refs[8:]
    for i, out in ((0, kept), (1, sent)):
        for j in range(2):
            own, *rest = refs[4 * j : 4 * j + 4]
            total = own[i]
            for term in rest:
                total += term[i].astype(f32)
            out[:, j * FEATURES : (j + 1) * FEATURES] = total.astype(out.dtype)


def last_body(kept, rest, cross_out, latent_grad):
    total = (kept[...] + rest[...].astype(f32)).astype(bf16)
    cross_out[...] = total[:, :FEATURES]
    latent_grad[...] = total[:, FEATURES:]


def shards(token_ids, embed_table, latents, w_query, w_key, w_value, w_out, out_grad, offsets):
    ctx_index = lax.axis_index("ctx").astype(jnp.int32)
    tp_index = lax.axis_index("tp").astype(jnp.int32)
    key_count = token_ids.shape[0]

    mirror_ids = swap(token_ids[SPAN:], "ctx", CTX_DEVICES - 1)
    info = jnp.stack(
        [
            tp_index,
            ctx_index,
            ctx_index * key_count,
            (CTX_DEVICES - 1 - ctx_index) * key_count + SPAN,
        ]
    )
    grouped = offsets.reshape(GROUPS, GROUP_ROWS)
    limits = jnp.stack([jnp.max(grouped, axis=1), jnp.min(grouped, axis=1)])
    offset_rows = offsets.reshape(GROUPS, 1, GROUP_ROWS)

    row_part = jnp.concatenate([latents, out_grad], axis=0)
    row_part, mirror_ids = lax.optimization_barrier((row_part, mirror_ids))
    near, back, side = (swap(row_part, "tp", bits) for bits in (1, 3, 4))
    far, side_near, side_back = far_blocks(near, back, side)
    ids = jnp.concatenate([token_ids[:SPAN], mirror_ids])
    context_part = embed_table.at[ids].get(mode="promise_in_bounds")
    far, side_near, side_back, context_part = lax.optimization_barrier(
        (far, side_near, side_back, context_part)
    )
    side_far = swap(side_back, "tp", 1)
    context_back, context_side = swap(context_part, "tp", 3), swap(context_part, "tp", 4)
    side_far, context_late = lax.optimization_barrier((side_far, context_part))
    context_first = (swap(context_late, "tp", 1), context_back, context_side)
    row_blocks = [row_part, near, far, back, side, side_near, side_far, side_back]

    own = kernel_call(
        rows_body,
        [((2 * ROWS, FEATURES), bf16)],
        [info],
        [w_query, w_out] + row_blocks,
    )[0]
    beside, context_first = lax.optimization_barrier((swap(own, "ctx", 2), context_first))
    near, back, side = context_first
    far, side_near, side_back = far_blocks(near, back, side)
    side_far = swap(side_back, "tp", 1)
    chips = [jnp.stack([own, beside])]
    chips += [swap(chips[0], "ctx", code) for code in (4, 8, 12)]
    chips, far, side_near, side_back = lax.optimization_barrier(
        (chips, far, side_near, side_back)
    )
    rows = both_cores(chips)
    context = [context_part, near, far, back, side, side_near, side_far, side_back]
    begun = resident_call(
        project_body,
        [((2 * SPAN, 2 * FEATURES), f32)],
        [info],
        [w_key, w_value] + [context[r] for r in FIRST_PEERS],
    )[0]

    part_shape = (CHIPS, FEATURES, ROWS)
    stats_shape = (GROUPS, 4, GROUP_ROWS)
    span_kind = ((2 * SPAN, FEATURES), bf16)
    keys, values, local, out_blocks = resident_call(
        forward_body,
        [
            (stats_shape, f32),
            ((CTX_DEVICES, FEATURES + LEVEL_ROWS, ROWS), bf16),
        ],
        [info, limits],
        [offset_rows, rows, w_key, w_value, begun, context[LAST_PEER]],
        far_out=[span_kind] * 2,
        scratch=[
            pltpu.VMEM(*span_kind),
            pltpu.VMEM(*span_kind),
            pltpu.VMEM((FEATURES, 2 * SPAN), bf16),
            pltpu.VMEM((FEATURES, GROUP_ROWS), f32),
            pltpu.SemaphoreType.DMA((2,)),
        ],
        room=24,
    )

    chip = kernel_call(
        join_body,
        [(stats_shape, f32)],
        [],
        [local] + [swap(local, "ctx", code) for code in (1, 2, 3)],
    )[0]
    chips = [chip] + [swap(chip, "ctx", code) for code in (4, 8, 12)]
    out_blocks, chips = lax.optimization_barrier((out_blocks, chips))
    attended_terms = exchange(out_blocks, "ctx")

    both, own_query, other_query = resident_call(
        backward_body,
        [((2 * FEATURES, 2 * SPAN), bf16), (part_shape, f32), (part_shape, bf16)],
        [info, limits],
        [offset_rows, rows] + chips,
        far_in=[keys, values],
        scratch=[
            pltpu.VMEM(*span_kind),
            pltpu.VMEM(*span_kind),
            pltpu.VMEM(stats_shape, f32),
            pltpu.VMEM((2 * SPAN, FEATURES), f32),
            pltpu.VMEM((2 * SPAN, FEATURES), f32),
            pltpu.VMEM((FEATURES, 2 * SPAN), bf16),
            pltpu.VMEM((GROUPS, FEATURES, GROUP_ROWS), f32),
            pltpu.SemaphoreType.DMA((2,)),
        ],
        room=28,
    )
    query_shape = (FEATURES, ROWS)
    kept, *sent = kernel_call(
        spread_z_body,
        [((2,) + query_shape, f32)] + [((2,) + query_shape, bf16)] * 3,
        [info],
        [own_query, swap(other_query, "ctx", 1)],
    )
    both, sent = lax.optimization_barrier((both, sent))
    arriving = [swap(block, "ctx", 4 * code) for code, block in zip((1, 2, 3), sent)]
    block_shape = (CHIPS, 2 * FEATURES, ROWS)
    own_weight, other_weight = resident_call(
        weight_body,
        [(block_shape, f32), (block_shape, bf16)],
        [info],
        context + [both],
    )
    own_weight, other_weight, attended_terms, arriving = lax.optimization_barrier(
        (own_weight, other_weight, attended_terms, arriving)
    )
    pair_shape = (2, ROWS, FEATURES)
    tp_kinds = [(pair_shape, f32)] + [(pair_shape, bf16)] * 3
    own_cross, *cross_terms = kernel_call(cross_body, tp_kinds, [info], [w_out, attended_terms])
    cross_terms = [swap(block, "tp", i + 1) for i, block in enumerate(cross_terms)]
    query_kept, sent = kernel_call(
        spread_y_body,
        [(query_shape, f32), (query_shape, bf16)],
        [info],
        [kept] + arriving,
    )
    weight_blocks = kernel_call(
        add_body,
        [(block_shape, bf16)],
        [],
        [own_weight, swap(other_weight, "ctx", 1)],
    )[0]
    query_rest, weight_blocks = lax.optimization_barrier((swap(sent, "ctx", 2), weight_blocks))
    same_core = [list(range(core, CTX_DEVICES, 2)) for core in range(2)]
    key_grad, value_grad = kernel_call(
        finish_body,
        [((ROWS, FEATURES), f32)] * 2,
        [],
        [exchange(weight_blocks, "ctx", same_core)],
    )

    own_latent, *latent_terms = kernel_call(
        latent_body, tp_kinds, [info], [w_query, query_kept, query_rest]
    )
    latent_terms, cross_terms = lax.optimization_barrier((latent_terms, cross_terms))
    latent_terms = [swap(block, "tp", i + 1) for i, block in enumerate(latent_terms)]
    sum_shape = (ROWS, 2 * FEATURES)
    kept, sent = kernel_call(
        fold_body,
        [(sum_shape, f32), (sum_shape, bf16)],
        [],
        [own_cross] + cross_terms + [own_latent] + latent_terms,
    )
    cross_out, latent_grad = kernel_call(
        last_body, [((ROWS, FEATURES), bf16)] * 2, [], [kept, swap(sent, "tp", 4)]
    )
    return (
        cross_out,
        latent_grad,
        key_grad,
        value_grad,
    )


def solution(mesh):
    placed = (
        P("ctx"),
        P(None, "tp"),
        P("ctx", "tp"),
        P(None, "tp"),
        P(None, "tp"),
        P(None, "tp"),
        P("tp", None),
        P("ctx", "tp"),
        P(),
    )
    return jax.shard_map(
        shards,
        mesh=mesh,
        in_specs=placed,
        out_specs=(P("ctx", "tp"), P("ctx", "tp"), P("ctx", "tp"), P("ctx", "tp")),
        check_vma=False,
    )
```

```python
import math

import jax
import jax.numpy as jnp
from jax import lax
from jax.experimental import pallas as pl
from jax.experimental.pallas import tpu as pltpu
from jax.sharding import PartitionSpec as P

HEAD_DIM = 128
CTX_DEVICES = 16
TP_DEVICES = 8
FEATURES = 256
HEADS_HERE = FEATURES // HEAD_DIM
ROWS = 128
LAST_PEER = 6
FIRST_PEERS = (0, 1, 2, 3, 4, 5, 7)
CHIPS = CTX_DEVICES // 2
GROUPS = 4
STORED = 120
LEVEL_ROWS = 16
GROUP_ROWS = 4 * ROWS
SPAN = 512

SCORE_SCALE = 1.0 / math.sqrt(HEAD_DIM)
LOG2_SCALE = SCORE_SCALE * math.log2(math.e)
MASKED = -1e30
FLOOR = -1e29

NN = (((1,), (0,)), ((), ()))
NT = (((1,), (1,)), ((), ()))
TN = (((0,), (0,)), ((), ()))

bf16 = jnp.bfloat16
f32 = jnp.float32


def mm(left, right, dims=NN):
    return lax.dot_general(left, right, dims, preferred_element_type=f32)


def swap(value, axis, bits):
    count = CTX_DEVICES if axis == "ctx" else TP_DEVICES
    return lax.ppermute(value, axis, [(i, i ^ bits) for i in range(count)])


def exchange(value, axis, groups=None):
    return lax.all_to_all(value, axis, 0, 0, axis_index_groups=groups, tiled=True)


def whole(shape):
    return pl.BlockSpec(shape, lambda i: (0,) * len(shape), pipeline_mode=pl.Buffered(1))


def kernel_call(body, outs, scalars, arrays, room=16):
    call = pl.pallas_call(
        body,
        grid=(1,),
        out_shape=[jax.ShapeDtypeStruct(shape, kind) for shape, kind in outs],
        in_specs=[pl.BlockSpec(memory_space=pltpu.SMEM)] * len(scalars)
        + [whole(a.shape) for a in arrays],
        out_specs=[whole(shape) for shape, _ in outs],
        compiler_params=pltpu.CompilerParams(vmem_limit_bytes=room * 1024 * 1024),
        cost_estimate=pl.CostEstimate(flops=0, bytes_accessed=0, transcendentals=0),
    )
    return list(call(*scalars, *arrays))


def resident_call(body, outs, scalars, arrays, far_in=(), far_out=(), scratch=(), room=16, flops=0):
    near, far = pl.BlockSpec(memory_space=pltpu.VMEM), pl.BlockSpec(memory_space=pltpu.HBM)
    call = pl.pallas_call(
        body,
        out_shape=[jax.ShapeDtypeStruct(shape, kind) for shape, kind in [*far_out, *outs]],
        in_specs=[pl.BlockSpec(memory_space=pltpu.SMEM)] * len(scalars)
        + [far] * len(far_in)
        + [near] * len(arrays),
        out_specs=[far] * len(far_out) + [near] * len(outs),
        scratch_shapes=list(scratch),
        compiler_params=pltpu.CompilerParams(vmem_limit_bytes=room * 1024 * 1024),
        cost_estimate=pl.CostEstimate(flops=flops, bytes_accessed=0, transcendentals=0),
    )
    return list(call(*scalars, *far_in, *arrays))


def far_blocks(near, back, side):
    return swap(back, "tp", 1), swap(near, "tp", 4), swap(side, "tp", 3)


def both_cores(chips):
    return jnp.concatenate(chips + [swap(pair, "ctx", 1) for pair in chips], axis=0)


def shard_start(tp_index, r):
    return pl.multiple_of((tp_index ^ r) * FEATURES, FEATURES)


def head_of(h):
    return slice(h * HEAD_DIM, (h + 1) * HEAD_DIM)


def rows_body(info, w_query, w_out, *refs):
    blocks, out = refs[:-1], refs[-1]
    query = jnp.zeros((ROWS, FEATURES), f32)
    grads = [jnp.zeros((HEAD_DIM, ROWS), f32) for _ in range(HEADS_HERE)]
    for r in range(TP_DEVICES):
        part = pl.ds(shard_start(info[0], r), FEATURES)
        query += mm(blocks[r][:ROWS, :], w_query[part, :])
        for h in range(HEADS_HERE):
            grads[h] += mm(w_out[head_of(h), part], blocks[r][ROWS:, :], NT)
    out[:ROWS, :] = query.astype(bf16)
    for h in range(HEADS_HERE):
        out[ROWS:, head_of(h)] = grads[h].astype(bf16)


def row_block(rows, ctx_index, block):
    distance = ctx_index ^ block
    return rows.at[(distance & 1) * CHIPS + (distance >> 1)]


def group_query(rows, ctx_index, group, h):
    blocks = [row_block(rows, ctx_index, GROUPS * group + i) for i in range(GROUPS)]
    return jnp.concatenate([block[:ROWS, head_of(h)] for block in blocks], axis=0)


def group_grad(rows, ctx_index, group, h):
    blocks = [row_block(rows, ctx_index, GROUPS * group + i) for i in range(GROUPS)]
    return jnp.concatenate([block[ROWS:, head_of(h)] for block in blocks], axis=1)


def masked(scores, base, offset_row):
    if offset_row is None:
        return scores
    places = base + lax.broadcasted_iota(jnp.int32, (SPAN, GROUP_ROWS), 0)
    return jnp.where(places <= offset_row, scores, MASKED)


def visit(bounds, base, offsets, group, block):
    whole_seen = bounds[1, group] >= base + (SPAN - 1)

    @pl.when(whole_seen)
    def _():
        block(None)

    @pl.when(jnp.logical_and(bounds[0, group] >= base, jnp.logical_not(whole_seen)))
    def _():
        block(offsets[group])


def pieces_of(level):
    pieces = []
    for _ in range(3):
        piece = level.astype(bf16).astype(f32)
        pieces.append(piece)
        level = level - piece
    return pieces


def turned(value):
    return value.astype(f32).T.astype(bf16)


def span_of(i):
    return slice(i * SPAN, (i + 1) * SPAN)


def ordered_rows(weight, tp_index, order):
    return jnp.concatenate(
        [weight[pl.ds(shard_start(tp_index, r), FEATURES), :] for r in order], axis=0
    )


def project_body(info, w_key, w_value, *refs):
    context = jnp.concatenate([ref[...] for ref in refs[:-1]], axis=1)
    out = refs[-1]
    out[:, :FEATURES] = mm(context, ordered_rows(w_key, info[0], FIRST_PEERS))
    out[:, FEATURES:] = mm(context, ordered_rows(w_value, info[0], FIRST_PEERS))


def forward_body(info, limits, *refs):
    offsets, rows, w_key, w_value, begun, last, stored = refs[:7]
    stats, blocks, keys, values, values_t, parts, copied = refs[7:]
    ctx_index = info[1]
    start = shard_start(info[0], LAST_PEER)
    for i, (weight, out) in enumerate(((w_key, keys), (w_value, values))):
        rest = mm(last[...], weight[pl.ds(start, FEATURES), :])
        out[...] = (begun[:, i * FEATURES : (i + 1) * FEATURES] + rest).astype(bf16)
    copies = [
        pltpu.make_async_copy(keys, stored.at[0], copied.at[0]),
        pltpu.make_async_copy(values, stored.at[1], copied.at[1]),
    ]
    for copy in copies:
        copy.start()
    for h in range(HEADS_HERE):
        values_t[head_of(h), :] = turned(values[:, head_of(h)])

    def step(group, carry):
        stats[group, :2, :] = jnp.full((2, GROUP_ROWS), MASKED, f32)
        stats[group, 2:, :] = jnp.zeros((2, GROUP_ROWS), f32)
        parts[...] = jnp.zeros((FEATURES, GROUP_ROWS), f32)
        for i in range(2):
            base = info[2 + i]

            def block(offset_row, i=i, base=base):
                for h in range(HEADS_HERE):
                    query = group_query(rows, ctx_index, group, h)
                    scores = mm(keys[span_of(i), head_of(h)], query, NT) * LOG2_SCALE
                    scores = masked(scores, base, offset_row)
                    old = stats[group, h : h + 1, :]
                    peak = jnp.maximum(jnp.max(scores, axis=0, keepdims=True), FLOOR)
                    peak = jnp.maximum(peak, old)
                    weights = jnp.exp2(scores - peak)
                    keep = jnp.exp2(old - peak)
                    total = keep * stats[group, h + 2 : h + 3, :]
                    total += jnp.sum(weights, axis=0, keepdims=True)
                    part = mm(values_t[head_of(h), span_of(i)], weights.astype(bf16))
                    parts[head_of(h), :] = keep * parts[head_of(h), :] + part
                    stats[group, h : h + 1, :] = peak
                    stats[group, h + 2 : h + 3, :] = total

            visit(limits, base, offsets, group, block)

        levels = []
        for h in range(HEADS_HERE):
            total = stats[group, h + 2 : h + 3, :]
            some = total > 0.0
            safe = jnp.where(some, total, 1.0)
            part = parts[head_of(h), :] * jnp.where(some, 1.0 / safe, 0.0)
            grad_t = group_grad(rows, ctx_index, group, h).astype(f32)
            level = jnp.where(some, stats[group, h : h + 1, :] + jnp.log2(safe), MASKED)
            stats[group, h : h + 1, :] = level
            stats[group, h + 2 : h + 3, :] = jnp.sum(part * grad_t, axis=0, keepdims=True)
            levels += pieces_of(level)
            for i in range(GROUPS):
                place = GROUPS * group + i
                lanes = slice(i * ROWS, (i + 1) * ROWS)
                blocks[place, head_of(h), :] = part[:, lanes].astype(bf16)
        levels.append(jnp.zeros((LEVEL_ROWS - len(levels), GROUP_ROWS), f32))
        levels = jnp.concatenate(levels, axis=0).astype(bf16)
        for i in range(GROUPS):
            place = GROUPS * group + i
            blocks[place, FEATURES:, :] = levels[:, i * ROWS : (i + 1) * ROWS]
        return carry

    lax.fori_loop(0, GROUPS, step, 0)
    for copy in copies:
        copy.wait()


def joined(refs, group):
    pieces = [ref[group] for ref in refs]
    top = pieces[0][:2]
    for piece in pieces[1:]:
        top = jnp.maximum(top, piece[:2])
    total = jnp.zeros((2, GROUP_ROWS), f32)
    delta = jnp.zeros((2, GROUP_ROWS), f32)
    for piece in pieces:
        weight = jnp.exp2(piece[:2] - top)
        total += weight
        delta += weight * piece[2:]
    return top + jnp.log2(total), delta / total


def join_body(own, one, two, three, stats):
    for group in range(GROUPS):
        level, delta = joined((own, one, two, three), group)
        stats[group, :2, :] = level
        stats[group, 2:, :] = delta


def split_parity(core, group, value, mine, other):
    for i in range(GROUPS // 2):
        low = value[:, 2 * i * ROWS : (2 * i + 1) * ROWS]
        high = value[:, (2 * i + 1) * ROWS : (2 * i + 2) * ROWS]
        chip = group * (GROUPS // 2) + i
        mine[chip] = jnp.where(core == 1, high, low)
        other[chip] = jnp.where(core == 1, low, high).astype(bf16)


def backward_body(info, limits, *refs):
    stored, offsets, rows, own, one, two, three, both, mine, other = refs[:10]
    keys, values, stats, key_acc, value_acc, keys_t, query_acc, copied = refs[10:]
    copies = [
        pltpu.make_async_copy(stored.at[0], keys, copied.at[0]),
        pltpu.make_async_copy(stored.at[1], values, copied.at[1]),
    ]
    for copy in copies:
        copy.start()
    for group in range(GROUPS):
        level, delta = joined((own, one, two, three), group)
        stats[group, :2, :] = level
        stats[group, 2:, :] = delta
    ctx_index = info[1]
    query_acc[...] = jnp.zeros(query_acc.shape, f32)
    key_acc[...] = jnp.zeros(key_acc.shape, f32)
    value_acc[...] = jnp.zeros(value_acc.shape, f32)
    for copy in copies:
        copy.wait()
    for h in range(HEADS_HERE):
        keys_t[head_of(h), :] = turned(keys[:, head_of(h)])

    def step(group, carry):
        for i in range(2):
            base = info[2 + i]
            span = span_of(i)

            def block(offset_row, span=span, base=base):
                for h in range(HEADS_HERE):
                    query = group_query(rows, ctx_index, group, h)
                    grad_t = group_grad(rows, ctx_index, group, h)
                    scores = mm(keys[span, head_of(h)], query, NT) * LOG2_SCALE
                    scores = masked(scores - stats[group, h : h + 1, :], base, offset_row)
                    probs = jnp.exp2(scores)
                    prob_grad = mm(values[span, head_of(h)], grad_t)
                    delta = stats[group, h + 2 : h + 3, :]
                    score_grad = (probs * (prob_grad - delta) * SCORE_SCALE).astype(bf16)
                    value_acc[span, head_of(h)] += mm(probs.astype(bf16), grad_t, NT)
                    key_acc[span, head_of(h)] += mm(score_grad, query)
                    query_acc[group, head_of(h), :] += mm(keys_t[head_of(h), span], score_grad)

            visit(limits, base, offsets, group, block)

        return carry

    lax.fori_loop(0, GROUPS, step, 0)
    both[:FEATURES, :] = turned(key_acc[...])
    both[FEATURES:, :] = turned(value_acc[...])
    for group in range(GROUPS):
        split_parity(ctx_index & 1, group, query_acc[group], mine, other)


def weight_body(info, *refs):
    both, mine, other = refs[TP_DEVICES:]
    flipped = (info[1] & 1) == 1
    for r in range(TP_DEVICES):
        terms = mm(both[...], refs[r][...])
        place = info[0] ^ r
        low, high = terms[:, :ROWS], terms[:, ROWS:]
        mine[place] = jnp.where(flipped, high, low)
        other[place] = jnp.where(flipped, low, high).astype(bf16)


def add_body(own, received, out):
    out[...] = (own[...] + received[...].astype(f32)).astype(bf16)


def spread_z_body(info, own, received, kept, one, two, three):
    z = info[1] >> 2
    for y in range(2):
        place = 2 * z + y
        kept[y] = own[place] + received[place].astype(f32)
        for code, out in ((1, one), (2, two), (3, three)):
            place = 2 * (z ^ code) + y
            out[y] = (own[place] + received[place].astype(f32)).astype(bf16)


def spread_y_body(info, own, one, two, three, kept, sent):
    y = (info[1] >> 1) & 1
    for place, out in ((y, kept), (1 - y, sent)):
        total = own[place]
        for term in (one, two, three):
            total += term[place].astype(f32)
        out[...] = total.astype(out.dtype)


def finish_body(terms, key_grad, value_grad):
    total = total_of(terms).T
    key_grad[...] = total[:, :FEATURES]
    value_grad[...] = total[:, FEATURES:]


def weighted_sum(blocks):
    heads = []
    for h in range(HEADS_HERE):
        levels = []
        for i in range(CTX_DEVICES):
            pieces = blocks[i, FEATURES:, :].astype(f32)[3 * h : 3 * h + 3]
            levels.append(pieces[0:1] + pieces[1:2] + pieces[2:3])
        top = levels[0]
        for level in levels[1:]:
            top = jnp.maximum(top, level)
        weights = [jnp.exp2(level - top) for level in levels]
        scale = 1.0 / sum(weights)
        total = jnp.zeros((HEAD_DIM, ROWS), f32)
        for i in range(CTX_DEVICES):
            total += weights[i] * blocks[i, head_of(h), :].astype(f32)
        heads.append(total * scale)
    return jnp.concatenate(heads, axis=0)


def total_of(terms):
    total = terms[0].astype(f32)
    for i in range(1, terms.shape[0]):
        total = total + terms[i].astype(f32)
    return total


def close_body(info, w_out, w_query, attended_terms, query_kept, query_rest, *outs):
    attended = weighted_sum(attended_terms).T.astype(bf16)
    query_grad = (query_kept[...] + query_rest[...].astype(f32)).T.astype(bf16)
    for r in range(TP_DEVICES):
        part = pl.ds(shard_start(info[0], r), FEATURES)
        out = outs[r % 4]
        out[r // 4, :, :FEATURES] = mm(attended, w_out[:, part]).astype(out.dtype)
        out[r // 4, :, FEATURES:] = mm(query_grad, w_query[part, :], NT).astype(out.dtype)


def fold_body(own, one, two, three, kept, sent):
    for i, out in ((0, kept), (1, sent)):
        total = own[i]
        for term in (one, two, three):
            total += term[i].astype(f32)
        out[...] = total.astype(out.dtype)


def last_body(kept, rest, cross_out, latent_grad):
    total = (kept[...] + rest[...].astype(f32)).astype(bf16)
    cross_out[...] = total[:, :FEATURES]
    latent_grad[...] = total[:, FEATURES:]


def shards(token_ids, embed_table, latents, w_query, w_key, w_value, w_out, out_grad, offsets):
    ctx_index = lax.axis_index("ctx").astype(jnp.int32)
    tp_index = lax.axis_index("tp").astype(jnp.int32)
    key_count = token_ids.shape[0]

    mirror_ids = swap(token_ids[SPAN:], "ctx", CTX_DEVICES - 1)
    info = jnp.stack(
        [
            tp_index,
            ctx_index,
            ctx_index * key_count,
            (CTX_DEVICES - 1 - ctx_index) * key_count + SPAN,
        ]
    )
    grouped = offsets.reshape(GROUPS, GROUP_ROWS)
    limits = jnp.stack([jnp.max(grouped, axis=1), jnp.min(grouped, axis=1)])
    offset_rows = offsets.reshape(GROUPS, 1, GROUP_ROWS)

    row_part = jnp.concatenate([latents, out_grad], axis=0)
    row_part, mirror_ids, info, limits, offset_rows = lax.optimization_barrier(
        (row_part, mirror_ids, info, limits, offset_rows)
    )
    near, back, side = (swap(row_part, "tp", bits) for bits in (1, 3, 4))
    far, side_near, side_back = far_blocks(near, back, side)
    ids = jnp.concatenate([token_ids[:SPAN], mirror_ids])
    context_part = embed_table.at[ids].get(mode="promise_in_bounds")
    far, side_near, side_back, context_part = lax.optimization_barrier(
        (far, side_near, side_back, context_part)
    )
    side_far = swap(side_back, "tp", 1)
    context_back, context_side = swap(context_part, "tp", 3), swap(context_part, "tp", 4)
    side_far, context_late = lax.optimization_barrier((side_far, context_part))
    context_first = (swap(context_late, "tp", 1), context_back, context_side)
    row_blocks = [row_part, near, far, back, side, side_near, side_far, side_back]

    own = kernel_call(
        rows_body,
        [((2 * ROWS, FEATURES), bf16)],
        [info],
        [w_query, w_out] + row_blocks,
        room=60,
    )[0]
    beside, context_first = lax.optimization_barrier((swap(own, "ctx", 2), context_first))
    near, back, side = context_first
    far, side_near, side_back = lax.optimization_barrier(far_blocks(near, back, side))
    side_far = swap(side_back, "tp", 1)
    chips = [jnp.stack([own, beside])]
    chips += [swap(chips[0], "ctx", code) for code in (4, 8, 12)]
    chips, far = lax.optimization_barrier((chips, far))
    rows = both_cores(chips)
    context = [context_part, near, far, back, side, side_near, side_far, side_back]
    begun = resident_call(
        project_body,
        [((2 * SPAN, 2 * FEATURES), f32)],
        [info],
        [w_key, w_value] + [context[r] for r in FIRST_PEERS],
    )[0]

    part_shape = (CHIPS, FEATURES, ROWS)
    stats_shape = (GROUPS, 4, GROUP_ROWS)
    span_kind = ((2 * SPAN, FEATURES), bf16)
    stored, local, out_blocks = resident_call(
        forward_body,
        [
            (stats_shape, f32),
            ((CTX_DEVICES, FEATURES + LEVEL_ROWS, ROWS), bf16),
        ],
        [info, limits],
        [offset_rows, rows, w_key, w_value, begun, context[LAST_PEER]],
        far_out=[((STORED,) + span_kind[0], bf16)],
        scratch=[
            pltpu.VMEM(*span_kind),
            pltpu.VMEM(*span_kind),
            pltpu.VMEM((FEATURES, 2 * SPAN), bf16),
            pltpu.VMEM((FEATURES, GROUP_ROWS), f32),
            pltpu.SemaphoreType.DMA((2,)),
        ],
        room=24,
    )

    chip = kernel_call(
        join_body,
        [(stats_shape, f32)],
        [],
        [local] + [swap(local, "ctx", code) for code in (1, 2, 3)],
    )[0]
    chips = [chip] + [swap(chip, "ctx", code) for code in (4, 8, 12)]
    out_blocks, chips = lax.optimization_barrier((out_blocks, chips))
    attended_terms = exchange(out_blocks, "ctx")

    both, own_query, other_query = resident_call(
        backward_body,
        [((2 * FEATURES, 2 * SPAN), bf16), (part_shape, f32), (part_shape, bf16)],
        [info, limits],
        [offset_rows, rows] + chips,
        far_in=[stored],
        scratch=[
            pltpu.VMEM(*span_kind),
            pltpu.VMEM(*span_kind),
            pltpu.VMEM(stats_shape, f32),
            pltpu.VMEM((2 * SPAN, FEATURES), f32),
            pltpu.VMEM((2 * SPAN, FEATURES), f32),
            pltpu.VMEM((FEATURES, 2 * SPAN), bf16),
            pltpu.VMEM((GROUPS, FEATURES, GROUP_ROWS), f32),
            pltpu.SemaphoreType.DMA((2,)),
        ],
        room=28,
    )
    query_shape = (FEATURES, ROWS)
    kept, *sent = kernel_call(
        spread_z_body,
        [((2,) + query_shape, f32)] + [((2,) + query_shape, bf16)] * 3,
        [info],
        [own_query, swap(other_query, "ctx", 1)],
    )
    both, sent = lax.optimization_barrier((both, sent))
    arriving = [swap(block, "ctx", 4 * code) for code, block in zip((1, 2, 3), sent)]
    block_shape = (CHIPS, 2 * FEATURES, ROWS)
    own_weight, other_weight = resident_call(
        weight_body,
        [(block_shape, f32), (block_shape, bf16)],
        [info],
        context + [both],
    )
    own_weight, other_weight, arriving = lax.optimization_barrier(
        (own_weight, other_weight, arriving)
    )
    query_kept, sent = kernel_call(
        spread_y_body,
        [(query_shape, f32), (query_shape, bf16)],
        [info],
        [kept] + arriving,
    )
    weight_blocks = kernel_call(
        add_body,
        [(block_shape, bf16)],
        [],
        [own_weight, swap(other_weight, "ctx", 1)],
    )[0]
    query_rest, weight_blocks, attended_terms = lax.optimization_barrier(
        (swap(sent, "ctx", 2), weight_blocks, attended_terms)
    )
    same_core = [list(range(core, CTX_DEVICES, 2)) for core in range(2)]
    key_grad, value_grad = kernel_call(
        finish_body,
        [((ROWS, FEATURES), f32)] * 2,
        [],
        [exchange(weight_blocks, "ctx", same_core)],
    )

    pair_shape = (2, ROWS, 2 * FEATURES)
    own_terms, *terms = kernel_call(
        close_body,
        [(pair_shape, f32)] + [(pair_shape, bf16)] * 3,
        [info],
        [w_out, w_query, attended_terms, query_kept, query_rest],
        room=60,
    )
    kept, sent = kernel_call(
        fold_body,
        [(pair_shape[1:], f32), (pair_shape[1:], bf16)],
        [],
        [own_terms] + [swap(block, "tp", bits) for bits, block in zip((1, 2, 3), terms)],
    )
    cross_out, latent_grad = kernel_call(
        last_body, [((ROWS, FEATURES), bf16)] * 2, [], [kept, swap(sent, "tp", 4)]
    )
    return (
        cross_out,
        latent_grad,
        key_grad,
        value_grad,
    )


def solution(mesh):
    placed = (
        P("ctx"),
        P(None, "tp"),
        P("ctx", "tp"),
        P(None, "tp"),
        P(None, "tp"),
        P(None, "tp"),
        P("tp", None),
        P("ctx", "tp"),
        P(),
    )
    return jax.shard_map(
        shards,
        mesh=mesh,
        in_specs=placed,
        out_specs=(P("ctx", "tp"), P("ctx", "tp"), P("ctx", "tp"), P("ctx", "tp")),
        check_vma=False,
    )
```

```python
import math

import jax
import jax.numpy as jnp
from jax import lax
from jax.experimental import pallas as pl
from jax.experimental.pallas import tpu as pltpu
from jax.sharding import PartitionSpec as P

HEAD_DIM = 128
CTX_DEVICES = 16
TP_DEVICES = 8
FEATURES = 256
HEADS_HERE = FEATURES // HEAD_DIM
ROWS = 128
LAST_PEER = 6
FIRST_PEERS = (0, 1, 2, 3, 4, 5, 7)
CHIPS = CTX_DEVICES // 2
GROUPS = 4
STORED = 120
FIRST_X, SECOND_X = (1, 3), (3, 1)
KEPT_PEERS = ((0, 3), (0, 1))
SENT_PEERS = ((1, 2), (3, 2))
LEVEL_ROWS = 16
GROUP_ROWS = 4 * ROWS
SPAN = 512

SCORE_SCALE = 1.0 / math.sqrt(HEAD_DIM)
LOG2_SCALE = SCORE_SCALE * math.log2(math.e)
MASKED = -1e30
FLOOR = -1e29

NN = (((1,), (0,)), ((), ()))
NT = (((1,), (1,)), ((), ()))
TN = (((0,), (0,)), ((), ()))

bf16 = jnp.bfloat16
f32 = jnp.float32


def mm(left, right, dims=NN):
    return lax.dot_general(left, right, dims, preferred_element_type=f32)


def swap(value, axis, bits):
    count = CTX_DEVICES if axis == "ctx" else TP_DEVICES
    return lax.ppermute(value, axis, [(i, i ^ bits) for i in range(count)])


def exchange(value, axis, groups=None):
    return lax.all_to_all(value, axis, 0, 0, axis_index_groups=groups, tiled=True)


def whole(shape):
    return pl.BlockSpec(shape, lambda i: (0,) * len(shape), pipeline_mode=pl.Buffered(1))


def kernel_call(body, outs, scalars, arrays, room=16):
    call = pl.pallas_call(
        body,
        grid=(1,),
        out_shape=[jax.ShapeDtypeStruct(shape, kind) for shape, kind in outs],
        in_specs=[pl.BlockSpec(memory_space=pltpu.SMEM)] * len(scalars)
        + [whole(a.shape) for a in arrays],
        out_specs=[whole(shape) for shape, _ in outs],
        compiler_params=pltpu.CompilerParams(vmem_limit_bytes=room * 1024 * 1024),
        cost_estimate=pl.CostEstimate(flops=0, bytes_accessed=0, transcendentals=0),
    )
    return list(call(*scalars, *arrays))


def resident_call(body, outs, scalars, arrays, far_in=(), far_out=(), scratch=(), room=16, flops=0):
    near, far = pl.BlockSpec(memory_space=pltpu.VMEM), pl.BlockSpec(memory_space=pltpu.HBM)
    call = pl.pallas_call(
        body,
        out_shape=[jax.ShapeDtypeStruct(shape, kind) for shape, kind in [*far_out, *outs]],
        in_specs=[pl.BlockSpec(memory_space=pltpu.SMEM)] * len(scalars)
        + [far] * len(far_in)
        + [near] * len(arrays),
        out_specs=[far] * len(far_out) + [near] * len(outs),
        scratch_shapes=list(scratch),
        compiler_params=pltpu.CompilerParams(vmem_limit_bytes=room * 1024 * 1024),
        cost_estimate=pl.CostEstimate(flops=flops, bytes_accessed=0, transcendentals=0),
    )
    return list(call(*scalars, *far_in, *arrays))


def far_blocks(near, back, side):
    return swap(back, "tp", 1), swap(near, "tp", 4), swap(side, "tp", 3)


def both_cores(chips):
    return jnp.concatenate(chips + [swap(pair, "ctx", 1) for pair in chips], axis=0)


def shard_start(tp_index, r):
    return pl.multiple_of((tp_index ^ r) * FEATURES, FEATURES)


def head_of(h):
    return slice(h * HEAD_DIM, (h + 1) * HEAD_DIM)


def rows_body(info, w_query, w_out, *refs):
    blocks, out = refs[:-1], refs[-1]
    query = jnp.zeros((ROWS, FEATURES), f32)
    grads = [jnp.zeros((HEAD_DIM, ROWS), f32) for _ in range(HEADS_HERE)]
    for r in range(TP_DEVICES):
        part = pl.ds(shard_start(info[0], r), FEATURES)
        query += mm(blocks[r][:ROWS, :], w_query[part, :])
        for h in range(HEADS_HERE):
            grads[h] += mm(w_out[head_of(h), part], blocks[r][ROWS:, :], NT)
    out[:ROWS, :] = query.astype(bf16)
    for h in range(HEADS_HERE):
        out[ROWS:, head_of(h)] = grads[h].astype(bf16)


def row_block(rows, ctx_index, block):
    distance = ctx_index ^ block
    return rows.at[(distance & 1) * CHIPS + (distance >> 1)]


def group_query(rows, ctx_index, group, h):
    blocks = [row_block(rows, ctx_index, GROUPS * group + i) for i in range(GROUPS)]
    return jnp.concatenate([block[:ROWS, head_of(h)] for block in blocks], axis=0)


def group_grad(rows, ctx_index, group, h):
    blocks = [row_block(rows, ctx_index, GROUPS * group + i) for i in range(GROUPS)]
    return jnp.concatenate([block[ROWS:, head_of(h)] for block in blocks], axis=1)


def masked(scores, base, offset_row):
    if offset_row is None:
        return scores
    places = base + lax.broadcasted_iota(jnp.int32, (SPAN, GROUP_ROWS), 0)
    return jnp.where(places <= offset_row, scores, MASKED)


def visit(bounds, base, offsets, group, block):
    whole_seen = bounds[1, group] >= base + (SPAN - 1)

    @pl.when(whole_seen)
    def _():
        block(None)

    @pl.when(jnp.logical_and(bounds[0, group] >= base, jnp.logical_not(whole_seen)))
    def _():
        block(offsets[group])


def pieces_of(level):
    pieces = []
    for _ in range(3):
        piece = level.astype(bf16).astype(f32)
        pieces.append(piece)
        level = level - piece
    return pieces


def turned(value):
    return value.astype(f32).T.astype(bf16)


def span_of(i):
    return slice(i * SPAN, (i + 1) * SPAN)


def ordered_rows(weight, tp_index, order):
    return jnp.concatenate(
        [weight[pl.ds(shard_start(tp_index, r), FEATURES), :] for r in order], axis=0
    )


def project_body(info, w_key, w_value, *refs):
    context = jnp.concatenate([ref[...] for ref in refs[:-1]], axis=1)
    out = refs[-1]
    out[:, :FEATURES] = mm(context, ordered_rows(w_key, info[0], FIRST_PEERS))
    out[:, FEATURES:] = mm(context, ordered_rows(w_value, info[0], FIRST_PEERS))


def forward_body(info, limits, *refs):
    offsets, rows, w_key, w_value, begun, last, stored = refs[:7]
    stats, blocks, keys, values, values_t, parts, copied = refs[7:]
    ctx_index = info[1]
    start = shard_start(info[0], LAST_PEER)
    for i, (weight, out) in enumerate(((w_key, keys), (w_value, values))):
        rest = mm(last[...], weight[pl.ds(start, FEATURES), :])
        out[...] = (begun[:, i * FEATURES : (i + 1) * FEATURES] + rest).astype(bf16)
    copies = [
        pltpu.make_async_copy(keys, stored.at[0], copied.at[0]),
        pltpu.make_async_copy(values, stored.at[1], copied.at[1]),
    ]
    for copy in copies:
        copy.start()
    for h in range(HEADS_HERE):
        values_t[head_of(h), :] = turned(values[:, head_of(h)])

    def step(group, carry):
        stats[group, :2, :] = jnp.full((2, GROUP_ROWS), MASKED, f32)
        stats[group, 2:, :] = jnp.zeros((2, GROUP_ROWS), f32)
        parts[...] = jnp.zeros((FEATURES, GROUP_ROWS), f32)
        for i in range(2):
            base = info[2 + i]

            def block(offset_row, i=i, base=base):
                for h in range(HEADS_HERE):
                    query = group_query(rows, ctx_index, group, h)
                    scores = mm(keys[span_of(i), head_of(h)], query, NT) * LOG2_SCALE
                    scores = masked(scores, base, offset_row)
                    old = stats[group, h : h + 1, :]
                    peak = jnp.maximum(jnp.max(scores, axis=0, keepdims=True), FLOOR)
                    peak = jnp.maximum(peak, old)
                    weights = jnp.exp2(scores - peak)
                    keep = jnp.exp2(old - peak)
                    total = keep * stats[group, h + 2 : h + 3, :]
                    total += jnp.sum(weights, axis=0, keepdims=True)
                    part = mm(values_t[head_of(h), span_of(i)], weights.astype(bf16))
                    parts[head_of(h), :] = keep * parts[head_of(h), :] + part
                    stats[group, h : h + 1, :] = peak
                    stats[group, h + 2 : h + 3, :] = total

            visit(limits, base, offsets, group, block)

        levels = []
        for h in range(HEADS_HERE):
            total = stats[group, h + 2 : h + 3, :]
            some = total > 0.0
            safe = jnp.where(some, total, 1.0)
            part = parts[head_of(h), :] * jnp.where(some, 1.0 / safe, 0.0)
            grad_t = group_grad(rows, ctx_index, group, h).astype(f32)
            level = jnp.where(some, stats[group, h : h + 1, :] + jnp.log2(safe), MASKED)
            stats[group, h : h + 1, :] = level
            stats[group, h + 2 : h + 3, :] = jnp.sum(part * grad_t, axis=0, keepdims=True)
            levels += pieces_of(level)
            for i in range(GROUPS):
                place = GROUPS * group + i
                lanes = slice(i * ROWS, (i + 1) * ROWS)
                blocks[place, head_of(h), :] = part[:, lanes].astype(bf16)
        levels.append(jnp.zeros((LEVEL_ROWS - len(levels), GROUP_ROWS), f32))
        levels = jnp.concatenate(levels, axis=0).astype(bf16)
        for i in range(GROUPS):
            place = GROUPS * group + i
            blocks[place, FEATURES:, :] = levels[:, i * ROWS : (i + 1) * ROWS]
        return carry

    lax.fori_loop(0, GROUPS, step, 0)
    for copy in copies:
        copy.wait()


def joined(refs, group):
    pieces = [ref[group] for ref in refs]
    top = pieces[0][:2]
    for piece in pieces[1:]:
        top = jnp.maximum(top, piece[:2])
    total = jnp.zeros((2, GROUP_ROWS), f32)
    delta = jnp.zeros((2, GROUP_ROWS), f32)
    for piece in pieces:
        weight = jnp.exp2(piece[:2] - top)
        total += weight
        delta += weight * piece[2:]
    return top + jnp.log2(total), delta / total


def join_body(own, one, two, three, stats):
    for group in range(GROUPS):
        level, delta = joined((own, one, two, three), group)
        stats[group, :2, :] = level
        stats[group, 2:, :] = delta


def split_parity(core, group, value, mine, other):
    for i in range(GROUPS // 2):
        low = value[:, 2 * i * ROWS : (2 * i + 1) * ROWS]
        high = value[:, (2 * i + 1) * ROWS : (2 * i + 2) * ROWS]
        chip = group * (GROUPS // 2) + i
        mine[chip] = jnp.where(core == 1, high, low)
        other[chip] = jnp.where(core == 1, low, high).astype(bf16)


def backward_body(info, limits, *refs):
    stored, offsets, rows, own, one, two, three, both, mine, other = refs[:10]
    keys, values, stats, key_acc, value_acc, keys_t, query_acc, copied = refs[10:]
    copies = [
        pltpu.make_async_copy(stored.at[0], keys, copied.at[0]),
        pltpu.make_async_copy(stored.at[1], values, copied.at[1]),
    ]
    for copy in copies:
        copy.start()
    for group in range(GROUPS):
        level, delta = joined((own, one, two, three), group)
        stats[group, :2, :] = level
        stats[group, 2:, :] = delta
    ctx_index = info[1]
    query_acc[...] = jnp.zeros(query_acc.shape, f32)
    key_acc[...] = jnp.zeros(key_acc.shape, f32)
    value_acc[...] = jnp.zeros(value_acc.shape, f32)
    for copy in copies:
        copy.wait()
    for h in range(HEADS_HERE):
        keys_t[head_of(h), :] = turned(keys[:, head_of(h)])

    def step(group, carry):
        for i in range(2):
            base = info[2 + i]
            span = span_of(i)

            def block(offset_row, span=span, base=base):
                for h in range(HEADS_HERE):
                    query = group_query(rows, ctx_index, group, h)
                    grad_t = group_grad(rows, ctx_index, group, h)
                    scores = mm(keys[span, head_of(h)], query, NT) * LOG2_SCALE
                    scores = masked(scores - stats[group, h : h + 1, :], base, offset_row)
                    probs = jnp.exp2(scores)
                    prob_grad = mm(values[span, head_of(h)], grad_t)
                    delta = stats[group, h + 2 : h + 3, :]
                    score_grad = (probs * (prob_grad - delta) * SCORE_SCALE).astype(bf16)
                    value_acc[span, head_of(h)] += mm(probs.astype(bf16), grad_t, NT)
                    key_acc[span, head_of(h)] += mm(score_grad, query)
                    query_acc[group, head_of(h), :] += mm(keys_t[head_of(h), span], score_grad)

            visit(limits, base, offsets, group, block)

        return carry

    lax.fori_loop(0, GROUPS, step, 0)
    both[:FEATURES, :] = turned(key_acc[...])
    both[FEATURES:, :] = turned(value_acc[...])
    for group in range(GROUPS):
        split_parity(ctx_index & 1, group, query_acc[group], mine, other)


def weight_body(info, *refs):
    both, mine, other = refs[TP_DEVICES:]
    flipped = (info[1] & 1) == 1
    for r in range(TP_DEVICES):
        terms = mm(both[...], refs[r][...])
        place = info[0] ^ r
        low, high = terms[:, :ROWS], terms[:, ROWS:]
        mine[place] = jnp.where(flipped, high, low)
        other[place] = jnp.where(flipped, low, high).astype(bf16)


def add_body(own, received, out):
    out[...] = (own[...] + received[...].astype(f32)).astype(bf16)


def spread_z_body(info, own, received, kept, one, two, three):
    z = info[1] >> 2
    for y in range(2):
        place = 2 * z + y
        kept[y] = own[place] + received[place].astype(f32)
        for code, out in ((1, one), (2, two), (3, three)):
            place = 2 * (z ^ code) + y
            out[y] = (own[place] + received[place].astype(f32)).astype(bf16)


def spread_y_body(info, own, one, two, three, kept, sent):
    y = (info[1] >> 1) & 1
    for place, out in ((y, kept), (1 - y, sent)):
        total = own[place]
        for term in (one, two, three):
            total += term[place].astype(f32)
        out[...] = total.astype(out.dtype)


def finish_body(terms, key_grad, value_grad):
    total = total_of(terms).T
    key_grad[...] = total[:, :FEATURES]
    value_grad[...] = total[:, FEATURES:]


def weighted_sum(blocks):
    heads = []
    for h in range(HEADS_HERE):
        levels = []
        for i in range(CTX_DEVICES):
            pieces = blocks[i, FEATURES:, :].astype(f32)[3 * h : 3 * h + 3]
            levels.append(pieces[0:1] + pieces[1:2] + pieces[2:3])
        top = levels[0]
        for level in levels[1:]:
            top = jnp.maximum(top, level)
        weights = [jnp.exp2(level - top) for level in levels]
        scale = 1.0 / sum(weights)
        total = jnp.zeros((HEAD_DIM, ROWS), f32)
        for i in range(CTX_DEVICES):
            total += weights[i] * blocks[i, head_of(h), :].astype(f32)
        heads.append(total * scale)
    return jnp.concatenate(heads, axis=0)


def total_of(terms):
    total = terms[0].astype(f32)
    for i in range(1, terms.shape[0]):
        total = total + terms[i].astype(f32)
    return total


def close_body(info, w_out, w_query, attended_terms, query_kept, query_rest, *outs):
    attended = weighted_sum(attended_terms).T.astype(bf16)
    query_grad = (query_kept[...] + query_rest[...].astype(f32)).T.astype(bf16)
    for y in range(2):
        for x in range(4):
            part = pl.ds(shard_start(info[0], 4 * y + x), FEATURES)
            cross = mm(attended, w_out[:, part])
            latent = mm(query_grad, w_query[part, :], NT)
            for half, terms in ((0, cross), (1, latent)):
                stays = KEPT_PEERS[half]
                out = outs[2 * half + (x not in stays)]
                place = (stays if x in stays else SENT_PEERS[half]).index(x)
                out[place, y] = terms.astype(out.dtype)


def fold_body(*refs):
    for half in range(2):
        stays, came = refs[2 * half : 2 * half + 2]
        kept, sent = refs[4 + 2 * half : 6 + 2 * half]
        kept[...] = stays[0] + came[0].astype(f32)
        sent[...] = (stays[1] + came[1].astype(f32)).astype(bf16)


def fold_last_body(cross, cross_came, latent, latent_came, kept, sent):
    for half, (own, came) in enumerate(((cross, cross_came), (latent, latent_came))):
        columns = slice(half * FEATURES, (half + 1) * FEATURES)
        kept[:, columns] = own[0] + came[0].astype(f32)
        sent[:, columns] = (own[1] + came[1].astype(f32)).astype(bf16)


def last_body(kept, rest, cross_out, latent_grad):
    total = (kept[...] + rest[...].astype(f32)).astype(bf16)
    cross_out[...] = total[:, :FEATURES]
    latent_grad[...] = total[:, FEATURES:]


def shards(token_ids, embed_table, latents, w_query, w_key, w_value, w_out, out_grad, offsets):
    ctx_index = lax.axis_index("ctx").astype(jnp.int32)
    tp_index = lax.axis_index("tp").astype(jnp.int32)
    key_count = token_ids.shape[0]

    mirror_ids = swap(token_ids[SPAN:], "ctx", CTX_DEVICES - 1)
    info = jnp.stack(
        [
            tp_index,
            ctx_index,
            ctx_index * key_count,
            (CTX_DEVICES - 1 - ctx_index) * key_count + SPAN,
        ]
    )
    grouped = offsets.reshape(GROUPS, GROUP_ROWS)
    limits = jnp.stack([jnp.max(grouped, axis=1), jnp.min(grouped, axis=1)])
    offset_rows = offsets.reshape(GROUPS, 1, GROUP_ROWS)

    row_part = jnp.concatenate([latents, out_grad], axis=0)
    row_part, mirror_ids, info, limits, offset_rows = lax.optimization_barrier(
        (row_part, mirror_ids, info, limits, offset_rows)
    )
    near, back, side = (swap(row_part, "tp", bits) for bits in (1, 3, 4))
    far, side_near, side_back = far_blocks(near, back, side)
    ids = jnp.concatenate([token_ids[:SPAN], mirror_ids])
    context_part = embed_table.at[ids].get(mode="promise_in_bounds")
    far, side_near, side_back, context_part = lax.optimization_barrier(
        (far, side_near, side_back, context_part)
    )
    side_far = swap(side_back, "tp", 1)
    context_back, context_side = swap(context_part, "tp", 3), swap(context_part, "tp", 4)
    side_far, context_late = lax.optimization_barrier((side_far, context_part))
    context_first = (swap(context_late, "tp", 1), context_back, context_side)
    row_blocks = [row_part, near, far, back, side, side_near, side_far, side_back]

    own = kernel_call(
        rows_body,
        [((2 * ROWS, FEATURES), bf16)],
        [info],
        [w_query, w_out] + row_blocks,
        room=60,
    )[0]
    beside, context_first = lax.optimization_barrier((swap(own, "ctx", 2), context_first))
    near, back, side = context_first
    far, side_near, side_back = lax.optimization_barrier(far_blocks(near, back, side))
    side_far = swap(side_back, "tp", 1)
    chips = [jnp.stack([own, beside])]
    chips += [swap(chips[0], "ctx", code) for code in (4, 8, 12)]
    context = [context_part, near, far, back, side, side_near, side_far, side_back]
    begun = resident_call(
        project_body,
        [((2 * SPAN, 2 * FEATURES), f32)],
        [info],
        [w_key, w_value] + [context[r] for r in FIRST_PEERS],
    )[0]
    chips, begun = lax.optimization_barrier((chips, begun))
    rows = both_cores(chips)

    part_shape = (CHIPS, FEATURES, ROWS)
    stats_shape = (GROUPS, 4, GROUP_ROWS)
    span_kind = ((2 * SPAN, FEATURES), bf16)
    stored, local, out_blocks = resident_call(
        forward_body,
        [
            (stats_shape, f32),
            ((CTX_DEVICES, FEATURES + LEVEL_ROWS, ROWS), bf16),
        ],
        [info, limits],
        [offset_rows, rows, w_key, w_value, begun, context[LAST_PEER]],
        far_out=[((STORED,) + span_kind[0], bf16)],
        scratch=[
            pltpu.VMEM(*span_kind),
            pltpu.VMEM(*span_kind),
            pltpu.VMEM((FEATURES, 2 * SPAN), bf16),
            pltpu.VMEM((FEATURES, GROUP_ROWS), f32),
            pltpu.SemaphoreType.DMA((2,)),
        ],
        room=24,
    )

    chip = kernel_call(
        join_body,
        [(stats_shape, f32)],
        [],
        [local] + [swap(local, "ctx", code) for code in (1, 2, 3)],
    )[0]
    chips = [chip] + [swap(chip, "ctx", code) for code in (4, 8, 12)]
    out_blocks, chips = lax.optimization_barrier((out_blocks, chips))
    attended_terms = exchange(out_blocks, "ctx")

    both, own_query, other_query = resident_call(
        backward_body,
        [((2 * FEATURES, 2 * SPAN), bf16), (part_shape, f32), (part_shape, bf16)],
        [info, limits],
        [offset_rows, rows] + chips,
        far_in=[stored],
        scratch=[
            pltpu.VMEM(*span_kind),
            pltpu.VMEM(*span_kind),
            pltpu.VMEM(stats_shape, f32),
            pltpu.VMEM((2 * SPAN, FEATURES), f32),
            pltpu.VMEM((2 * SPAN, FEATURES), f32),
            pltpu.VMEM((FEATURES, 2 * SPAN), bf16),
            pltpu.VMEM((GROUPS, FEATURES, GROUP_ROWS), f32),
            pltpu.SemaphoreType.DMA((2,)),
        ],
        room=28,
    )
    query_shape = (FEATURES, ROWS)
    kept, *sent = kernel_call(
        spread_z_body,
        [((2,) + query_shape, f32)] + [((2,) + query_shape, bf16)] * 3,
        [info],
        [own_query, swap(other_query, "ctx", 1)],
    )
    both, sent = lax.optimization_barrier((both, sent))
    arriving = [swap(block, "ctx", 4 * code) for code, block in zip((1, 2, 3), sent)]
    block_shape = (CHIPS, 2 * FEATURES, ROWS)
    own_weight, other_weight = resident_call(
        weight_body,
        [(block_shape, f32), (block_shape, bf16)],
        [info],
        context + [both],
    )
    own_weight, other_weight, attended_terms, arriving = lax.optimization_barrier(
        (own_weight, other_weight, attended_terms, arriving)
    )
    query_kept, sent = kernel_call(
        spread_y_body,
        [(query_shape, f32), (query_shape, bf16)],
        [info],
        [kept] + arriving,
        room=60,
    )
    weight_blocks = kernel_call(
        add_body,
        [(block_shape, bf16)],
        [],
        [own_weight, swap(other_weight, "ctx", 1)],
    )[0]
    query_rest, weight_blocks = lax.optimization_barrier((swap(sent, "ctx", 2), weight_blocks))
    same_core = [list(range(core, CTX_DEVICES, 2)) for core in range(2)]
    key_grad, value_grad = kernel_call(
        finish_body,
        [((ROWS, FEATURES), f32)] * 2,
        [],
        [exchange(weight_blocks, "ctx", same_core)],
    )

    pair_shape = (2, ROWS, FEATURES)
    four_shape = (2,) + pair_shape
    terms = kernel_call(
        close_body,
        [(four_shape, f32), (four_shape, bf16)] * 2,
        [info],
        [w_out, w_query, attended_terms, query_kept, query_rest],
        room=60,
    )
    came = [swap(terms[1], "tp", FIRST_X[0]), swap(terms[3], "tp", FIRST_X[1])]
    cross, cross_sent, latent, latent_sent = kernel_call(
        fold_body,
        [(pair_shape, f32), (pair_shape, bf16)] * 2,
        [],
        [terms[0], came[0], terms[2], came[1]],
    )
    came = [swap(cross_sent, "tp", SECOND_X[0]), swap(latent_sent, "tp", SECOND_X[1])]
    sum_shape = (ROWS, 2 * FEATURES)
    kept, sent = kernel_call(
        fold_last_body,
        [(sum_shape, f32), (sum_shape, bf16)],
        [],
        [cross, came[0], latent, came[1]],
    )
    cross_out, latent_grad = kernel_call(
        last_body, [((ROWS, FEATURES), bf16)] * 2, [], [kept, swap(sent, "tp", 4)]
    )
    return (
        cross_out,
        latent_grad,
        key_grad,
        value_grad,
    )


def solution(mesh):
    placed = (
        P("ctx"),
        P(None, "tp"),
        P("ctx", "tp"),
        P(None, "tp"),
        P(None, "tp"),
        P(None, "tp"),
        P("tp", None),
        P("ctx", "tp"),
        P(),
    )
    return jax.shard_map(
        shards,
        mesh=mesh,
        in_specs=placed,
        out_specs=(P("ctx", "tp"), P("ctx", "tp"), P("ctx", "tp"), P("ctx", "tp")),
        check_vma=False,
    )
```

```python
import math

import jax
import jax.numpy as jnp
from jax import lax
from jax.experimental import pallas as pl
from jax.experimental.pallas import tpu as pltpu
from jax.sharding import PartitionSpec as P

HEAD_DIM = 128
CTX_DEVICES = 16
TP_DEVICES = 8
FEATURES = 256
HEADS_HERE = FEATURES // HEAD_DIM
ROWS = 128
LAST_PEER = 6
FIRST_PEERS = (0, 1, 2, 3, 4, 5, 7)
CHIPS = CTX_DEVICES // 2
GROUPS = 4
STORED = 120
FIRST_X, SECOND_X = (1, 3), (3, 1)
KEPT_PEERS = ((0, 3), (0, 1))
SENT_PEERS = ((1, 2), (3, 2))
MIRROR = 12
LEVEL_ROWS = 16
GROUP_ROWS = 4 * ROWS
SPAN = 512

SCORE_SCALE = 1.0 / math.sqrt(HEAD_DIM)
LOG2_SCALE = SCORE_SCALE * math.log2(math.e)
MASKED = -1e30
FLOOR = -1e29

NN = (((1,), (0,)), ((), ()))
NT = (((1,), (1,)), ((), ()))
TN = (((0,), (0,)), ((), ()))

bf16 = jnp.bfloat16
f32 = jnp.float32


def mm(left, right, dims=NN):
    return lax.dot_general(left, right, dims, preferred_element_type=f32)


def swap(value, axis, bits):
    count = CTX_DEVICES if axis == "ctx" else TP_DEVICES
    return lax.ppermute(value, axis, [(i, i ^ bits) for i in range(count)])


def exchange(value, axis, groups=None):
    return lax.all_to_all(value, axis, 0, 0, axis_index_groups=groups, tiled=True)


def whole(shape):
    return pl.BlockSpec(shape, lambda i: (0,) * len(shape), pipeline_mode=pl.Buffered(1))


def kernel_call(body, outs, scalars, arrays, room=16):
    call = pl.pallas_call(
        body,
        grid=(1,),
        out_shape=[jax.ShapeDtypeStruct(shape, kind) for shape, kind in outs],
        in_specs=[pl.BlockSpec(memory_space=pltpu.SMEM)] * len(scalars)
        + [whole(a.shape) for a in arrays],
        out_specs=[whole(shape) for shape, _ in outs],
        compiler_params=pltpu.CompilerParams(vmem_limit_bytes=room * 1024 * 1024),
        cost_estimate=pl.CostEstimate(flops=0, bytes_accessed=0, transcendentals=0),
    )
    return list(call(*scalars, *arrays))


def resident_call(body, outs, scalars, arrays, far_in=(), far_out=(), scratch=(), room=16, flops=0):
    near, far = pl.BlockSpec(memory_space=pltpu.VMEM), pl.BlockSpec(memory_space=pltpu.HBM)
    call = pl.pallas_call(
        body,
        out_shape=[jax.ShapeDtypeStruct(shape, kind) for shape, kind in [*far_out, *outs]],
        in_specs=[pl.BlockSpec(memory_space=pltpu.SMEM)] * len(scalars)
        + [far] * len(far_in)
        + [near] * len(arrays),
        out_specs=[far] * len(far_out) + [near] * len(outs),
        scratch_shapes=list(scratch),
        compiler_params=pltpu.CompilerParams(vmem_limit_bytes=room * 1024 * 1024),
        cost_estimate=pl.CostEstimate(flops=flops, bytes_accessed=0, transcendentals=0),
    )
    return list(call(*scalars, *far_in, *arrays))


def far_blocks(near, back, side):
    return swap(back, "tp", 1), swap(near, "tp", 4), swap(side, "tp", 3)


def both_cores(chips):
    return jnp.concatenate(chips + [swap(pair, "ctx", 1) for pair in chips], axis=0)


def shard_start(tp_index, r):
    return pl.multiple_of((tp_index ^ r) * FEATURES, FEATURES)


def head_of(h):
    return slice(h * HEAD_DIM, (h + 1) * HEAD_DIM)


def rows_body(info, w_query, w_out, *refs):
    blocks, out = refs[:-1], refs[-1]
    query = jnp.zeros((ROWS, FEATURES), f32)
    grads = [jnp.zeros((HEAD_DIM, ROWS), f32) for _ in range(HEADS_HERE)]
    for r in range(TP_DEVICES):
        part = pl.ds(shard_start(info[0], r), FEATURES)
        query += mm(blocks[r][:ROWS, :], w_query[part, :])
        for h in range(HEADS_HERE):
            grads[h] += mm(w_out[head_of(h), part], blocks[r][ROWS:, :], NT)
    out[:ROWS, :] = query.astype(bf16)
    for h in range(HEADS_HERE):
        out[ROWS:, head_of(h)] = grads[h].astype(bf16)


def row_block(rows, ctx_index, block):
    distance = ctx_index ^ block
    return rows.at[(distance & 1) * CHIPS + (distance >> 1)]


def group_query(rows, ctx_index, group, h):
    blocks = [row_block(rows, ctx_index, GROUPS * group + i) for i in range(GROUPS)]
    return jnp.concatenate([block[:ROWS, head_of(h)] for block in blocks], axis=0)


def group_grad(rows, ctx_index, group, h):
    blocks = [row_block(rows, ctx_index, GROUPS * group + i) for i in range(GROUPS)]
    return jnp.concatenate([block[ROWS:, head_of(h)] for block in blocks], axis=1)


def masked(scores, base, offset_row):
    if offset_row is None:
        return scores
    places = base + lax.broadcasted_iota(jnp.int32, (SPAN, GROUP_ROWS), 0)
    return jnp.where(places <= offset_row, scores, MASKED)


def visit(bounds, base, offsets, group, block):
    whole_seen = bounds[1, group] >= base + (SPAN - 1)

    @pl.when(whole_seen)
    def _():
        block(None)

    @pl.when(jnp.logical_and(bounds[0, group] >= base, jnp.logical_not(whole_seen)))
    def _():
        block(offsets[group])


def pieces_of(level):
    pieces = []
    for _ in range(3):
        piece = level.astype(bf16).astype(f32)
        pieces.append(piece)
        level = level - piece
    return pieces


def turned(value):
    return value.astype(f32).T.astype(bf16)


def span_of(i):
    return slice(i * SPAN, (i + 1) * SPAN)


def ordered_rows(weight, tp_index, order):
    return jnp.concatenate(
        [weight[pl.ds(shard_start(tp_index, r), FEATURES), :] for r in order], axis=0
    )


def project_body(info, w_key, w_value, *refs):
    context = jnp.concatenate([ref[...] for ref in refs[:-1]], axis=1)
    out = refs[-1]
    out[:, :FEATURES] = mm(context, ordered_rows(w_key, info[0], FIRST_PEERS))
    out[:, FEATURES:] = mm(context, ordered_rows(w_value, info[0], FIRST_PEERS))


def forward_body(info, limits, *refs):
    offsets, rows, w_key, w_value, begun, last, stored = refs[:7]
    stats, blocks, keys, values, values_t, parts, copied = refs[7:]
    ctx_index = info[1]
    start = shard_start(info[0], LAST_PEER)
    for i, (weight, out) in enumerate(((w_key, keys), (w_value, values))):
        rest = mm(last[...], weight[pl.ds(start, FEATURES), :])
        out[...] = (begun[:, i * FEATURES : (i + 1) * FEATURES] + rest).astype(bf16)
    copies = [
        pltpu.make_async_copy(keys, stored.at[0], copied.at[0]),
        pltpu.make_async_copy(values, stored.at[1], copied.at[1]),
    ]
    for copy in copies:
        copy.start()
    for h in range(HEADS_HERE):
        values_t[head_of(h), :] = turned(values[:, head_of(h)])

    def step(group, carry):
        stats[group, :2, :] = jnp.full((2, GROUP_ROWS), MASKED, f32)
        stats[group, 2:, :] = jnp.zeros((2, GROUP_ROWS), f32)
        parts[...] = jnp.zeros((FEATURES, GROUP_ROWS), f32)
        for i in range(2):
            base = info[2 + i]

            def block(offset_row, i=i, base=base):
                for h in range(HEADS_HERE):
                    query = group_query(rows, ctx_index, group, h)
                    scores = mm(keys[span_of(i), head_of(h)], query, NT) * LOG2_SCALE
                    scores = masked(scores, base, offset_row)
                    old = stats[group, h : h + 1, :]
                    peak = jnp.maximum(jnp.max(scores, axis=0, keepdims=True), FLOOR)
                    peak = jnp.maximum(peak, old)
                    weights = jnp.exp2(scores - peak)
                    keep = jnp.exp2(old - peak)
                    total = keep * stats[group, h + 2 : h + 3, :]
                    total += jnp.sum(weights, axis=0, keepdims=True)
                    part = mm(values_t[head_of(h), span_of(i)], weights.astype(bf16))
                    parts[head_of(h), :] = keep * parts[head_of(h), :] + part
                    stats[group, h : h + 1, :] = peak
                    stats[group, h + 2 : h + 3, :] = total

            visit(limits, base, offsets, group, block)

        levels = []
        for h in range(HEADS_HERE):
            total = stats[group, h + 2 : h + 3, :]
            some = total > 0.0
            safe = jnp.where(some, total, 1.0)
            part = parts[head_of(h), :] * jnp.where(some, 1.0 / safe, 0.0)
            grad_t = group_grad(rows, ctx_index, group, h).astype(f32)
            level = jnp.where(some, stats[group, h : h + 1, :] + jnp.log2(safe), MASKED)
            stats[group, h : h + 1, :] = level
            stats[group, h + 2 : h + 3, :] = jnp.sum(part * grad_t, axis=0, keepdims=True)
            levels += pieces_of(level)
            for i in range(GROUPS):
                place = GROUPS * group + i
                lanes = slice(i * ROWS, (i + 1) * ROWS)
                blocks[place, head_of(h), :] = part[:, lanes].astype(bf16)
        levels.append(jnp.zeros((LEVEL_ROWS - len(levels), GROUP_ROWS), f32))
        levels = jnp.concatenate(levels, axis=0).astype(bf16)
        for i in range(GROUPS):
            place = GROUPS * group + i
            blocks[place, FEATURES:, :] = levels[:, i * ROWS : (i + 1) * ROWS]
        return carry

    lax.fori_loop(0, GROUPS, step, 0)
    for copy in copies:
        copy.wait()


def joined(refs, group):
    pieces = [ref[group] for ref in refs]
    top = pieces[0][:2]
    for piece in pieces[1:]:
        top = jnp.maximum(top, piece[:2])
    total = jnp.zeros((2, GROUP_ROWS), f32)
    delta = jnp.zeros((2, GROUP_ROWS), f32)
    for piece in pieces:
        weight = jnp.exp2(piece[:2] - top)
        total += weight
        delta += weight * piece[2:]
    return top + jnp.log2(total), delta / total


def join_body(own, one, two, three, stats):
    for group in range(GROUPS):
        level, delta = joined((own, one, two, three), group)
        stats[group, :2, :] = level
        stats[group, 2:, :] = delta


def split_parity(core, group, value, mine, other):
    for i in range(GROUPS // 2):
        low = value[:, 2 * i * ROWS : (2 * i + 1) * ROWS]
        high = value[:, (2 * i + 1) * ROWS : (2 * i + 2) * ROWS]
        chip = group * (GROUPS // 2) + i
        mine[chip] = jnp.where(core == 1, high, low)
        other[chip] = jnp.where(core == 1, low, high).astype(bf16)


def backward_body(info, limits, *refs):
    stored, offsets, rows, own, one, two, three, both, mine, other = refs[:10]
    keys, values, stats, key_acc, value_acc, keys_t, query_acc, copied = refs[10:]
    copies = [
        pltpu.make_async_copy(stored.at[0], keys, copied.at[0]),
        pltpu.make_async_copy(stored.at[1], values, copied.at[1]),
    ]
    for copy in copies:
        copy.start()
    for group in range(GROUPS):
        level, delta = joined((own, one, two, three), group)
        stats[group, :2, :] = level
        stats[group, 2:, :] = delta
    ctx_index = info[1]
    query_acc[...] = jnp.zeros(query_acc.shape, f32)
    key_acc[...] = jnp.zeros(key_acc.shape, f32)
    value_acc[...] = jnp.zeros(value_acc.shape, f32)
    for copy in copies:
        copy.wait()
    for h in range(HEADS_HERE):
        keys_t[head_of(h), :] = turned(keys[:, head_of(h)])

    def step(group, carry):
        for i in range(2):
            base = info[2 + i]
            span = span_of(i)

            def block(offset_row, span=span, base=base):
                for h in range(HEADS_HERE):
                    query = group_query(rows, ctx_index, group, h)
                    grad_t = group_grad(rows, ctx_index, group, h)
                    scores = mm(keys[span, head_of(h)], query, NT) * LOG2_SCALE
                    scores = masked(scores - stats[group, h : h + 1, :], base, offset_row)
                    probs = jnp.exp2(scores)
                    prob_grad = mm(values[span, head_of(h)], grad_t)
                    delta = stats[group, h + 2 : h + 3, :]
                    score_grad = (probs * (prob_grad - delta) * SCORE_SCALE).astype(bf16)
                    value_acc[span, head_of(h)] += mm(probs.astype(bf16), grad_t, NT)
                    key_acc[span, head_of(h)] += mm(score_grad, query)
                    query_acc[group, head_of(h), :] += mm(keys_t[head_of(h), span], score_grad)

            visit(limits, base, offsets, group, block)

        return carry

    lax.fori_loop(0, GROUPS, step, 0)
    both[:FEATURES, :] = turned(key_acc[...])
    both[FEATURES:, :] = turned(value_acc[...])
    for group in range(GROUPS):
        split_parity(ctx_index & 1, group, query_acc[group], mine, other)


def weight_body(info, *refs):
    both, mine, other = refs[TP_DEVICES:]
    flipped = (info[1] & 1) == 1
    for r in range(TP_DEVICES):
        terms = mm(both[...], refs[r][...])
        place = info[0] ^ r
        low, high = terms[:, :ROWS], terms[:, ROWS:]
        mine[place] = jnp.where(flipped, high, low)
        other[place] = jnp.where(flipped, low, high).astype(bf16)


def add_body(own, received, out):
    out[...] = (own[...] + received[...].astype(f32)).astype(bf16)


def spread_z_body(info, own, received, kept, one, two, three):
    z = info[1] >> 2
    for y in range(2):
        place = 2 * z + y
        kept[y] = own[place] + received[place].astype(f32)
        for code, out in ((1, one), (2, two), (3, three)):
            place = 2 * (z ^ code) + y
            out[y] = (own[place] + received[place].astype(f32)).astype(bf16)


def spread_y_body(info, own, one, two, three, kept, sent):
    y = (info[1] >> 1) & 1
    for place, out in ((y, kept), (1 - y, sent)):
        total = own[place]
        for term in (one, two, three):
            total += term[place].astype(f32)
        out[...] = total.astype(out.dtype)


def weighted_sum(blocks):
    heads = []
    for h in range(HEADS_HERE):
        levels = []
        for i in range(CTX_DEVICES):
            pieces = blocks[i, FEATURES:, :].astype(f32)[3 * h : 3 * h + 3]
            levels.append(pieces[0:1] + pieces[1:2] + pieces[2:3])
        top = levels[0]
        for level in levels[1:]:
            top = jnp.maximum(top, level)
        weights = [jnp.exp2(level - top) for level in levels]
        scale = 1.0 / sum(weights)
        total = jnp.zeros((HEAD_DIM, ROWS), f32)
        for i in range(CTX_DEVICES):
            total += weights[i] * blocks[i, head_of(h), :].astype(f32)
        heads.append(total * scale)
    return jnp.concatenate(heads, axis=0)


def total_of(terms):
    total = terms[0].astype(f32)
    for i in range(1, terms.shape[0]):
        total = total + terms[i].astype(f32)
    return total


def close_body(info, w_out, w_query, attended_terms, query_kept, query_rest, *outs):
    attended = weighted_sum(attended_terms).T.astype(bf16)
    query_grad = (query_kept[...] + query_rest[...].astype(f32)).T.astype(bf16)
    for y in range(2):
        for x in range(4):
            part = pl.ds(shard_start(info[0], 4 * y + x), FEATURES)
            cross = mm(attended, w_out[:, part])
            latent = mm(query_grad, w_query[part, :], NT)
            for half, terms in ((0, cross), (1, latent)):
                stays = KEPT_PEERS[half]
                out = outs[2 * half + (x not in stays)]
                place = (stays if x in stays else SENT_PEERS[half]).index(x)
                out[place, y] = terms.astype(out.dtype)


def fold_body(*refs):
    for half in range(2):
        stays, came = refs[2 * half : 2 * half + 2]
        kept, sent = refs[4 + 2 * half : 6 + 2 * half]
        kept[...] = stays[0] + came[0].astype(f32)
        sent[...] = (stays[1] + came[1].astype(f32)).astype(bf16)


def fold_last_body(cross, cross_came, latent, latent_came, kept, sent):
    for half, (own, came) in enumerate(((cross, cross_came), (latent, latent_came))):
        columns = slice(half * FEATURES, (half + 1) * FEATURES)
        kept[:, columns] = own[0] + came[0].astype(f32)
        sent[:, columns] = (own[1] + came[1].astype(f32)).astype(bf16)


def last_body(kept, rest, terms, cross_out, latent_grad, key_grad, value_grad):
    total = (kept[...] + rest[...].astype(f32)).astype(bf16)
    cross_out[...] = total[:, :FEATURES]
    latent_grad[...] = total[:, FEATURES:]
    total = total_of(terms).T
    key_grad[...] = total[:, :FEATURES]
    value_grad[...] = total[:, FEATURES:]


def shards(token_ids, embed_table, latents, w_query, w_key, w_value, w_out, out_grad, offsets):
    ctx_index = lax.axis_index("ctx").astype(jnp.int32)
    tp_index = lax.axis_index("tp").astype(jnp.int32)
    key_count = token_ids.shape[0]

    mirror_ids = swap(token_ids[SPAN:], "ctx", MIRROR)
    info = jnp.stack(
        [
            tp_index,
            ctx_index,
            ctx_index * key_count,
            (ctx_index ^ MIRROR) * key_count + SPAN,
        ]
    )
    grouped = offsets.reshape(GROUPS, GROUP_ROWS)
    limits = jnp.stack([jnp.max(grouped, axis=1), jnp.min(grouped, axis=1)])
    offset_rows = offsets.reshape(GROUPS, 1, GROUP_ROWS)

    row_part = jnp.concatenate([latents, out_grad], axis=0)
    row_part, mirror_ids = lax.optimization_barrier((row_part, mirror_ids))
    near, back, side = (swap(row_part, "tp", bits) for bits in (1, 3, 4))
    near, back, side, info, limits, offset_rows = lax.optimization_barrier(
        (near, back, side, info, limits, offset_rows)
    )
    far, side_near, side_back = far_blocks(near, back, side)
    ids = jnp.concatenate([token_ids[:SPAN], mirror_ids])
    context_part = embed_table.at[ids].get(mode="promise_in_bounds")
    far, side_near, side_back, context_part = lax.optimization_barrier(
        (far, side_near, side_back, context_part)
    )
    side_far = swap(side_back, "tp", 1)
    context_back, context_side = swap(context_part, "tp", 3), swap(context_part, "tp", 4)
    side_far, context_late = lax.optimization_barrier((side_far, context_part))
    context_first = (swap(context_late, "tp", 1), context_back, context_side)
    row_blocks = [row_part, near, far, back, side, side_near, side_far, side_back]

    own = kernel_call(
        rows_body,
        [((2 * ROWS, FEATURES), bf16)],
        [info],
        [w_query, w_out] + row_blocks,
        room=60,
    )[0]
    beside, context_first = lax.optimization_barrier((swap(own, "ctx", 2), context_first))
    near, back, side = context_first
    far, side_near, side_back = lax.optimization_barrier(far_blocks(near, back, side))
    side_far = swap(side_back, "tp", 1)
    chips = [jnp.stack([own, beside])]
    chips += [swap(chips[0], "ctx", code) for code in (4, 8, 12)]
    context = [context_part, near, far, back, side, side_near, side_far, side_back]
    begun = resident_call(
        project_body,
        [((2 * SPAN, 2 * FEATURES), f32)],
        [info],
        [w_key, w_value] + [context[r] for r in FIRST_PEERS],
    )[0]
    chips, begun = lax.optimization_barrier((chips, begun))
    rows = both_cores(chips)

    part_shape = (CHIPS, FEATURES, ROWS)
    stats_shape = (GROUPS, 4, GROUP_ROWS)
    span_kind = ((2 * SPAN, FEATURES), bf16)
    stored, local, out_blocks = resident_call(
        forward_body,
        [
            (stats_shape, f32),
            ((CTX_DEVICES, FEATURES + LEVEL_ROWS, ROWS), bf16),
        ],
        [info, limits],
        [offset_rows, rows, w_key, w_value, begun, context[LAST_PEER]],
        far_out=[((STORED,) + span_kind[0], bf16)],
        scratch=[
            pltpu.VMEM(*span_kind),
            pltpu.VMEM(*span_kind),
            pltpu.VMEM((FEATURES, 2 * SPAN), bf16),
            pltpu.VMEM((FEATURES, GROUP_ROWS), f32),
            pltpu.SemaphoreType.DMA((2,)),
        ],
        room=24,
    )

    chip = kernel_call(
        join_body,
        [(stats_shape, f32)],
        [],
        [local] + [swap(local, "ctx", code) for code in (1, 2, 3)],
    )[0]
    chips = [chip] + [swap(chip, "ctx", code) for code in (4, 8, 12)]
    out_blocks, chips = lax.optimization_barrier((out_blocks, chips))
    attended_terms = exchange(out_blocks, "ctx")

    both, own_query, other_query = resident_call(
        backward_body,
        [((2 * FEATURES, 2 * SPAN), bf16), (part_shape, f32), (part_shape, bf16)],
        [info, limits],
        [offset_rows, rows] + chips,
        far_in=[stored],
        scratch=[
            pltpu.VMEM(*span_kind),
            pltpu.VMEM(*span_kind),
            pltpu.VMEM(stats_shape, f32),
            pltpu.VMEM((2 * SPAN, FEATURES), f32),
            pltpu.VMEM((2 * SPAN, FEATURES), f32),
            pltpu.VMEM((FEATURES, 2 * SPAN), bf16),
            pltpu.VMEM((GROUPS, FEATURES, GROUP_ROWS), f32),
            pltpu.SemaphoreType.DMA((2,)),
        ],
        room=28,
    )
    query_shape = (FEATURES, ROWS)
    kept, *sent = kernel_call(
        spread_z_body,
        [((2,) + query_shape, f32)] + [((2,) + query_shape, bf16)] * 3,
        [info],
        [own_query, swap(other_query, "ctx", 1)],
    )
    both, sent = lax.optimization_barrier((both, sent))
    arriving = [swap(block, "ctx", 4 * code) for code, block in zip((1, 2, 3), sent)]
    block_shape = (CHIPS, 2 * FEATURES, ROWS)
    own_weight, other_weight = resident_call(
        weight_body,
        [(block_shape, f32), (block_shape, bf16)],
        [info],
        context + [both],
    )
    own_weight, other_weight, attended_terms, arriving = lax.optimization_barrier(
        (own_weight, other_weight, attended_terms, arriving)
    )
    query_kept, sent = kernel_call(
        spread_y_body,
        [(query_shape, f32), (query_shape, bf16)],
        [info],
        [kept] + arriving,
        room=60,
    )
    weight_blocks = kernel_call(
        add_body,
        [(block_shape, bf16)],
        [],
        [own_weight, swap(other_weight, "ctx", 1)],
    )[0]
    query_rest, weight_blocks = lax.optimization_barrier((swap(sent, "ctx", 2), weight_blocks))
    same_core = [list(range(core, CTX_DEVICES, 2)) for core in range(2)]
    weight_terms = exchange(weight_blocks, "ctx", same_core)
    pair_shape = (2, ROWS, FEATURES)
    four_shape = (2,) + pair_shape
    terms = kernel_call(
        close_body,
        [(four_shape, f32), (four_shape, bf16)] * 2,
        [info],
        [w_out, w_query, attended_terms, query_kept, query_rest],
    )
    came = [swap(terms[1], "tp", FIRST_X[0]), swap(terms[3], "tp", FIRST_X[1])]
    cross, cross_sent, latent, latent_sent = kernel_call(
        fold_body,
        [(pair_shape, f32), (pair_shape, bf16)] * 2,
        [],
        [terms[0], came[0], terms[2], came[1]],
    )
    came = [swap(cross_sent, "tp", SECOND_X[0]), swap(latent_sent, "tp", SECOND_X[1])]
    sum_shape = (ROWS, 2 * FEATURES)
    kept, sent = kernel_call(
        fold_last_body,
        [(sum_shape, f32), (sum_shape, bf16)],
        [],
        [cross, came[0], latent, came[1]],
    )
    own_shape = (ROWS, FEATURES)
    return tuple(
        kernel_call(
            last_body,
            [(own_shape, bf16), (own_shape, bf16), (own_shape, f32), (own_shape, f32)],
            [],
            [kept, swap(sent, "tp", 4), weight_terms],
        )
    )


def solution(mesh):
    placed = (
        P("ctx"),
        P(None, "tp"),
        P("ctx", "tp"),
        P(None, "tp"),
        P(None, "tp"),
        P(None, "tp"),
        P("tp", None),
        P("ctx", "tp"),
        P(),
    )
    return jax.shard_map(
        shards,
        mesh=mesh,
        in_specs=placed,
        out_specs=(P("ctx", "tp"), P("ctx", "tp"), P("ctx", "tp"), P("ctx", "tp")),
        check_vma=False,
    )
```

```python
import math

import jax
import jax.numpy as jnp
from jax import lax
from jax.experimental import pallas as pl
from jax.experimental.pallas import tpu as pltpu
from jax.sharding import PartitionSpec as P

HEAD_DIM = 128
CTX_DEVICES = 16
TP_DEVICES = 8
FEATURES = 256
HEADS_HERE = FEATURES // HEAD_DIM
ROWS = 128
LAST_PEER = 6
FIRST_PEERS = (0, 1, 2, 3, 4, 5, 7)
CHIPS = CTX_DEVICES // 2
GROUPS = 4
STORED = 120
FIRST_PEER, SECOND_PEER = (1, 3), (3, 1)
KEPT_PEERS = ((0, 3), (0, 1))
SENT_PEERS = ((1, 2), (3, 2))
MIRROR = 12
LEVEL_ROWS = 16
GROUP_ROWS = 4 * ROWS
SPAN = 512

SCORE_SCALE = 1.0 / math.sqrt(HEAD_DIM)
LOG2_SCALE = SCORE_SCALE * math.log2(math.e)
MASKED = -1e30
FLOOR = -1e29

NN = (((1,), (0,)), ((), ()))
NT = (((1,), (1,)), ((), ()))
TN = (((0,), (0,)), ((), ()))

bf16 = jnp.bfloat16
f32 = jnp.float32


def mm(left, right, dims=NN):
    return lax.dot_general(left, right, dims, preferred_element_type=f32)


def swap(value, axis, bits):
    count = CTX_DEVICES if axis == "ctx" else TP_DEVICES
    return lax.ppermute(value, axis, [(i, i ^ bits) for i in range(count)])


def exchange(value, axis, groups=None):
    return lax.all_to_all(value, axis, 0, 0, axis_index_groups=groups, tiled=True)


def whole(shape):
    return pl.BlockSpec(shape, lambda i: (0,) * len(shape), pipeline_mode=pl.Buffered(1))


def kernel_call(body, outs, scalars, arrays, room=16):
    call = pl.pallas_call(
        body,
        grid=(1,),
        out_shape=[jax.ShapeDtypeStruct(shape, kind) for shape, kind in outs],
        in_specs=[pl.BlockSpec(memory_space=pltpu.SMEM)] * len(scalars)
        + [whole(a.shape) for a in arrays],
        out_specs=[whole(shape) for shape, _ in outs],
        compiler_params=pltpu.CompilerParams(vmem_limit_bytes=room * 1024 * 1024),
        cost_estimate=pl.CostEstimate(flops=0, bytes_accessed=0, transcendentals=0),
    )
    return list(call(*scalars, *arrays))


def resident_call(body, outs, scalars, arrays, far_in=(), far_out=(), scratch=(), room=16, flops=0):
    near, far = pl.BlockSpec(memory_space=pltpu.VMEM), pl.BlockSpec(memory_space=pltpu.HBM)
    call = pl.pallas_call(
        body,
        out_shape=[jax.ShapeDtypeStruct(shape, kind) for shape, kind in [*far_out, *outs]],
        in_specs=[pl.BlockSpec(memory_space=pltpu.SMEM)] * len(scalars)
        + [far] * len(far_in)
        + [near] * len(arrays),
        out_specs=[far] * len(far_out) + [near] * len(outs),
        scratch_shapes=list(scratch),
        compiler_params=pltpu.CompilerParams(vmem_limit_bytes=room * 1024 * 1024),
        cost_estimate=pl.CostEstimate(flops=flops, bytes_accessed=0, transcendentals=0),
    )
    return list(call(*scalars, *far_in, *arrays))


def far_blocks(near, back, side):
    return swap(back, "tp", 1), swap(near, "tp", 4), swap(side, "tp", 3)


def both_cores(chips):
    return jnp.concatenate(chips + [swap(pair, "ctx", 1) for pair in chips], axis=0)


def shard_start(tp_index, r):
    return pl.multiple_of((tp_index ^ r) * FEATURES, FEATURES)


def head_of(h):
    return slice(h * HEAD_DIM, (h + 1) * HEAD_DIM)


def rows_body(info, w_query, w_out, *refs):
    blocks, out = refs[:-1], refs[-1]
    query = jnp.zeros((ROWS, FEATURES), f32)
    grads = [jnp.zeros((HEAD_DIM, ROWS), f32) for _ in range(HEADS_HERE)]
    for r in range(TP_DEVICES):
        part = pl.ds(shard_start(info[0], r), FEATURES)
        query += mm(blocks[r][:ROWS, :], w_query[part, :])
        for h in range(HEADS_HERE):
            grads[h] += mm(w_out[head_of(h), part], blocks[r][ROWS:, :], NT)
    out[:ROWS, :] = query.astype(bf16)
    for h in range(HEADS_HERE):
        out[ROWS:, head_of(h)] = grads[h].astype(bf16)


def row_block(rows, ctx_index, block):
    distance = ctx_index ^ block
    return rows.at[(distance & 1) * CHIPS + (distance >> 1)]


def group_query(rows, ctx_index, group, h):
    blocks = [row_block(rows, ctx_index, GROUPS * group + i) for i in range(GROUPS)]
    return jnp.concatenate([block[:ROWS, head_of(h)] for block in blocks], axis=0)


def group_grad(rows, ctx_index, group, h):
    blocks = [row_block(rows, ctx_index, GROUPS * group + i) for i in range(GROUPS)]
    return jnp.concatenate([block[ROWS:, head_of(h)] for block in blocks], axis=1)


def masked(scores, base, offset_row):
    if offset_row is None:
        return scores
    places = base + lax.broadcasted_iota(jnp.int32, (SPAN, GROUP_ROWS), 0)
    return jnp.where(places <= offset_row, scores, MASKED)


def visit(bounds, base, offsets, group, block):
    whole_seen = bounds[1, group] >= base + (SPAN - 1)

    @pl.when(whole_seen)
    def _():
        block(None)

    @pl.when(jnp.logical_and(bounds[0, group] >= base, jnp.logical_not(whole_seen)))
    def _():
        block(offsets[group])


def pieces_of(level):
    pieces = []
    for _ in range(3):
        piece = level.astype(bf16).astype(f32)
        pieces.append(piece)
        level = level - piece
    return pieces


def turned(value):
    return value.astype(f32).T.astype(bf16)


def span_of(i):
    return slice(i * SPAN, (i + 1) * SPAN)


def ordered_rows(weight, tp_index, order):
    return jnp.concatenate(
        [weight[pl.ds(shard_start(tp_index, r), FEATURES), :] for r in order], axis=0
    )


def project_body(info, w_key, w_value, *refs):
    context = jnp.concatenate([ref[...] for ref in refs[:-1]], axis=1)
    out = refs[-1]
    out[:, :FEATURES] = mm(context, ordered_rows(w_key, info[0], FIRST_PEERS))
    out[:, FEATURES:] = mm(context, ordered_rows(w_value, info[0], FIRST_PEERS))


def forward_body(info, limits, *refs):
    offsets, rows, w_key, w_value, begun, last, stored = refs[:7]
    stats, blocks, keys, values, values_t, parts, copied = refs[7:]
    ctx_index = info[1]
    start = shard_start(info[0], LAST_PEER)
    for i, (weight, out) in enumerate(((w_key, keys), (w_value, values))):
        rest = mm(last[...], weight[pl.ds(start, FEATURES), :])
        out[...] = (begun[:, i * FEATURES : (i + 1) * FEATURES] + rest).astype(bf16)
    copies = [
        pltpu.make_async_copy(keys, stored.at[0], copied.at[0]),
        pltpu.make_async_copy(values, stored.at[1], copied.at[1]),
    ]
    for copy in copies:
        copy.start()
    for h in range(HEADS_HERE):
        values_t[head_of(h), :] = turned(values[:, head_of(h)])

    def step(group, carry):
        stats[group, :2, :] = jnp.full((2, GROUP_ROWS), MASKED, f32)
        stats[group, 2:, :] = jnp.zeros((2, GROUP_ROWS), f32)
        parts[...] = jnp.zeros((FEATURES, GROUP_ROWS), f32)
        for i in range(2):
            base = info[2 + i]

            def block(offset_row, i=i, base=base):
                for h in range(HEADS_HERE):
                    query = group_query(rows, ctx_index, group, h)
                    scores = mm(keys[span_of(i), head_of(h)], query, NT) * LOG2_SCALE
                    scores = masked(scores, base, offset_row)
                    old = stats[group, h : h + 1, :]
                    peak = jnp.maximum(jnp.max(scores, axis=0, keepdims=True), FLOOR)
                    peak = jnp.maximum(peak, old)
                    weights = jnp.exp2(scores - peak)
                    keep = jnp.exp2(old - peak)
                    total = keep * stats[group, h + 2 : h + 3, :]
                    total += jnp.sum(weights, axis=0, keepdims=True)
                    part = mm(values_t[head_of(h), span_of(i)], weights.astype(bf16))
                    parts[head_of(h), :] = keep * parts[head_of(h), :] + part
                    stats[group, h : h + 1, :] = peak
                    stats[group, h + 2 : h + 3, :] = total

            visit(limits, base, offsets, group, block)

        levels = []
        for h in range(HEADS_HERE):
            total = stats[group, h + 2 : h + 3, :]
            some = total > 0.0
            safe = jnp.where(some, total, 1.0)
            part = parts[head_of(h), :] * jnp.where(some, 1.0 / safe, 0.0)
            grad_t = group_grad(rows, ctx_index, group, h).astype(f32)
            level = jnp.where(some, stats[group, h : h + 1, :] + jnp.log2(safe), MASKED)
            stats[group, h : h + 1, :] = level
            stats[group, h + 2 : h + 3, :] = jnp.sum(part * grad_t, axis=0, keepdims=True)
            levels += pieces_of(level)
            for i in range(GROUPS):
                place = GROUPS * group + i
                lanes = slice(i * ROWS, (i + 1) * ROWS)
                blocks[place, head_of(h), :] = part[:, lanes].astype(bf16)
        levels.append(jnp.zeros((LEVEL_ROWS - len(levels), GROUP_ROWS), f32))
        levels = jnp.concatenate(levels, axis=0).astype(bf16)
        for i in range(GROUPS):
            place = GROUPS * group + i
            blocks[place, FEATURES:, :] = levels[:, i * ROWS : (i + 1) * ROWS]
        return carry

    lax.fori_loop(0, GROUPS, step, 0)
    for copy in copies:
        copy.wait()


def join_body(own, other, stats):
    for group in range(GROUPS):
        one, two = own[group], other[group]
        top = jnp.maximum(one[:2], two[:2])
        first, second = jnp.exp2(one[:2] - top), jnp.exp2(two[:2] - top)
        total = first + second
        stats[group, :2, :] = top + jnp.log2(total)
        stats[group, 2:, :] = (first * one[2:] + second * two[2:]) / total


def split_parity(core, group, value, mine, other):
    for i in range(GROUPS // 2):
        low = value[:, 2 * i * ROWS : (2 * i + 1) * ROWS]
        high = value[:, (2 * i + 1) * ROWS : (2 * i + 2) * ROWS]
        chip = group * (GROUPS // 2) + i
        mine[chip] = jnp.where(core == 1, high, low)
        other[chip] = jnp.where(core == 1, low, high).astype(bf16)


def backward_body(info, limits, *refs):
    stored, offsets, rows, stats, both, mine, other = refs[:7]
    keys, values, key_acc, value_acc, keys_t, query_acc, copied = refs[7:]
    copies = [
        pltpu.make_async_copy(stored.at[0], keys, copied.at[0]),
        pltpu.make_async_copy(stored.at[1], values, copied.at[1]),
    ]
    for copy in copies:
        copy.start()
    ctx_index = info[1]
    query_acc[...] = jnp.zeros(query_acc.shape, f32)
    key_acc[...] = jnp.zeros(key_acc.shape, f32)
    value_acc[...] = jnp.zeros(value_acc.shape, f32)
    for copy in copies:
        copy.wait()
    for h in range(HEADS_HERE):
        keys_t[head_of(h), :] = turned(keys[:, head_of(h)])

    def step(group, carry):
        for i in range(2):
            base = info[2 + i]
            span = span_of(i)

            def block(offset_row, span=span, base=base):
                for h in range(HEADS_HERE):
                    query = group_query(rows, ctx_index, group, h)
                    grad_t = group_grad(rows, ctx_index, group, h)
                    scores = mm(keys[span, head_of(h)], query, NT) * LOG2_SCALE
                    scores = masked(scores - stats[group, h : h + 1, :], base, offset_row)
                    probs = jnp.exp2(scores)
                    prob_grad = mm(values[span, head_of(h)], grad_t)
                    delta = stats[group, h + 2 : h + 3, :]
                    score_grad = (probs * (prob_grad - delta) * SCORE_SCALE).astype(bf16)
                    value_acc[span, head_of(h)] += mm(probs.astype(bf16), grad_t, NT)
                    key_acc[span, head_of(h)] += mm(score_grad, query)
                    query_acc[group, head_of(h), :] += mm(keys_t[head_of(h), span], score_grad)

            visit(limits, base, offsets, group, block)

        return carry

    lax.fori_loop(0, GROUPS, step, 0)
    both[:FEATURES, :] = turned(key_acc[...])
    both[FEATURES:, :] = turned(value_acc[...])
    for group in range(GROUPS):
        split_parity(ctx_index & 1, group, query_acc[group], mine, other)


def weight_body(info, *refs):
    both, mine, other = refs[TP_DEVICES:]
    flipped = (info[1] & 1) == 1
    for r in range(TP_DEVICES):
        terms = mm(both[...], refs[r][...])
        place = info[0] ^ r
        low, high = terms[:, :ROWS], terms[:, ROWS:]
        mine[place] = jnp.where(flipped, high, low)
        other[place] = jnp.where(flipped, low, high).astype(bf16)


def add_body(own, received, out):
    out[...] = (own[...] + received[...].astype(f32)).astype(bf16)


def spread_z_body(info, own, received, *outs):
    z = info[1] >> 2
    for h in range(HEADS_HERE):
        for peers, out in ((KEPT_PEERS[h], outs[2 * h]), (SENT_PEERS[h], outs[2 * h + 1])):
            for i, peer in enumerate(peers):
                for y in range(2):
                    place = 2 * (z ^ peer) + y
                    term = own[place, head_of(h), :] + received[place, head_of(h), :].astype(f32)
                    out[i, y] = term.astype(out.dtype)


def spread_y_body(info, one, one_came, two, two_came, kept, sent):
    y = (info[1] >> 1) & 1
    for h, (own, came) in enumerate(((one, one_came), (two, two_came))):
        for place, out in ((y, kept), (1 - y, sent)):
            total = own[place] + came[place].astype(f32)
            out[head_of(h), :] = total.astype(out.dtype)


def weighted_sum(blocks):
    heads = []
    for h in range(HEADS_HERE):
        levels = []
        for i in range(CTX_DEVICES):
            pieces = blocks[i, FEATURES:, :].astype(f32)[3 * h : 3 * h + 3]
            levels.append(pieces[0:1] + pieces[1:2] + pieces[2:3])
        top = levels[0]
        for level in levels[1:]:
            top = jnp.maximum(top, level)
        weights = [jnp.exp2(level - top) for level in levels]
        scale = 1.0 / sum(weights)
        total = jnp.zeros((HEAD_DIM, ROWS), f32)
        for i in range(CTX_DEVICES):
            total += weights[i] * blocks[i, head_of(h), :].astype(f32)
        heads.append(total * scale)
    return jnp.concatenate(heads, axis=0)


def total_of(terms):
    total = terms[0].astype(f32)
    for i in range(1, terms.shape[0]):
        total = total + terms[i].astype(f32)
    return total


def close_body(info, w_out, w_query, attended_terms, query_kept, query_rest, *outs):
    attended = weighted_sum(attended_terms).T.astype(bf16)
    query_grad = (query_kept[...] + query_rest[...].astype(f32)).T.astype(bf16)
    for y in range(2):
        for x in range(4):
            part = pl.ds(shard_start(info[0], 4 * y + x), FEATURES)
            cross = mm(attended, w_out[:, part])
            latent = mm(query_grad, w_query[part, :], NT)
            for half, terms in ((0, cross), (1, latent)):
                stays = KEPT_PEERS[half]
                out = outs[2 * half + (x not in stays)]
                place = (stays if x in stays else SENT_PEERS[half]).index(x)
                out[place, y] = terms.astype(out.dtype)


def fold_body(*refs):
    for half in range(2):
        stays, came = refs[2 * half : 2 * half + 2]
        kept, sent = refs[4 + 2 * half : 6 + 2 * half]
        kept[...] = stays[0] + came[0].astype(f32)
        sent[...] = (stays[1] + came[1].astype(f32)).astype(bf16)


def fold_last_body(cross, cross_came, latent, latent_came, kept, sent):
    for half, (own, came) in enumerate(((cross, cross_came), (latent, latent_came))):
        columns = slice(half * FEATURES, (half + 1) * FEATURES)
        kept[:, columns] = own[0] + came[0].astype(f32)
        sent[:, columns] = (own[1] + came[1].astype(f32)).astype(bf16)


def last_body(kept, rest, terms, cross_out, latent_grad, key_grad, value_grad):
    total = (kept[...] + rest[...].astype(f32)).astype(bf16)
    cross_out[...] = total[:, :FEATURES]
    latent_grad[...] = total[:, FEATURES:]
    total = total_of(terms).T
    key_grad[...] = total[:, :FEATURES]
    value_grad[...] = total[:, FEATURES:]


def shards(token_ids, embed_table, latents, w_query, w_key, w_value, w_out, out_grad, offsets):
    ctx_index = lax.axis_index("ctx").astype(jnp.int32)
    tp_index = lax.axis_index("tp").astype(jnp.int32)
    key_count = token_ids.shape[0]

    mirror_ids = swap(token_ids[SPAN:], "ctx", MIRROR)
    info = jnp.stack(
        [
            tp_index,
            ctx_index,
            ctx_index * key_count,
            (ctx_index ^ MIRROR) * key_count + SPAN,
        ]
    )
    grouped = offsets.reshape(GROUPS, GROUP_ROWS)
    limits = jnp.stack([jnp.max(grouped, axis=1), jnp.min(grouped, axis=1)])
    offset_rows = offsets.reshape(GROUPS, 1, GROUP_ROWS)

    row_part = jnp.concatenate([latents, out_grad], axis=0)
    row_part, mirror_ids = lax.optimization_barrier((row_part, mirror_ids))
    near, back, side = (swap(row_part, "tp", bits) for bits in (1, 3, 4))
    near, back, side, info, limits, offset_rows = lax.optimization_barrier(
        (near, back, side, info, limits, offset_rows)
    )
    far, side_near, side_back = far_blocks(near, back, side)
    ids = jnp.concatenate([token_ids[:SPAN], mirror_ids])
    context_part = embed_table.at[ids].get(mode="promise_in_bounds")
    far, side_near, side_back, context_part = lax.optimization_barrier(
        (far, side_near, side_back, context_part)
    )
    side_far = swap(side_back, "tp", 1)
    context_back, context_side = swap(context_part, "tp", 3), swap(context_part, "tp", 4)
    side_far, context_late = lax.optimization_barrier((side_far, context_part))
    context_first = (swap(context_late, "tp", 1), context_back, context_side)
    row_blocks = [row_part, near, far, back, side, side_near, side_far, side_back]

    own = kernel_call(
        rows_body,
        [((2 * ROWS, FEATURES), bf16)],
        [info],
        [w_query, w_out] + row_blocks,
        room=60,
    )[0]
    beside, context_first = lax.optimization_barrier((swap(own, "ctx", 2), context_first))
    near, back, side = context_first
    far, side_near, side_back = lax.optimization_barrier(far_blocks(near, back, side))
    side_far = swap(side_back, "tp", 1)
    chips = [jnp.stack([own, beside])]
    chips += [swap(chips[0], "ctx", code) for code in (4, 8, 12)]
    context = [context_part, near, far, back, side, side_near, side_far, side_back]
    begun = resident_call(
        project_body,
        [((2 * SPAN, 2 * FEATURES), f32)],
        [info],
        [w_key, w_value] + [context[r] for r in FIRST_PEERS],
    )[0]
    chips, begun = lax.optimization_barrier((chips, begun))
    rows = both_cores(chips)

    part_shape = (CHIPS, FEATURES, ROWS)
    stats_shape = (GROUPS, 4, GROUP_ROWS)
    span_kind = ((2 * SPAN, FEATURES), bf16)
    stored, local, out_blocks = resident_call(
        forward_body,
        [
            (stats_shape, f32),
            ((CTX_DEVICES, FEATURES + LEVEL_ROWS, ROWS), bf16),
        ],
        [info, limits],
        [offset_rows, rows, w_key, w_value, begun, context[LAST_PEER]],
        far_out=[((STORED,) + span_kind[0], bf16)],
        scratch=[
            pltpu.VMEM(*span_kind),
            pltpu.VMEM(*span_kind),
            pltpu.VMEM((FEATURES, 2 * SPAN), bf16),
            pltpu.VMEM((FEATURES, GROUP_ROWS), f32),
            pltpu.SemaphoreType.DMA((2,)),
        ],
        room=24,
    )

    stats = local
    for code in (1, 2, 4, 12):
        peers = swap(stats, "ctx", code)
        stats = kernel_call(join_body, [(stats_shape, f32)], [], [stats, peers])[0]
    out_blocks, stats = lax.optimization_barrier((out_blocks, stats))
    attended_terms = exchange(out_blocks, "ctx")

    both, own_query, other_query = resident_call(
        backward_body,
        [((2 * FEATURES, 2 * SPAN), bf16), (part_shape, f32), (part_shape, bf16)],
        [info, limits],
        [offset_rows, rows, stats],
        far_in=[stored],
        scratch=[
            pltpu.VMEM(*span_kind),
            pltpu.VMEM(*span_kind),
            pltpu.VMEM((2 * SPAN, FEATURES), f32),
            pltpu.VMEM((2 * SPAN, FEATURES), f32),
            pltpu.VMEM((FEATURES, 2 * SPAN), bf16),
            pltpu.VMEM((GROUPS, FEATURES, GROUP_ROWS), f32),
            pltpu.SemaphoreType.DMA((2,)),
        ],
        room=28,
    )
    query_shape = (FEATURES, ROWS)
    head_shape = (2, HEAD_DIM, ROWS)
    terms = kernel_call(
        spread_z_body,
        [((2,) + head_shape, f32), ((2,) + head_shape, bf16)] * 2,
        [info],
        [own_query, swap(other_query, "ctx", 1)],
    )
    both, terms = lax.optimization_barrier((both, terms))
    came = [swap(terms[1], "ctx", 4 * FIRST_PEER[0]), swap(terms[3], "ctx", 4 * FIRST_PEER[1])]
    block_shape = (CHIPS, 2 * FEATURES, ROWS)
    own_weight, other_weight = resident_call(
        weight_body,
        [(block_shape, f32), (block_shape, bf16)],
        [info],
        context + [both],
    )
    own_weight, other_weight, attended_terms, came = lax.optimization_barrier(
        (own_weight, other_weight, attended_terms, came)
    )
    one, one_sent, two, two_sent = kernel_call(
        fold_body,
        [(head_shape, f32), (head_shape, bf16)] * 2,
        [],
        [terms[0], came[0], terms[2], came[1]],
        room=60,
    )
    came = [swap(one_sent, "ctx", 4 * SECOND_PEER[0]), swap(two_sent, "ctx", 4 * SECOND_PEER[1])]
    query_kept, sent = kernel_call(
        spread_y_body,
        [(query_shape, f32), (query_shape, bf16)],
        [info],
        [one, came[0], two, came[1]],
        room=60,
    )
    weight_blocks = kernel_call(
        add_body,
        [(block_shape, bf16)],
        [],
        [own_weight, swap(other_weight, "ctx", 1)],
    )[0]
    query_rest, weight_blocks = lax.optimization_barrier((swap(sent, "ctx", 2), weight_blocks))
    same_core = [list(range(core, CTX_DEVICES, 2)) for core in range(2)]
    weight_terms = exchange(weight_blocks, "ctx", same_core)
    pair_shape = (2, ROWS, FEATURES)
    four_shape = (2,) + pair_shape
    terms = kernel_call(
        close_body,
        [(four_shape, f32), (four_shape, bf16)] * 2,
        [info],
        [w_out, w_query, attended_terms, query_kept, query_rest],
    )
    came = [swap(terms[1], "tp", FIRST_PEER[0]), swap(terms[3], "tp", FIRST_PEER[1])]
    cross, cross_sent, latent, latent_sent = kernel_call(
        fold_body,
        [(pair_shape, f32), (pair_shape, bf16)] * 2,
        [],
        [terms[0], came[0], terms[2], came[1]],
    )
    came = [swap(cross_sent, "tp", SECOND_PEER[0]), swap(latent_sent, "tp", SECOND_PEER[1])]
    sum_shape = (ROWS, 2 * FEATURES)
    kept, sent = kernel_call(
        fold_last_body,
        [(sum_shape, f32), (sum_shape, bf16)],
        [],
        [cross, came[0], latent, came[1]],
    )
    own_shape = (ROWS, FEATURES)
    return tuple(
        kernel_call(
            last_body,
            [(own_shape, bf16), (own_shape, bf16), (own_shape, f32), (own_shape, f32)],
            [],
            [kept, swap(sent, "tp", 4), weight_terms],
        )
    )


def solution(mesh):
    placed = (
        P("ctx"),
        P(None, "tp"),
        P("ctx", "tp"),
        P(None, "tp"),
        P(None, "tp"),
        P(None, "tp"),
        P("tp", None),
        P("ctx", "tp"),
        P(),
    )
    return jax.shard_map(
        shards,
        mesh=mesh,
        in_specs=placed,
        out_specs=(P("ctx", "tp"), P("ctx", "tp"), P("ctx", "tp"), P("ctx", "tp")),
        check_vma=False,
    )
```

```python
import math

import jax
import jax.numpy as jnp
from jax import lax
from jax.experimental import pallas as pl
from jax.experimental.pallas import tpu as pltpu
from jax.sharding import PartitionSpec as P

HEAD_DIM = 128
CTX_DEVICES = 16
TP_DEVICES = 8
FEATURES = 256
HEADS_HERE = FEATURES // HEAD_DIM
ROWS = 128
LAST_PEER = 6
FIRST_PEERS = (0, 1, 2, 3, 4, 5, 7)
CHIPS = CTX_DEVICES // 2
GROUPS = 4
STORED = 120
FIRST_X, SECOND_X = (1, 3), (3, 1)
KEPT_PEERS = ((0, 3), (0, 1))
SENT_PEERS = ((1, 2), (3, 2))
MIRROR = 12
LEVEL_ROWS = 16
GROUP_ROWS = 4 * ROWS
SPAN = 512

SCORE_SCALE = 1.0 / math.sqrt(HEAD_DIM)
LOG2_SCALE = SCORE_SCALE * math.log2(math.e)
MASKED = -1e30
FLOOR = -1e29

NN = (((1,), (0,)), ((), ()))
NT = (((1,), (1,)), ((), ()))
TN = (((0,), (0,)), ((), ()))

bf16 = jnp.bfloat16
f32 = jnp.float32


def mm(left, right, dims=NN):
    return lax.dot_general(left, right, dims, preferred_element_type=f32)


def swap(value, axis, bits):
    count = CTX_DEVICES if axis == "ctx" else TP_DEVICES
    return lax.ppermute(value, axis, [(i, i ^ bits) for i in range(count)])


def exchange(value, axis, groups=None):
    return lax.all_to_all(value, axis, 0, 0, axis_index_groups=groups, tiled=True)


def whole(shape):
    return pl.BlockSpec(shape, lambda i: (0,) * len(shape), pipeline_mode=pl.Buffered(1))


def kernel_call(body, outs, scalars, arrays, room=16):
    call = pl.pallas_call(
        body,
        grid=(1,),
        out_shape=[jax.ShapeDtypeStruct(shape, kind) for shape, kind in outs],
        in_specs=[pl.BlockSpec(memory_space=pltpu.SMEM)] * len(scalars)
        + [whole(a.shape) for a in arrays],
        out_specs=[whole(shape) for shape, _ in outs],
        compiler_params=pltpu.CompilerParams(vmem_limit_bytes=room * 1024 * 1024),
        cost_estimate=pl.CostEstimate(flops=0, bytes_accessed=0, transcendentals=0),
    )
    return list(call(*scalars, *arrays))


def resident_call(body, outs, scalars, arrays, far_in=(), far_out=(), scratch=(), room=16, flops=0):
    near, far = pl.BlockSpec(memory_space=pltpu.VMEM), pl.BlockSpec(memory_space=pltpu.HBM)
    call = pl.pallas_call(
        body,
        out_shape=[jax.ShapeDtypeStruct(shape, kind) for shape, kind in [*far_out, *outs]],
        in_specs=[pl.BlockSpec(memory_space=pltpu.SMEM)] * len(scalars)
        + [far] * len(far_in)
        + [near] * len(arrays),
        out_specs=[far] * len(far_out) + [near] * len(outs),
        scratch_shapes=list(scratch),
        compiler_params=pltpu.CompilerParams(vmem_limit_bytes=room * 1024 * 1024),
        cost_estimate=pl.CostEstimate(flops=flops, bytes_accessed=0, transcendentals=0),
    )
    return list(call(*scalars, *far_in, *arrays))


def far_blocks(near, back, side):
    return swap(back, "tp", 1), swap(near, "tp", 4), swap(side, "tp", 3)


def both_cores(chips):
    return jnp.concatenate(chips + [swap(pair, "ctx", 1) for pair in chips], axis=0)


def shard_start(tp_index, r):
    return pl.multiple_of((tp_index ^ r) * FEATURES, FEATURES)


def tp_place():
    return lax.axis_index("tp").astype(jnp.int32)


def ctx_place():
    return lax.axis_index("ctx").astype(jnp.int32)


def key_bases(ctx_index):
    return ctx_index * (2 * SPAN), (ctx_index ^ MIRROR) * (2 * SPAN) + SPAN


def head_of(h):
    return slice(h * HEAD_DIM, (h + 1) * HEAD_DIM)


def rows_body(w_query, w_out, *refs):
    blocks, out = refs[:-1], refs[-1]
    query = jnp.zeros((ROWS, FEATURES), f32)
    grads = [jnp.zeros((HEAD_DIM, ROWS), f32) for _ in range(HEADS_HERE)]
    for r in range(TP_DEVICES):
        part = pl.ds(shard_start(tp_place(), r), FEATURES)
        query += mm(blocks[r][:ROWS, :], w_query[part, :])
        for h in range(HEADS_HERE):
            grads[h] += mm(w_out[head_of(h), part], blocks[r][ROWS:, :], NT)
    out[:ROWS, :] = query.astype(bf16)
    for h in range(HEADS_HERE):
        out[ROWS:, head_of(h)] = grads[h].astype(bf16)


def row_block(rows, ctx_index, block):
    distance = ctx_index ^ block
    return rows.at[(distance & 1) * CHIPS + (distance >> 1)]


def group_query(rows, ctx_index, group, h):
    blocks = [row_block(rows, ctx_index, GROUPS * group + i) for i in range(GROUPS)]
    return jnp.concatenate([block[:ROWS, head_of(h)] for block in blocks], axis=0)


def group_grad(rows, ctx_index, group, h):
    blocks = [row_block(rows, ctx_index, GROUPS * group + i) for i in range(GROUPS)]
    return jnp.concatenate([block[ROWS:, head_of(h)] for block in blocks], axis=1)


def masked(scores, base, offset_row):
    if offset_row is None:
        return scores
    places = base + lax.broadcasted_iota(jnp.int32, (SPAN, GROUP_ROWS), 0)
    return jnp.where(places <= offset_row, scores, MASKED)


def visit(bounds, base, offsets, group, block):
    first, last = bounds[group * GROUP_ROWS], bounds[group * GROUP_ROWS + GROUP_ROWS - 1]
    whole_seen = first >= base + (SPAN - 1)

    @pl.when(whole_seen)
    def _():
        block(None)

    @pl.when(jnp.logical_and(last >= base, jnp.logical_not(whole_seen)))
    def _():
        lanes = [offsets[pl.ds(group * GROUPS + i, 1), :] for i in range(GROUPS)]
        block(jnp.concatenate(lanes, axis=1))


def pieces_of(level):
    pieces = []
    for _ in range(3):
        piece = level.astype(bf16).astype(f32)
        pieces.append(piece)
        level = level - piece
    return pieces


def turned(value):
    return value.astype(f32).T.astype(bf16)


def span_of(i):
    return slice(i * SPAN, (i + 1) * SPAN)


def ordered_rows(weight, tp_index, order):
    return jnp.concatenate(
        [weight[pl.ds(shard_start(tp_index, r), FEATURES), :] for r in order], axis=0
    )


def project_body(w_key, w_value, *refs):
    context = jnp.concatenate([ref[...] for ref in refs[:-1]], axis=1)
    out = refs[-1]
    out[:, :FEATURES] = mm(context, ordered_rows(w_key, tp_place(), FIRST_PEERS))
    out[:, FEATURES:] = mm(context, ordered_rows(w_value, tp_place(), FIRST_PEERS))


def forward_body(bounds, *refs):
    offsets, rows, w_key, w_value, begun, last, stored = refs[:7]
    stats, blocks, keys, values, values_t, parts, copied = refs[7:]
    ctx_index = ctx_place()
    bases = key_bases(ctx_index)
    start = shard_start(tp_place(), LAST_PEER)
    for i, (weight, out) in enumerate(((w_key, keys), (w_value, values))):
        rest = mm(last[...], weight[pl.ds(start, FEATURES), :])
        out[...] = (begun[:, i * FEATURES : (i + 1) * FEATURES] + rest).astype(bf16)
    copies = [
        pltpu.make_async_copy(keys, stored.at[0], copied.at[0]),
        pltpu.make_async_copy(values, stored.at[1], copied.at[1]),
    ]
    for copy in copies:
        copy.start()
    for h in range(HEADS_HERE):
        values_t[head_of(h), :] = turned(values[:, head_of(h)])

    def step(group, carry):
        stats[group, :2, :] = jnp.full((2, GROUP_ROWS), MASKED, f32)
        stats[group, 2:, :] = jnp.zeros((2, GROUP_ROWS), f32)
        parts[...] = jnp.zeros((FEATURES, GROUP_ROWS), f32)
        for i in range(2):
            base = bases[i]

            def block(offset_row, i=i, base=base):
                for h in range(HEADS_HERE):
                    query = group_query(rows, ctx_index, group, h)
                    scores = mm(keys[span_of(i), head_of(h)], query, NT) * LOG2_SCALE
                    scores = masked(scores, base, offset_row)
                    old = stats[group, h : h + 1, :]
                    peak = jnp.maximum(jnp.max(scores, axis=0, keepdims=True), FLOOR)
                    peak = jnp.maximum(peak, old)
                    weights = jnp.exp2(scores - peak)
                    keep = jnp.exp2(old - peak)
                    total = keep * stats[group, h + 2 : h + 3, :]
                    total += jnp.sum(weights, axis=0, keepdims=True)
                    part = mm(values_t[head_of(h), span_of(i)], weights.astype(bf16))
                    parts[head_of(h), :] = keep * parts[head_of(h), :] + part
                    stats[group, h : h + 1, :] = peak
                    stats[group, h + 2 : h + 3, :] = total

            visit(bounds, base, offsets, group, block)

        levels = []
        for h in range(HEADS_HERE):
            total = stats[group, h + 2 : h + 3, :]
            some = total > 0.0
            safe = jnp.where(some, total, 1.0)
            part = parts[head_of(h), :] * jnp.where(some, 1.0 / safe, 0.0)
            grad_t = group_grad(rows, ctx_index, group, h).astype(f32)
            level = jnp.where(some, stats[group, h : h + 1, :] + jnp.log2(safe), MASKED)
            stats[group, h : h + 1, :] = level
            stats[group, h + 2 : h + 3, :] = jnp.sum(part * grad_t, axis=0, keepdims=True)
            levels += pieces_of(level)
            for i in range(GROUPS):
                place = GROUPS * group + i
                lanes = slice(i * ROWS, (i + 1) * ROWS)
                blocks[place, head_of(h), :] = part[:, lanes].astype(bf16)
        levels.append(jnp.zeros((LEVEL_ROWS - len(levels), GROUP_ROWS), f32))
        levels = jnp.concatenate(levels, axis=0).astype(bf16)
        for i in range(GROUPS):
            place = GROUPS * group + i
            blocks[place, FEATURES:, :] = levels[:, i * ROWS : (i + 1) * ROWS]
        return carry

    lax.fori_loop(0, GROUPS, step, 0)
    for copy in copies:
        copy.wait()


def joined(refs, group):
    pieces = [ref[group] for ref in refs]
    top = pieces[0][:2]
    for piece in pieces[1:]:
        top = jnp.maximum(top, piece[:2])
    total = jnp.zeros((2, GROUP_ROWS), f32)
    delta = jnp.zeros((2, GROUP_ROWS), f32)
    for piece in pieces:
        weight = jnp.exp2(piece[:2] - top)
        total += weight
        delta += weight * piece[2:]
    return top + jnp.log2(total), delta / total


def join_body(own, one, two, three, stats):
    for group in range(GROUPS):
        level, delta = joined((own, one, two, three), group)
        stats[group, :2, :] = level
        stats[group, 2:, :] = delta


def split_parity(core, group, value, mine, other):
    for i in range(GROUPS // 2):
        low = value[:, 2 * i * ROWS : (2 * i + 1) * ROWS]
        high = value[:, (2 * i + 1) * ROWS : (2 * i + 2) * ROWS]
        chip = group * (GROUPS // 2) + i
        mine[chip] = jnp.where(core == 1, high, low)
        other[chip] = jnp.where(core == 1, low, high).astype(bf16)


def backward_body(bounds, *refs):
    stored, offsets, rows, own, one, two, three, both, mine, other = refs[:10]
    keys, values, stats, key_acc, value_acc, keys_t, query_acc, copied = refs[10:]
    copies = [
        pltpu.make_async_copy(stored.at[0], keys, copied.at[0]),
        pltpu.make_async_copy(stored.at[1], values, copied.at[1]),
    ]
    for copy in copies:
        copy.start()
    for group in range(GROUPS):
        level, delta = joined((own, one, two, three), group)
        stats[group, :2, :] = level
        stats[group, 2:, :] = delta
    ctx_index = ctx_place()
    bases = key_bases(ctx_index)
    query_acc[...] = jnp.zeros(query_acc.shape, f32)
    key_acc[...] = jnp.zeros(key_acc.shape, f32)
    value_acc[...] = jnp.zeros(value_acc.shape, f32)
    for copy in copies:
        copy.wait()
    for h in range(HEADS_HERE):
        keys_t[head_of(h), :] = turned(keys[:, head_of(h)])

    def step(group, carry):
        for i in range(2):
            base = bases[i]
            span = span_of(i)

            def block(offset_row, span=span, base=base):
                for h in range(HEADS_HERE):
                    query = group_query(rows, ctx_index, group, h)
                    grad_t = group_grad(rows, ctx_index, group, h)
                    scores = mm(keys[span, head_of(h)], query, NT) * LOG2_SCALE
                    scores = masked(scores - stats[group, h : h + 1, :], base, offset_row)
                    probs = jnp.exp2(scores)
                    prob_grad = mm(values[span, head_of(h)], grad_t)
                    delta = stats[group, h + 2 : h + 3, :]
                    score_grad = (probs * (prob_grad - delta) * SCORE_SCALE).astype(bf16)
                    value_acc[span, head_of(h)] += mm(probs.astype(bf16), grad_t, NT)
                    key_acc[span, head_of(h)] += mm(score_grad, query)
                    query_acc[group, head_of(h), :] += mm(keys_t[head_of(h), span], score_grad)

            visit(bounds, base, offsets, group, block)

        return carry

    lax.fori_loop(0, GROUPS, step, 0)
    both[:FEATURES, :] = turned(key_acc[...])
    both[FEATURES:, :] = turned(value_acc[...])
    for group in range(GROUPS):
        split_parity(ctx_index & 1, group, query_acc[group], mine, other)


def weight_body(*refs):
    both, mine, other = refs[TP_DEVICES:]
    flipped = (ctx_place() & 1) == 1
    for r in range(TP_DEVICES):
        terms = mm(both[...], refs[r][...])
        place = tp_place() ^ r
        low, high = terms[:, :ROWS], terms[:, ROWS:]
        mine[place] = jnp.where(flipped, high, low)
        other[place] = jnp.where(flipped, low, high).astype(bf16)


def add_body(own, received, out):
    out[...] = (own[...] + received[...].astype(f32)).astype(bf16)


def spread_z_body(own, received, kept, one, two, three):
    z = ctx_place() >> 2
    for y in range(2):
        place = 2 * z + y
        kept[y] = own[place] + received[place].astype(f32)
        for code, out in ((1, one), (2, two), (3, three)):
            place = 2 * (z ^ code) + y
            out[y] = (own[place] + received[place].astype(f32)).astype(bf16)


def spread_y_body(own, one, two, three, kept, sent):
    y = (ctx_place() >> 1) & 1
    for place, out in ((y, kept), (1 - y, sent)):
        total = own[place]
        for term in (one, two, three):
            total += term[place].astype(f32)
        out[...] = total.astype(out.dtype)


def weighted_sum(blocks):
    heads = []
    for h in range(HEADS_HERE):
        levels = []
        for i in range(CTX_DEVICES):
            pieces = blocks[i, FEATURES:, :].astype(f32)[3 * h : 3 * h + 3]
            levels.append(pieces[0:1] + pieces[1:2] + pieces[2:3])
        top = levels[0]
        for level in levels[1:]:
            top = jnp.maximum(top, level)
        weights = [jnp.exp2(level - top) for level in levels]
        scale = 1.0 / sum(weights)
        total = jnp.zeros((HEAD_DIM, ROWS), f32)
        for i in range(CTX_DEVICES):
            total += weights[i] * blocks[i, head_of(h), :].astype(f32)
        heads.append(total * scale)
    return jnp.concatenate(heads, axis=0)


def total_of(terms):
    total = terms[0].astype(f32)
    for i in range(1, terms.shape[0]):
        total = total + terms[i].astype(f32)
    return total


def close_body(w_out, w_query, attended_terms, query_kept, query_rest, *outs):
    attended = weighted_sum(attended_terms).T.astype(bf16)
    query_grad = (query_kept[...] + query_rest[...].astype(f32)).T.astype(bf16)
    for y in range(2):
        for x in range(4):
            part = pl.ds(shard_start(tp_place(), 4 * y + x), FEATURES)
            cross = mm(attended, w_out[:, part])
            latent = mm(query_grad, w_query[part, :], NT)
            for half, terms in ((0, cross), (1, latent)):
                stays = KEPT_PEERS[half]
                out = outs[2 * half + (x not in stays)]
                place = (stays if x in stays else SENT_PEERS[half]).index(x)
                out[place, y] = terms.astype(out.dtype)


def fold_body(*refs):
    for half in range(2):
        stays, came = refs[2 * half : 2 * half + 2]
        kept, sent = refs[4 + 2 * half : 6 + 2 * half]
        kept[...] = stays[0] + came[0].astype(f32)
        sent[...] = (stays[1] + came[1].astype(f32)).astype(bf16)


def fold_last_body(cross, cross_came, latent, latent_came, kept, sent):
    for half, (own, came) in enumerate(((cross, cross_came), (latent, latent_came))):
        columns = slice(half * FEATURES, (half + 1) * FEATURES)
        kept[:, columns] = own[0] + came[0].astype(f32)
        sent[:, columns] = (own[1] + came[1].astype(f32)).astype(bf16)


def last_body(kept, rest, terms, cross_out, latent_grad, key_grad, value_grad):
    total = (kept[...] + rest[...].astype(f32)).astype(bf16)
    cross_out[...] = total[:, :FEATURES]
    latent_grad[...] = total[:, FEATURES:]
    total = total_of(terms).T
    key_grad[...] = total[:, :FEATURES]
    value_grad[...] = total[:, FEATURES:]


def shards(token_ids, embed_table, latents, w_query, w_key, w_value, w_out, out_grad, offsets):
    mirror_ids = swap(token_ids[SPAN:], "ctx", MIRROR)
    offset_lanes = offsets.reshape(CTX_DEVICES, ROWS)

    row_part = jnp.concatenate([latents, out_grad], axis=0)
    row_part, mirror_ids = lax.optimization_barrier((row_part, mirror_ids))
    row_blocks = [swap(row_part, "tp", r) for r in range(1, TP_DEVICES)]
    ids = jnp.concatenate([token_ids[:SPAN], mirror_ids])
    context_part = embed_table.at[ids].get(mode="promise_in_bounds")
    row_blocks, context_part = lax.optimization_barrier((row_blocks, context_part))
    row_blocks = [row_part] + row_blocks
    context_first = [swap(context_part, "tp", bits) for bits in (1, 3, 4)]

    own = kernel_call(
        rows_body,
        [((2 * ROWS, FEATURES), bf16)],
        [],
        [w_query, w_out] + row_blocks,
        room=60,
    )[0]
    beside, context_first = lax.optimization_barrier((swap(own, "ctx", 2), context_first))
    near, back, side = context_first
    far, side_near, side_back = lax.optimization_barrier(far_blocks(near, back, side))
    side_far = swap(side_back, "tp", 1)
    chips = [jnp.stack([own, beside])]
    chips += [swap(chips[0], "ctx", code) for code in (4, 8, 12)]
    context = [context_part, near, far, back, side, side_near, side_far, side_back]
    begun = resident_call(
        project_body,
        [((2 * SPAN, 2 * FEATURES), f32)],
        [],
        [w_key, w_value] + [context[r] for r in FIRST_PEERS],
    )[0]
    chips, begun = lax.optimization_barrier((chips, begun))
    rows = both_cores(chips)

    part_shape = (CHIPS, FEATURES, ROWS)
    stats_shape = (GROUPS, 4, GROUP_ROWS)
    span_kind = ((2 * SPAN, FEATURES), bf16)
    stored, local, out_blocks = resident_call(
        forward_body,
        [
            (stats_shape, f32),
            ((CTX_DEVICES, FEATURES + LEVEL_ROWS, ROWS), bf16),
        ],
        [offsets],
        [offset_lanes, rows, w_key, w_value, begun, context[LAST_PEER]],
        far_out=[((STORED,) + span_kind[0], bf16)],
        scratch=[
            pltpu.VMEM(*span_kind),
            pltpu.VMEM(*span_kind),
            pltpu.VMEM((FEATURES, 2 * SPAN), bf16),
            pltpu.VMEM((FEATURES, GROUP_ROWS), f32),
            pltpu.SemaphoreType.DMA((2,)),
        ],
        room=24,
    )

    chip = kernel_call(
        join_body,
        [(stats_shape, f32)],
        [],
        [local] + [swap(local, "ctx", code) for code in (1, 2, 3)],
    )[0]
    chips = [chip] + [swap(chip, "ctx", code) for code in (4, 8, 12)]
    out_blocks, chips = lax.optimization_barrier((out_blocks, chips))
    attended_terms = exchange(out_blocks, "ctx")

    both, own_query, other_query = resident_call(
        backward_body,
        [((2 * FEATURES, 2 * SPAN), bf16), (part_shape, f32), (part_shape, bf16)],
        [offsets],
        [offset_lanes, rows] + chips,
        far_in=[stored],
        scratch=[
            pltpu.VMEM(*span_kind),
            pltpu.VMEM(*span_kind),
            pltpu.VMEM(stats_shape, f32),
            pltpu.VMEM((2 * SPAN, FEATURES), f32),
            pltpu.VMEM((2 * SPAN, FEATURES), f32),
            pltpu.VMEM((FEATURES, 2 * SPAN), bf16),
            pltpu.VMEM((GROUPS, FEATURES, GROUP_ROWS), f32),
            pltpu.SemaphoreType.DMA((2,)),
        ],
        room=28,
    )
    query_shape = (FEATURES, ROWS)
    kept, *sent = kernel_call(
        spread_z_body,
        [((2,) + query_shape, f32)] + [((2,) + query_shape, bf16)] * 3,
        [],
        [own_query, swap(other_query, "ctx", 1)],
    )
    both, sent = lax.optimization_barrier((both, sent))
    arriving = [swap(block, "ctx", 4 * code) for code, block in zip((1, 2, 3), sent)]
    block_shape = (CHIPS, 2 * FEATURES, ROWS)
    own_weight, other_weight = resident_call(
        weight_body,
        [(block_shape, f32), (block_shape, bf16)],
        [],
        context + [both],
    )
    own_weight, other_weight, attended_terms, arriving = lax.optimization_barrier(
        (own_weight, other_weight, attended_terms, arriving)
    )
    query_kept, sent = kernel_call(
        spread_y_body,
        [(query_shape, f32), (query_shape, bf16)],
        [],
        [kept] + arriving,
        room=60,
    )
    weight_blocks = kernel_call(
        add_body,
        [(block_shape, bf16)],
        [],
        [own_weight, swap(other_weight, "ctx", 1)],
    )[0]
    query_rest, weight_blocks = lax.optimization_barrier((swap(sent, "ctx", 2), weight_blocks))
    same_core = [list(range(core, CTX_DEVICES, 2)) for core in range(2)]
    weight_terms = exchange(weight_blocks, "ctx", same_core)
    pair_shape = (2, ROWS, FEATURES)
    four_shape = (2,) + pair_shape
    terms = kernel_call(
        close_body,
        [(four_shape, f32), (four_shape, bf16)] * 2,
        [],
        [w_out, w_query, attended_terms, query_kept, query_rest],
    )
    came = [swap(terms[1], "tp", FIRST_X[0]), swap(terms[3], "tp", FIRST_X[1])]
    cross, cross_sent, latent, latent_sent = kernel_call(
        fold_body,
        [(pair_shape, f32), (pair_shape, bf16)] * 2,
        [],
        [terms[0], came[0], terms[2], came[1]],
    )
    came = [swap(cross_sent, "tp", SECOND_X[0]), swap(latent_sent, "tp", SECOND_X[1])]
    sum_shape = (ROWS, 2 * FEATURES)
    kept, sent = kernel_call(
        fold_last_body,
        [(sum_shape, f32), (sum_shape, bf16)],
        [],
        [cross, came[0], latent, came[1]],
    )
    own_shape = (ROWS, FEATURES)
    return tuple(
        kernel_call(
            last_body,
            [(own_shape, bf16), (own_shape, bf16), (own_shape, f32), (own_shape, f32)],
            [],
            [kept, swap(sent, "tp", 4), weight_terms],
        )
    )


def solution(mesh):
    placed = (
        P("ctx"),
        P(None, "tp"),
        P("ctx", "tp"),
        P(None, "tp"),
        P(None, "tp"),
        P(None, "tp"),
        P("tp", None),
        P("ctx", "tp"),
        P(),
    )
    return jax.shard_map(
        shards,
        mesh=mesh,
        in_specs=placed,
        out_specs=(P("ctx", "tp"), P("ctx", "tp"), P("ctx", "tp"), P("ctx", "tp")),
        check_vma=False,
    )
```

```python
import math

import jax
import jax.numpy as jnp
from jax import lax
from jax.experimental import pallas as pl
from jax.experimental.pallas import tpu as pltpu
from jax.sharding import PartitionSpec as P

HEAD_DIM = 128
CTX_DEVICES = 16
TP_DEVICES = 8
FEATURES = 256
HEADS_HERE = FEATURES // HEAD_DIM
ROWS = 128
LAST_PEER = 6
FIRST_PEERS = (0, 1, 2, 3, 4, 5, 7)
CHIPS = CTX_DEVICES // 2
GROUPS = 4
STORED = 120
FIRST_X, SECOND_X = (1, 3), (3, 1)
KEPT_PEERS = ((0, 3), (0, 1))
SENT_PEERS = ((1, 2), (3, 2))
MIRROR = 12
LEVEL_ROWS = 16
GROUP_ROWS = 4 * ROWS
SPAN = 512

SCORE_SCALE = 1.0 / math.sqrt(HEAD_DIM)
LOG2_SCALE = SCORE_SCALE * math.log2(math.e)
MASKED = -1e30
FLOOR = -1e29

NN = (((1,), (0,)), ((), ()))
NT = (((1,), (1,)), ((), ()))
TN = (((0,), (0,)), ((), ()))

bf16 = jnp.bfloat16
f32 = jnp.float32


def mm(left, right, dims=NN):
    return lax.dot_general(left, right, dims, preferred_element_type=f32)


def swap(value, axis, bits):
    count = CTX_DEVICES if axis == "ctx" else TP_DEVICES
    return lax.ppermute(value, axis, [(i, i ^ bits) for i in range(count)])


def exchange(value, axis, groups=None):
    return lax.all_to_all(value, axis, 0, 0, axis_index_groups=groups, tiled=True)


def whole(shape):
    return pl.BlockSpec(shape, lambda i: (0,) * len(shape), pipeline_mode=pl.Buffered(1))


def kernel_call(body, outs, scalars, arrays, room=16):
    call = pl.pallas_call(
        body,
        grid=(1,),
        out_shape=[jax.ShapeDtypeStruct(shape, kind) for shape, kind in outs],
        in_specs=[pl.BlockSpec(memory_space=pltpu.SMEM)] * len(scalars)
        + [whole(a.shape) for a in arrays],
        out_specs=[whole(shape) for shape, _ in outs],
        compiler_params=pltpu.CompilerParams(vmem_limit_bytes=room * 1024 * 1024),
        cost_estimate=pl.CostEstimate(flops=0, bytes_accessed=0, transcendentals=0),
    )
    return list(call(*scalars, *arrays))


def resident_call(body, outs, scalars, arrays, far_in=(), far_out=(), scratch=(), room=16, flops=0):
    near, far = pl.BlockSpec(memory_space=pltpu.VMEM), pl.BlockSpec(memory_space=pltpu.HBM)
    call = pl.pallas_call(
        body,
        out_shape=[jax.ShapeDtypeStruct(shape, kind) for shape, kind in [*far_out, *outs]],
        in_specs=[pl.BlockSpec(memory_space=pltpu.SMEM)] * len(scalars)
        + [far] * len(far_in)
        + [near] * len(arrays),
        out_specs=[far] * len(far_out) + [near] * len(outs),
        scratch_shapes=list(scratch),
        compiler_params=pltpu.CompilerParams(vmem_limit_bytes=room * 1024 * 1024),
        cost_estimate=pl.CostEstimate(flops=flops, bytes_accessed=0, transcendentals=0),
    )
    return list(call(*scalars, *far_in, *arrays))


def far_blocks(near, back, side):
    return swap(back, "tp", 1), swap(near, "tp", 4), swap(side, "tp", 3)


def both_cores(chips):
    return jnp.concatenate(chips + [swap(pair, "ctx", 1) for pair in chips], axis=0)


def shard_start(tp_index, r):
    return pl.multiple_of((tp_index ^ r) * FEATURES, FEATURES)


def tp_place():
    return lax.axis_index("tp").astype(jnp.int32)


def ctx_place():
    return lax.axis_index("ctx").astype(jnp.int32)


def key_bases(ctx_index):
    return ctx_index * (2 * SPAN), (ctx_index ^ MIRROR) * (2 * SPAN) + SPAN


def head_of(h):
    return slice(h * HEAD_DIM, (h + 1) * HEAD_DIM)


def rows_body(w_query, w_out, *refs):
    blocks, out = refs[:-1], refs[-1]
    query = jnp.zeros((ROWS, FEATURES), f32)
    grads = [jnp.zeros((HEAD_DIM, ROWS), f32) for _ in range(HEADS_HERE)]
    for r in range(TP_DEVICES):
        part = pl.ds(shard_start(tp_place(), r), FEATURES)
        query += mm(blocks[r][:ROWS, :], w_query[part, :])
        for h in range(HEADS_HERE):
            grads[h] += mm(w_out[head_of(h), part], blocks[r][ROWS:, :], NT)
    out[:ROWS, :] = query.astype(bf16)
    for h in range(HEADS_HERE):
        out[ROWS:, head_of(h)] = grads[h].astype(bf16)


def row_block(rows, ctx_index, block):
    distance = ctx_index ^ block
    return rows.at[(distance & 1) * CHIPS + (distance >> 1)]


def group_query(rows, ctx_index, group, h):
    blocks = [row_block(rows, ctx_index, GROUPS * group + i) for i in range(GROUPS)]
    return jnp.concatenate([block[:ROWS, head_of(h)] for block in blocks], axis=0)


def group_grad(rows, ctx_index, group, h):
    blocks = [row_block(rows, ctx_index, GROUPS * group + i) for i in range(GROUPS)]
    return jnp.concatenate([block[ROWS:, head_of(h)] for block in blocks], axis=1)


def masked(scores, base, offset_row):
    if offset_row is None:
        return scores
    places = base + lax.broadcasted_iota(jnp.int32, (SPAN, GROUP_ROWS), 0)
    return jnp.where(places <= offset_row, scores, MASKED)


def visit(bounds, base, offsets, group, block):
    first, last = bounds[group * GROUP_ROWS], bounds[group * GROUP_ROWS + GROUP_ROWS - 1]
    whole_seen = first >= base + (SPAN - 1)

    @pl.when(whole_seen)
    def _():
        block(None)

    @pl.when(jnp.logical_and(last >= base, jnp.logical_not(whole_seen)))
    def _():
        lanes = [offsets[pl.ds(group * GROUPS + i, 1), :] for i in range(GROUPS)]
        block(jnp.concatenate(lanes, axis=1))


def pieces_of(level):
    pieces = []
    for _ in range(3):
        piece = level.astype(bf16).astype(f32)
        pieces.append(piece)
        level = level - piece
    return pieces


def turned(value):
    return value.astype(f32).T.astype(bf16)


def span_of(i):
    return slice(i * SPAN, (i + 1) * SPAN)


def ordered_rows(weight, tp_index, order):
    return jnp.concatenate(
        [weight[pl.ds(shard_start(tp_index, r), FEATURES), :] for r in order], axis=0
    )


def project_body(w_key, w_value, *refs):
    context = jnp.concatenate([ref[...] for ref in refs[:-1]], axis=1)
    out = refs[-1]
    out[:, :FEATURES] = mm(context, ordered_rows(w_key, tp_place(), FIRST_PEERS))
    out[:, FEATURES:] = mm(context, ordered_rows(w_value, tp_place(), FIRST_PEERS))


def forward_body(bounds, *refs):
    offsets, rows, w_key, w_value, begun, last, stored = refs[:7]
    stats, blocks, keys, values, values_t, parts, copied = refs[7:]
    ctx_index = ctx_place()
    bases = key_bases(ctx_index)
    start = shard_start(tp_place(), LAST_PEER)
    for i, (weight, out) in enumerate(((w_key, keys), (w_value, values))):
        rest = mm(last[...], weight[pl.ds(start, FEATURES), :])
        out[...] = (begun[:, i * FEATURES : (i + 1) * FEATURES] + rest).astype(bf16)
    copies = [
        pltpu.make_async_copy(keys, stored.at[0], copied.at[0]),
        pltpu.make_async_copy(values, stored.at[1], copied.at[1]),
    ]
    for copy in copies:
        copy.start()
    for h in range(HEADS_HERE):
        values_t[head_of(h), :] = turned(values[:, head_of(h)])

    def step(group, carry):
        stats[group, :2, :] = jnp.full((2, GROUP_ROWS), MASKED, f32)
        stats[group, 2:, :] = jnp.zeros((2, GROUP_ROWS), f32)
        parts[...] = jnp.zeros((FEATURES, GROUP_ROWS), f32)
        for i in range(2):
            base = bases[i]

            def block(offset_row, i=i, base=base):
                for h in range(HEADS_HERE):
                    query = group_query(rows, ctx_index, group, h)
                    scores = mm(keys[span_of(i), head_of(h)], query, NT) * LOG2_SCALE
                    scores = masked(scores, base, offset_row)
                    old = stats[group, h : h + 1, :]
                    peak = jnp.maximum(jnp.max(scores, axis=0, keepdims=True), FLOOR)
                    peak = jnp.maximum(peak, old)
                    weights = jnp.exp2(scores - peak)
                    keep = jnp.exp2(old - peak)
                    total = keep * stats[group, h + 2 : h + 3, :]
                    total += jnp.sum(weights, axis=0, keepdims=True)
                    part = mm(values_t[head_of(h), span_of(i)], weights.astype(bf16))
                    parts[head_of(h), :] = keep * parts[head_of(h), :] + part
                    stats[group, h : h + 1, :] = peak
                    stats[group, h + 2 : h + 3, :] = total

            visit(bounds, base, offsets, group, block)

        levels = []
        for h in range(HEADS_HERE):
            total = stats[group, h + 2 : h + 3, :]
            some = total > 0.0
            safe = jnp.where(some, total, 1.0)
            part = parts[head_of(h), :] * jnp.where(some, 1.0 / safe, 0.0)
            grad_t = group_grad(rows, ctx_index, group, h).astype(f32)
            level = jnp.where(some, stats[group, h : h + 1, :] + jnp.log2(safe), MASKED)
            stats[group, h : h + 1, :] = level
            stats[group, h + 2 : h + 3, :] = jnp.sum(part * grad_t, axis=0, keepdims=True)
            levels += pieces_of(level)
            for i in range(GROUPS):
                place = GROUPS * group + i
                lanes = slice(i * ROWS, (i + 1) * ROWS)
                blocks[place, head_of(h), :] = part[:, lanes].astype(bf16)
        levels.append(jnp.zeros((LEVEL_ROWS - len(levels), GROUP_ROWS), f32))
        levels = jnp.concatenate(levels, axis=0).astype(bf16)
        for i in range(GROUPS):
            place = GROUPS * group + i
            blocks[place, FEATURES:, :] = levels[:, i * ROWS : (i + 1) * ROWS]
        return carry

    lax.fori_loop(0, GROUPS, step, 0)
    for copy in copies:
        copy.wait()


def joined(refs, group):
    pieces = [ref[group] for ref in refs]
    top = pieces[0][:2]
    for piece in pieces[1:]:
        top = jnp.maximum(top, piece[:2])
    total = jnp.zeros((2, GROUP_ROWS), f32)
    delta = jnp.zeros((2, GROUP_ROWS), f32)
    for piece in pieces:
        weight = jnp.exp2(piece[:2] - top)
        total += weight
        delta += weight * piece[2:]
    return top + jnp.log2(total), delta / total


def join_body(own, one, two, three, stats):
    for group in range(GROUPS):
        level, delta = joined((own, one, two, three), group)
        stats[group, :2, :] = level
        stats[group, 2:, :] = delta


def split_parity(core, group, value, mine, other):
    for i in range(GROUPS // 2):
        low = value[:, 2 * i * ROWS : (2 * i + 1) * ROWS]
        high = value[:, (2 * i + 1) * ROWS : (2 * i + 2) * ROWS]
        chip = group * (GROUPS // 2) + i
        mine[chip] = jnp.where(core == 1, high, low)
        other[chip] = jnp.where(core == 1, low, high).astype(bf16)


def query_body(bounds, *refs):
    stored, offsets, rows, own, one, two, three, saved, mine, other = refs[:10]
    keys, values, stats, keys_t, query_acc, copied = refs[10:]
    copies = [
        pltpu.make_async_copy(stored.at[0], keys, copied.at[0]),
        pltpu.make_async_copy(stored.at[1], values, copied.at[1]),
    ]
    for copy in copies:
        copy.start()
    ctx_index = ctx_place()
    bases = key_bases(ctx_index)
    query_acc[...] = jnp.zeros(query_acc.shape, f32)
    for group in range(GROUPS):
        level, delta = joined((own, one, two, three), group)
        stats[group, :2, :] = level
        stats[group, 2:, :] = delta
    for copy in copies:
        copy.wait()
    for h in range(HEADS_HERE):
        keys_t[head_of(h), :] = turned(keys[:, head_of(h)])

    def step(group, carry):
        for i in range(2):
            span = span_of(i)

            def block(offset_row, i=i, span=span):
                for h in range(HEADS_HERE):
                    query = group_query(rows, ctx_index, group, h)
                    grad_t = group_grad(rows, ctx_index, group, h)
                    scores = mm(keys[span, head_of(h)], query, NT) * LOG2_SCALE
                    scores = masked(scores - stats[group, h : h + 1, :], bases[i], offset_row)
                    probs = jnp.exp2(scores)
                    prob_grad = mm(values[span, head_of(h)], grad_t)
                    delta = stats[group, h + 2 : h + 3, :]
                    score_grad = (probs * (prob_grad - delta) * SCORE_SCALE).astype(bf16)
                    saved[group, i, h, 0] = probs.astype(bf16)
                    saved[group, i, h, 1] = score_grad
                    query_acc[group, head_of(h), :] += mm(keys_t[head_of(h), span], score_grad)

            visit(bounds, bases[i], offsets, group, block)

        return carry

    lax.fori_loop(0, GROUPS, step, 0)
    for group in range(GROUPS):
        split_parity(ctx_index & 1, group, query_acc[group], mine, other)


def weight_body(bounds, *refs):
    context, refs = refs[:TP_DEVICES], refs[TP_DEVICES:]
    rows, saved, mine, other, key_acc, value_acc, both = refs
    ctx_index = ctx_place()
    bases = key_bases(ctx_index)
    key_acc[...] = jnp.zeros(key_acc.shape, f32)
    value_acc[...] = jnp.zeros(value_acc.shape, f32)

    def step(group, carry):
        for i in range(2):
            span = span_of(i)

            @pl.when(bounds[group * GROUP_ROWS + GROUP_ROWS - 1] >= bases[i])
            def _():
                for h in range(HEADS_HERE):
                    query = group_query(rows, ctx_index, group, h)
                    grad_t = group_grad(rows, ctx_index, group, h)
                    value_acc[span, head_of(h)] += mm(saved[group, i, h, 0], grad_t, NT)
                    key_acc[span, head_of(h)] += mm(saved[group, i, h, 1], query)

        return carry

    lax.fori_loop(0, GROUPS, step, 0)
    both[:FEATURES, :] = turned(key_acc[...])
    both[FEATURES:, :] = turned(value_acc[...])
    flipped = (ctx_index & 1) == 1
    for r in range(TP_DEVICES):
        terms = mm(both[...], context[r][...])
        place = tp_place() ^ r
        low, high = terms[:, :ROWS], terms[:, ROWS:]
        mine[place] = jnp.where(flipped, high, low)
        other[place] = jnp.where(flipped, low, high).astype(bf16)


def add_body(own, received, out):
    out[...] = (own[...] + received[...].astype(f32)).astype(bf16)


def spread_z_body(own, received, kept, one, two, three):
    z = ctx_place() >> 2
    for y in range(2):
        place = 2 * z + y
        kept[y] = own[place] + received[place].astype(f32)
        for code, out in ((1, one), (2, two), (3, three)):
            place = 2 * (z ^ code) + y
            out[y] = (own[place] + received[place].astype(f32)).astype(bf16)


def spread_y_body(own, one, two, three, kept, sent):
    y = (ctx_place() >> 1) & 1
    for place, out in ((y, kept), (1 - y, sent)):
        total = own[place]
        for term in (one, two, three):
            total += term[place].astype(f32)
        out[...] = total.astype(out.dtype)


def weighted_sum(blocks):
    heads = []
    for h in range(HEADS_HERE):
        levels = []
        for i in range(CTX_DEVICES):
            pieces = blocks[i, FEATURES:, :].astype(f32)[3 * h : 3 * h + 3]
            levels.append(pieces[0:1] + pieces[1:2] + pieces[2:3])
        top = levels[0]
        for level in levels[1:]:
            top = jnp.maximum(top, level)
        weights = [jnp.exp2(level - top) for level in levels]
        scale = 1.0 / sum(weights)
        total = jnp.zeros((HEAD_DIM, ROWS), f32)
        for i in range(CTX_DEVICES):
            total += weights[i] * blocks[i, head_of(h), :].astype(f32)
        heads.append(total * scale)
    return jnp.concatenate(heads, axis=0)


def total_of(terms):
    total = terms[0].astype(f32)
    for i in range(1, terms.shape[0]):
        total = total + terms[i].astype(f32)
    return total


def close_body(w_out, w_query, attended_terms, query_kept, query_rest, *outs):
    attended = weighted_sum(attended_terms).T.astype(bf16)
    query_grad = (query_kept[...] + query_rest[...].astype(f32)).T.astype(bf16)
    for y in range(2):
        for x in range(4):
            part = pl.ds(shard_start(tp_place(), 4 * y + x), FEATURES)
            cross = mm(attended, w_out[:, part])
            latent = mm(query_grad, w_query[part, :], NT)
            for half, terms in ((0, cross), (1, latent)):
                stays = KEPT_PEERS[half]
                out = outs[2 * half + (x not in stays)]
                place = (stays if x in stays else SENT_PEERS[half]).index(x)
                out[place, y] = terms.astype(out.dtype)


def fold_body(*refs):
    for half in range(2):
        stays, came = refs[2 * half : 2 * half + 2]
        kept, sent = refs[4 + 2 * half : 6 + 2 * half]
        kept[...] = stays[0] + came[0].astype(f32)
        sent[...] = (stays[1] + came[1].astype(f32)).astype(bf16)


def fold_last_body(cross, cross_came, latent, latent_came, kept, sent):
    for half, (own, came) in enumerate(((cross, cross_came), (latent, latent_came))):
        columns = slice(half * FEATURES, (half + 1) * FEATURES)
        kept[:, columns] = own[0] + came[0].astype(f32)
        sent[:, columns] = (own[1] + came[1].astype(f32)).astype(bf16)


def last_body(kept, rest, terms, cross_out, latent_grad, key_grad, value_grad):
    total = (kept[...] + rest[...].astype(f32)).astype(bf16)
    cross_out[...] = total[:, :FEATURES]
    latent_grad[...] = total[:, FEATURES:]
    total = total_of(terms).T
    key_grad[...] = total[:, :FEATURES]
    value_grad[...] = total[:, FEATURES:]


def shards(token_ids, embed_table, latents, w_query, w_key, w_value, w_out, out_grad, offsets):
    mirror_ids = swap(token_ids[SPAN:], "ctx", MIRROR)
    offset_lanes = offsets.reshape(CTX_DEVICES, ROWS)

    row_part = jnp.concatenate([latents, out_grad], axis=0)
    row_part, mirror_ids = lax.optimization_barrier((row_part, mirror_ids))
    row_blocks = [swap(row_part, "tp", r) for r in range(1, TP_DEVICES)]
    ids = jnp.concatenate([token_ids[:SPAN], mirror_ids])
    context_part = embed_table.at[ids].get(mode="promise_in_bounds")
    row_blocks, context_part = lax.optimization_barrier((row_blocks, context_part))
    row_blocks = [row_part] + row_blocks
    context_first = [swap(context_part, "tp", bits) for bits in (1, 3, 4)]

    own = kernel_call(
        rows_body,
        [((2 * ROWS, FEATURES), bf16)],
        [],
        [w_query, w_out] + row_blocks,
        room=60,
    )[0]
    beside, context_first = lax.optimization_barrier((swap(own, "ctx", 2), context_first))
    near, back, side = context_first
    far, side_near, side_back = lax.optimization_barrier(far_blocks(near, back, side))
    side_far = swap(side_back, "tp", 1)
    chips = [jnp.stack([own, beside])]
    chips += [swap(chips[0], "ctx", code) for code in (4, 8, 12)]
    context = [context_part, near, far, back, side, side_near, side_far, side_back]
    begun = resident_call(
        project_body,
        [((2 * SPAN, 2 * FEATURES), f32)],
        [],
        [w_key, w_value] + [context[r] for r in FIRST_PEERS],
    )[0]
    chips, begun = lax.optimization_barrier((chips, begun))
    rows = both_cores(chips)

    part_shape = (CHIPS, FEATURES, ROWS)
    stats_shape = (GROUPS, 4, GROUP_ROWS)
    span_kind = ((2 * SPAN, FEATURES), bf16)
    stored, local, out_blocks = resident_call(
        forward_body,
        [
            (stats_shape, f32),
            ((CTX_DEVICES, FEATURES + LEVEL_ROWS, ROWS), bf16),
        ],
        [offsets],
        [offset_lanes, rows, w_key, w_value, begun, context[LAST_PEER]],
        far_out=[((STORED,) + span_kind[0], bf16)],
        scratch=[
            pltpu.VMEM(*span_kind),
            pltpu.VMEM(*span_kind),
            pltpu.VMEM((FEATURES, 2 * SPAN), bf16),
            pltpu.VMEM((FEATURES, GROUP_ROWS), f32),
            pltpu.SemaphoreType.DMA((2,)),
        ],
        room=24,
    )

    chip = kernel_call(
        join_body,
        [(stats_shape, f32)],
        [],
        [local] + [swap(local, "ctx", code) for code in (1, 2, 3)],
    )[0]
    chips = [chip] + [swap(chip, "ctx", code) for code in (4, 8, 12)]
    out_blocks, chips = lax.optimization_barrier((out_blocks, chips))
    attended_terms = exchange(out_blocks, "ctx")

    saved, own_query, other_query = resident_call(
        query_body,
        [
            ((GROUPS, 2, HEADS_HERE, 2, SPAN, GROUP_ROWS), bf16),
            (part_shape, f32),
            (part_shape, bf16),
        ],
        [offsets],
        [offset_lanes, rows] + chips,
        far_in=[stored],
        scratch=[
            pltpu.VMEM(*span_kind),
            pltpu.VMEM(*span_kind),
            pltpu.VMEM(stats_shape, f32),
            pltpu.VMEM((FEATURES, 2 * SPAN), bf16),
            pltpu.VMEM((GROUPS, FEATURES, GROUP_ROWS), f32),
            pltpu.SemaphoreType.DMA((2,)),
        ],
        room=24,
    )
    query_shape = (FEATURES, ROWS)
    kept, *sent = kernel_call(
        spread_z_body,
        [((2,) + query_shape, f32)] + [((2,) + query_shape, bf16)] * 3,
        [],
        [own_query, swap(other_query, "ctx", 1)],
    )
    saved, sent = lax.optimization_barrier((saved, sent))
    arriving = [swap(block, "ctx", 4 * code) for code, block in zip((1, 2, 3), sent)]
    block_shape = (CHIPS, 2 * FEATURES, ROWS)
    own_weight, other_weight = resident_call(
        weight_body,
        [(block_shape, f32), (block_shape, bf16)],
        [offsets],
        context + [rows, saved],
        scratch=[
            pltpu.VMEM((2 * SPAN, FEATURES), f32),
            pltpu.VMEM((2 * SPAN, FEATURES), f32),
            pltpu.VMEM((2 * FEATURES, 2 * SPAN), bf16),
        ],
        room=20,
    )
    own_weight, other_weight, attended_terms, arriving = lax.optimization_barrier(
        (own_weight, other_weight, attended_terms, arriving)
    )
    query_kept, sent = kernel_call(
        spread_y_body,
        [(query_shape, f32), (query_shape, bf16)],
        [],
        [kept] + arriving,
        room=60,
    )
    weight_blocks = kernel_call(
        add_body,
        [(block_shape, bf16)],
        [],
        [own_weight, swap(other_weight, "ctx", 1)],
    )[0]
    query_rest, weight_blocks = lax.optimization_barrier((swap(sent, "ctx", 2), weight_blocks))
    same_core = [list(range(core, CTX_DEVICES, 2)) for core in range(2)]
    weight_terms = exchange(weight_blocks, "ctx", same_core)
    pair_shape = (2, ROWS, FEATURES)
    four_shape = (2,) + pair_shape
    terms = kernel_call(
        close_body,
        [(four_shape, f32), (four_shape, bf16)] * 2,
        [],
        [w_out, w_query, attended_terms, query_kept, query_rest],
    )
    came = [swap(terms[1], "tp", FIRST_X[0]), swap(terms[3], "tp", FIRST_X[1])]
    cross, cross_sent, latent, latent_sent = kernel_call(
        fold_body,
        [(pair_shape, f32), (pair_shape, bf16)] * 2,
        [],
        [terms[0], came[0], terms[2], came[1]],
    )
    came = [swap(cross_sent, "tp", SECOND_X[0]), swap(latent_sent, "tp", SECOND_X[1])]
    sum_shape = (ROWS, 2 * FEATURES)
    kept, sent = kernel_call(
        fold_last_body,
        [(sum_shape, f32), (sum_shape, bf16)],
        [],
        [cross, came[0], latent, came[1]],
    )
    own_shape = (ROWS, FEATURES)
    return tuple(
        kernel_call(
            last_body,
            [(own_shape, bf16), (own_shape, bf16), (own_shape, f32), (own_shape, f32)],
            [],
            [kept, swap(sent, "tp", 4), weight_terms],
        )
    )


def solution(mesh):
    placed = (
        P("ctx"),
        P(None, "tp"),
        P("ctx", "tp"),
        P(None, "tp"),
        P(None, "tp"),
        P(None, "tp"),
        P("tp", None),
        P("ctx", "tp"),
        P(),
    )
    return jax.shard_map(
        shards,
        mesh=mesh,
        in_specs=placed,
        out_specs=(P("ctx", "tp"), P("ctx", "tp"), P("ctx", "tp"), P("ctx", "tp")),
        check_vma=False,
    )
```

```python
import math

import jax
import jax.numpy as jnp
from jax import lax
from jax.experimental import pallas as pl
from jax.experimental.pallas import tpu as pltpu
from jax.sharding import PartitionSpec as P

HEAD_DIM = 128
CTX_DEVICES = 16
TP_DEVICES = 8
FEATURES = 256
HEADS_HERE = FEATURES // HEAD_DIM
ROWS = 128
LAST_PEER = 6
FIRST_PEERS = (0, 1, 2, 3, 4, 5, 7)
CHIPS = CTX_DEVICES // 2
GROUPS = 4
STORED = 120
FIRST_X, SECOND_X = (1, 3), (3, 1)
KEPT_PEERS = ((0, 3), (0, 1))
SENT_PEERS = ((1, 2), (3, 2))
MIRROR = 12
LEVEL_ROWS = 16
GROUP_ROWS = 4 * ROWS
SPAN = 512

SCORE_SCALE = 1.0 / math.sqrt(HEAD_DIM)
LOG2_SCALE = SCORE_SCALE * math.log2(math.e)
MASKED = -1e30
FLOOR = -1e29

NN = (((1,), (0,)), ((), ()))
NT = (((1,), (1,)), ((), ()))
TN = (((0,), (0,)), ((), ()))

bf16 = jnp.bfloat16
f32 = jnp.float32


def mm(left, right, dims=NN):
    return lax.dot_general(left, right, dims, preferred_element_type=f32)


def swap(value, axis, bits):
    count = CTX_DEVICES if axis == "ctx" else TP_DEVICES
    return lax.ppermute(value, axis, [(i, i ^ bits) for i in range(count)])


def exchange(value, axis, groups=None):
    return lax.all_to_all(value, axis, 0, 0, axis_index_groups=groups, tiled=True)


def whole(shape):
    return pl.BlockSpec(shape, lambda i: (0,) * len(shape), pipeline_mode=pl.Buffered(1))


def kernel_call(body, outs, scalars, arrays, room=16):
    call = pl.pallas_call(
        body,
        grid=(1,),
        out_shape=[jax.ShapeDtypeStruct(shape, kind) for shape, kind in outs],
        in_specs=[pl.BlockSpec(memory_space=pltpu.SMEM)] * len(scalars)
        + [whole(a.shape) for a in arrays],
        out_specs=[whole(shape) for shape, _ in outs],
        compiler_params=pltpu.CompilerParams(vmem_limit_bytes=room * 1024 * 1024),
        cost_estimate=pl.CostEstimate(flops=0, bytes_accessed=0, transcendentals=0),
    )
    return list(call(*scalars, *arrays))


def resident_call(body, outs, scalars, arrays, far_in=(), far_out=(), scratch=(), room=16, flops=0):
    near, far = pl.BlockSpec(memory_space=pltpu.VMEM), pl.BlockSpec(memory_space=pltpu.HBM)
    call = pl.pallas_call(
        body,
        out_shape=[jax.ShapeDtypeStruct(shape, kind) for shape, kind in [*far_out, *outs]],
        in_specs=[pl.BlockSpec(memory_space=pltpu.SMEM)] * len(scalars)
        + [far] * len(far_in)
        + [near] * len(arrays),
        out_specs=[far] * len(far_out) + [near] * len(outs),
        scratch_shapes=list(scratch),
        compiler_params=pltpu.CompilerParams(vmem_limit_bytes=room * 1024 * 1024),
        cost_estimate=pl.CostEstimate(flops=flops, bytes_accessed=0, transcendentals=0),
    )
    return list(call(*scalars, *far_in, *arrays))


def far_blocks(near, back, side):
    return swap(back, "tp", 1), swap(near, "tp", 4), swap(side, "tp", 3)


def both_cores(chips):
    return jnp.concatenate(chips + [swap(pair, "ctx", 1) for pair in chips], axis=0)


def shard_start(tp_index, r):
    return pl.multiple_of((tp_index ^ r) * FEATURES, FEATURES)


def tp_place():
    return lax.axis_index("tp").astype(jnp.int32)


def ctx_place():
    return lax.axis_index("ctx").astype(jnp.int32)


def key_bases(ctx_index):
    return ctx_index * (2 * SPAN), (ctx_index ^ MIRROR) * (2 * SPAN) + SPAN


def head_of(h):
    return slice(h * HEAD_DIM, (h + 1) * HEAD_DIM)


def rows_body(w_query, w_out, *refs):
    blocks, out = refs[:-1], refs[-1]
    query = jnp.zeros((ROWS, FEATURES), f32)
    grads = [jnp.zeros((HEAD_DIM, ROWS), f32) for _ in range(HEADS_HERE)]
    for r in range(TP_DEVICES):
        part = pl.ds(shard_start(tp_place(), r), FEATURES)
        query += mm(blocks[r][:ROWS, :], w_query[part, :])
        for h in range(HEADS_HERE):
            grads[h] += mm(w_out[head_of(h), part], blocks[r][ROWS:, :], NT)
    out[:ROWS, :] = query.astype(bf16)
    for h in range(HEADS_HERE):
        out[ROWS:, head_of(h)] = grads[h].astype(bf16)


def row_block(rows, ctx_index, block):
    distance = ctx_index ^ block
    return rows.at[(distance & 1) * CHIPS + (distance >> 1)]


def group_query(rows, ctx_index, group, h):
    blocks = [row_block(rows, ctx_index, GROUPS * group + i) for i in range(GROUPS)]
    return jnp.concatenate([block[:ROWS, head_of(h)] for block in blocks], axis=0)


def group_grad(rows, ctx_index, group, h):
    blocks = [row_block(rows, ctx_index, GROUPS * group + i) for i in range(GROUPS)]
    return jnp.concatenate([block[ROWS:, head_of(h)] for block in blocks], axis=1)


def masked(scores, base, offset_row):
    if offset_row is None:
        return scores
    places = base + lax.broadcasted_iota(jnp.int32, (SPAN, GROUP_ROWS), 0)
    return jnp.where(places <= offset_row, scores, MASKED)


def visit(bounds, base, offsets, group, block):
    first, last = bounds[group * GROUP_ROWS], bounds[group * GROUP_ROWS + GROUP_ROWS - 1]
    whole_seen = first >= base + (SPAN - 1)

    @pl.when(whole_seen)
    def _():
        block(None)

    @pl.when(jnp.logical_and(last >= base, jnp.logical_not(whole_seen)))
    def _():
        lanes = [offsets[pl.ds(group * GROUPS + i, 1), :] for i in range(GROUPS)]
        block(jnp.concatenate(lanes, axis=1))


def pieces_of(level):
    pieces = []
    for _ in range(3):
        piece = level.astype(bf16).astype(f32)
        pieces.append(piece)
        level = level - piece
    return pieces


def turned(value):
    return value.astype(f32).T.astype(bf16)


def span_of(i):
    return slice(i * SPAN, (i + 1) * SPAN)


def ordered_rows(weight, tp_index, order):
    return jnp.concatenate(
        [weight[pl.ds(shard_start(tp_index, r), FEATURES), :] for r in order], axis=0
    )


def project_body(w_key, w_value, *refs):
    context = jnp.concatenate([ref[...] for ref in refs[:-1]], axis=1)
    out = refs[-1]
    out[:, :FEATURES] = mm(context, ordered_rows(w_key, tp_place(), FIRST_PEERS))
    out[:, FEATURES:] = mm(context, ordered_rows(w_value, tp_place(), FIRST_PEERS))


def forward_body(bounds, *refs):
    offsets, rows, w_key, w_value, begun, last, stored = refs[:7]
    stats, blocks, keys, values, values_t, parts, copied = refs[7:]
    ctx_index = ctx_place()
    bases = key_bases(ctx_index)
    start = shard_start(tp_place(), LAST_PEER)
    for i, (weight, out) in enumerate(((w_key, keys), (w_value, values))):
        rest = mm(last[...], weight[pl.ds(start, FEATURES), :])
        out[...] = (begun[:, i * FEATURES : (i + 1) * FEATURES] + rest).astype(bf16)
    copies = [
        pltpu.make_async_copy(keys, stored.at[0], copied.at[0]),
        pltpu.make_async_copy(values, stored.at[1], copied.at[1]),
    ]
    for copy in copies:
        copy.start()
    for h in range(HEADS_HERE):
        values_t[head_of(h), :] = turned(values[:, head_of(h)])

    def step(group, carry):
        stats[group, :2, :] = jnp.full((2, GROUP_ROWS), MASKED, f32)
        stats[group, 2:, :] = jnp.zeros((2, GROUP_ROWS), f32)
        parts[...] = jnp.zeros((FEATURES, GROUP_ROWS), f32)
        for i in range(2):
            base = bases[i]

            def block(offset_row, i=i, base=base):
                for h in range(HEADS_HERE):
                    query = group_query(rows, ctx_index, group, h)
                    scores = mm(keys[span_of(i), head_of(h)], query, NT) * LOG2_SCALE
                    scores = masked(scores, base, offset_row)
                    old = stats[group, h : h + 1, :]
                    peak = jnp.maximum(jnp.max(scores, axis=0, keepdims=True), FLOOR)
                    peak = jnp.maximum(peak, old)
                    weights = jnp.exp2(scores - peak)
                    keep = jnp.exp2(old - peak)
                    total = keep * stats[group, h + 2 : h + 3, :]
                    total += jnp.sum(weights, axis=0, keepdims=True)
                    part = mm(values_t[head_of(h), span_of(i)], weights.astype(bf16))
                    parts[head_of(h), :] = keep * parts[head_of(h), :] + part
                    stats[group, h : h + 1, :] = peak
                    stats[group, h + 2 : h + 3, :] = total

            visit(bounds, base, offsets, group, block)

        levels = []
        for h in range(HEADS_HERE):
            total = stats[group, h + 2 : h + 3, :]
            some = total > 0.0
            safe = jnp.where(some, total, 1.0)
            part = parts[head_of(h), :] * jnp.where(some, 1.0 / safe, 0.0)
            grad_t = group_grad(rows, ctx_index, group, h).astype(f32)
            level = jnp.where(some, stats[group, h : h + 1, :] + jnp.log2(safe), MASKED)
            stats[group, h : h + 1, :] = level
            stats[group, h + 2 : h + 3, :] = jnp.sum(part * grad_t, axis=0, keepdims=True)
            levels += pieces_of(level)
            for i in range(GROUPS):
                place = GROUPS * group + i
                lanes = slice(i * ROWS, (i + 1) * ROWS)
                blocks[place, head_of(h), :] = part[:, lanes].astype(bf16)
        levels.append(jnp.zeros((LEVEL_ROWS - len(levels), GROUP_ROWS), f32))
        levels = jnp.concatenate(levels, axis=0).astype(bf16)
        for i in range(GROUPS):
            place = GROUPS * group + i
            blocks[place, FEATURES:, :] = levels[:, i * ROWS : (i + 1) * ROWS]
        return carry

    lax.fori_loop(0, GROUPS, step, 0)
    for copy in copies:
        copy.wait()


def joined(refs, group):
    pieces = [ref[group] for ref in refs]
    top = pieces[0][:2]
    for piece in pieces[1:]:
        top = jnp.maximum(top, piece[:2])
    total = jnp.zeros((2, GROUP_ROWS), f32)
    delta = jnp.zeros((2, GROUP_ROWS), f32)
    for piece in pieces:
        weight = jnp.exp2(piece[:2] - top)
        total += weight
        delta += weight * piece[2:]
    return top + jnp.log2(total), delta / total


def join_body(own, one, two, three, stats):
    for group in range(GROUPS):
        level, delta = joined((own, one, two, three), group)
        stats[group, :2, :] = level
        stats[group, 2:, :] = delta


def split_parity(core, group, value, mine, other):
    for i in range(GROUPS // 2):
        low = value[:, 2 * i * ROWS : (2 * i + 1) * ROWS]
        high = value[:, (2 * i + 1) * ROWS : (2 * i + 2) * ROWS]
        chip = group * (GROUPS // 2) + i
        mine[chip] = jnp.where(core == 1, high, low)
        other[chip] = jnp.where(core == 1, low, high).astype(bf16)


def backward_body(bounds, *refs):
    stored, offsets, rows, own, one, two, three, both, mine, other = refs[:10]
    keys, values, stats, key_acc, value_acc, keys_t, query_acc, copied = refs[10:]
    copies = [
        pltpu.make_async_copy(stored.at[0], keys, copied.at[0]),
        pltpu.make_async_copy(stored.at[1], values, copied.at[1]),
    ]
    for copy in copies:
        copy.start()
    for group in range(GROUPS):
        level, delta = joined((own, one, two, three), group)
        stats[group, :2, :] = level
        stats[group, 2:, :] = delta
    ctx_index = ctx_place()
    bases = key_bases(ctx_index)
    query_acc[...] = jnp.zeros(query_acc.shape, f32)
    key_acc[...] = jnp.zeros(key_acc.shape, f32)
    value_acc[...] = jnp.zeros(value_acc.shape, f32)
    for copy in copies:
        copy.wait()
    for h in range(HEADS_HERE):
        keys_t[head_of(h), :] = turned(keys[:, head_of(h)])

    def step(group, carry):
        for i in range(2):
            base = bases[i]
            span = span_of(i)

            def block(offset_row, span=span, base=base):
                for h in range(HEADS_HERE):
                    query = group_query(rows, ctx_index, group, h)
                    grad_t = group_grad(rows, ctx_index, group, h)
                    scores = mm(keys[span, head_of(h)], query, NT) * LOG2_SCALE
                    scores = masked(scores - stats[group, h : h + 1, :], base, offset_row)
                    probs = jnp.exp2(scores)
                    prob_grad = mm(values[span, head_of(h)], grad_t)
                    delta = stats[group, h + 2 : h + 3, :]
                    score_grad = (probs * (prob_grad - delta) * SCORE_SCALE).astype(bf16)
                    value_acc[span, head_of(h)] += mm(probs.astype(bf16), grad_t, NT)
                    key_acc[span, head_of(h)] += mm(score_grad, query)
                    query_acc[group, head_of(h), :] += mm(keys_t[head_of(h), span], score_grad)

            visit(bounds, base, offsets, group, block)

        return carry

    lax.fori_loop(0, GROUPS, step, 0)
    both[:FEATURES, :] = turned(key_acc[...])
    both[FEATURES:, :] = turned(value_acc[...])
    for group in range(GROUPS):
        split_parity(ctx_index & 1, group, query_acc[group], mine, other)


def weight_body(*refs):
    both, mine, other = refs[TP_DEVICES:]
    flipped = (ctx_place() & 1) == 1
    for r in range(TP_DEVICES):
        terms = mm(both[...], refs[r][...])
        place = tp_place() ^ r
        low, high = terms[:, :ROWS], terms[:, ROWS:]
        mine[place] = jnp.where(flipped, high, low)
        other[place] = jnp.where(flipped, low, high).astype(bf16)


def add_body(own, received, out):
    out[...] = (own[...] + received[...].astype(f32)).astype(bf16)


def spread_z_body(own, received, kept, one, two, three):
    z = ctx_place() >> 2
    for y in range(2):
        place = 2 * z + y
        kept[y] = own[place] + received[place].astype(f32)
        for code, out in ((1, one), (2, two), (3, three)):
            place = 2 * (z ^ code) + y
            out[y] = (own[place] + received[place].astype(f32)).astype(bf16)


def spread_y_body(own, one, two, three, kept, sent):
    y = (ctx_place() >> 1) & 1
    for place, out in ((y, kept), (1 - y, sent)):
        total = own[place]
        for term in (one, two, three):
            total += term[place].astype(f32)
        out[...] = total.astype(out.dtype)


def weighted_sum(blocks):
    heads = []
    for h in range(HEADS_HERE):
        levels = []
        for i in range(CTX_DEVICES):
            pieces = blocks[i, FEATURES:, :].astype(f32)[3 * h : 3 * h + 3]
            levels.append(pieces[0:1] + pieces[1:2] + pieces[2:3])
        top = levels[0]
        for level in levels[1:]:
            top = jnp.maximum(top, level)
        weights = [jnp.exp2(level - top) for level in levels]
        scale = 1.0 / sum(weights)
        total = jnp.zeros((HEAD_DIM, ROWS), f32)
        for i in range(CTX_DEVICES):
            total += weights[i] * blocks[i, head_of(h), :].astype(f32)
        heads.append(total * scale)
    return jnp.concatenate(heads, axis=0)


def total_of(terms):
    total = terms[0].astype(f32)
    for i in range(1, terms.shape[0]):
        total = total + terms[i].astype(f32)
    return total


def close_body(w_out, w_query, attended_terms, query_kept, query_rest, *outs):
    attended = weighted_sum(attended_terms).T.astype(bf16)
    query_grad = (query_kept[...] + query_rest[...].astype(f32)).T.astype(bf16)
    for y in range(2):
        for x in range(4):
            part = pl.ds(shard_start(tp_place(), 4 * y + x), FEATURES)
            cross = mm(attended, w_out[:, part])
            latent = mm(query_grad, w_query[part, :], NT)
            for half, terms in ((0, cross), (1, latent)):
                stays = KEPT_PEERS[half]
                out = outs[2 * half + (x not in stays)]
                place = (stays if x in stays else SENT_PEERS[half]).index(x)
                out[place, y] = terms.astype(out.dtype)


def fold_body(*refs):
    for half in range(2):
        stays, came = refs[2 * half : 2 * half + 2]
        kept, sent = refs[4 + 2 * half : 6 + 2 * half]
        kept[...] = stays[0] + came[0].astype(f32)
        sent[...] = (stays[1] + came[1].astype(f32)).astype(bf16)


def fold_last_body(cross, cross_came, latent, latent_came, kept, sent):
    for half, (own, came) in enumerate(((cross, cross_came), (latent, latent_came))):
        columns = slice(half * FEATURES, (half + 1) * FEATURES)
        kept[:, columns] = own[0] + came[0].astype(f32)
        sent[:, columns] = (own[1] + came[1].astype(f32)).astype(bf16)


def last_body(kept, rest, terms, cross_out, latent_grad, key_grad, value_grad):
    total = (kept[...] + rest[...].astype(f32)).astype(bf16)
    cross_out[...] = total[:, :FEATURES]
    latent_grad[...] = total[:, FEATURES:]
    total = total_of(terms).T
    key_grad[...] = total[:, :FEATURES]
    value_grad[...] = total[:, FEATURES:]


def shards(token_ids, embed_table, latents, w_query, w_key, w_value, w_out, out_grad, offsets):
    mirror_ids = swap(token_ids[SPAN:], "ctx", MIRROR)
    offset_lanes = offsets.reshape(CTX_DEVICES, ROWS)

    row_part = jnp.concatenate([latents, out_grad], axis=0)
    row_part, mirror_ids = lax.optimization_barrier((row_part, mirror_ids))
    far_rows = [swap(row_part, "tp", r) for r in (2, 4, 5, 6, 7)]
    ids = jnp.concatenate([token_ids[:SPAN], mirror_ids])
    context_part = embed_table.at[ids].get(mode="promise_in_bounds")
    far_rows, context_part, row_part = lax.optimization_barrier(
        (far_rows, context_part, row_part)
    )
    near_rows = [swap(row_part, "tp", r) for r in (1, 3)]
    context_side = swap(context_part, "tp", 4)
    near_rows, context_late = lax.optimization_barrier((near_rows, context_part))
    context_first = [swap(context_late, "tp", r) for r in (1, 3)] + [context_side]
    row_blocks = [row_part, near_rows[0], far_rows[0], near_rows[1]] + far_rows[1:]

    own = kernel_call(
        rows_body,
        [((2 * ROWS, FEATURES), bf16)],
        [],
        [w_query, w_out] + row_blocks,
        room=60,
    )[0]
    beside, context_first = lax.optimization_barrier((swap(own, "ctx", 2), context_first))
    near, back, side = context_first
    far, side_near, side_back = lax.optimization_barrier(far_blocks(near, back, side))
    side_far = swap(side_back, "tp", 1)
    chips = [jnp.stack([own, beside])]
    chips += [swap(chips[0], "ctx", code) for code in (4, 8, 12)]
    context = [context_part, near, far, back, side, side_near, side_far, side_back]
    begun = resident_call(
        project_body,
        [((2 * SPAN, 2 * FEATURES), f32)],
        [],
        [w_key, w_value] + [context[r] for r in FIRST_PEERS],
    )[0]
    chips, begun = lax.optimization_barrier((chips, begun))
    rows = both_cores(chips)

    part_shape = (CHIPS, FEATURES, ROWS)
    stats_shape = (GROUPS, 4, GROUP_ROWS)
    span_kind = ((2 * SPAN, FEATURES), bf16)
    stored, local, out_blocks = resident_call(
        forward_body,
        [
            (stats_shape, f32),
            ((CTX_DEVICES, FEATURES + LEVEL_ROWS, ROWS), bf16),
        ],
        [offsets],
        [offset_lanes, rows, w_key, w_value, begun, context[LAST_PEER]],
        far_out=[((STORED,) + span_kind[0], bf16)],
        scratch=[
            pltpu.VMEM(*span_kind),
            pltpu.VMEM(*span_kind),
            pltpu.VMEM((FEATURES, 2 * SPAN), bf16),
            pltpu.VMEM((FEATURES, GROUP_ROWS), f32),
            pltpu.SemaphoreType.DMA((2,)),
        ],
        room=24,
    )

    chip = kernel_call(
        join_body,
        [(stats_shape, f32)],
        [],
        [local] + [swap(local, "ctx", code) for code in (1, 2, 3)],
    )[0]
    chips = [chip] + [swap(chip, "ctx", code) for code in (4, 8, 12)]
    out_blocks, chips = lax.optimization_barrier((out_blocks, chips))
    attended_terms = exchange(out_blocks, "ctx")

    both, own_query, other_query = resident_call(
        backward_body,
        [((2 * FEATURES, 2 * SPAN), bf16), (part_shape, f32), (part_shape, bf16)],
        [offsets],
        [offset_lanes, rows] + chips,
        far_in=[stored],
        scratch=[
            pltpu.VMEM(*span_kind),
            pltpu.VMEM(*span_kind),
            pltpu.VMEM(stats_shape, f32),
            pltpu.VMEM((2 * SPAN, FEATURES), f32),
            pltpu.VMEM((2 * SPAN, FEATURES), f32),
            pltpu.VMEM((FEATURES, 2 * SPAN), bf16),
            pltpu.VMEM((GROUPS, FEATURES, GROUP_ROWS), f32),
            pltpu.SemaphoreType.DMA((2,)),
        ],
        room=28,
    )
    query_shape = (FEATURES, ROWS)
    kept, *sent = kernel_call(
        spread_z_body,
        [((2,) + query_shape, f32)] + [((2,) + query_shape, bf16)] * 3,
        [],
        [own_query, swap(other_query, "ctx", 1)],
    )
    both, sent = lax.optimization_barrier((both, sent))
    arriving = [swap(block, "ctx", 4 * code) for code, block in zip((1, 2, 3), sent)]
    block_shape = (CHIPS, 2 * FEATURES, ROWS)
    own_weight, other_weight = resident_call(
        weight_body,
        [(block_shape, f32), (block_shape, bf16)],
        [],
        context + [both],
    )
    own_weight, other_weight, attended_terms, arriving = lax.optimization_barrier(
        (own_weight, other_weight, attended_terms, arriving)
    )
    query_kept, sent = kernel_call(
        spread_y_body,
        [(query_shape, f32), (query_shape, bf16)],
        [],
        [kept] + arriving,
        room=60,
    )
    weight_blocks = kernel_call(
        add_body,
        [(block_shape, bf16)],
        [],
        [own_weight, swap(other_weight, "ctx", 1)],
    )[0]
    query_rest, weight_blocks = lax.optimization_barrier((swap(sent, "ctx", 2), weight_blocks))
    same_core = [list(range(core, CTX_DEVICES, 2)) for core in range(2)]
    weight_terms = exchange(weight_blocks, "ctx", same_core)
    pair_shape = (2, ROWS, FEATURES)
    four_shape = (2,) + pair_shape
    terms = kernel_call(
        close_body,
        [(four_shape, f32), (four_shape, bf16)] * 2,
        [],
        [w_out, w_query, attended_terms, query_kept, query_rest],
    )
    came = [swap(terms[1], "tp", FIRST_X[0]), swap(terms[3], "tp", FIRST_X[1])]
    cross, cross_sent, latent, latent_sent = kernel_call(
        fold_body,
        [(pair_shape, f32), (pair_shape, bf16)] * 2,
        [],
        [terms[0], came[0], terms[2], came[1]],
    )
    came = [swap(cross_sent, "tp", SECOND_X[0]), swap(latent_sent, "tp", SECOND_X[1])]
    sum_shape = (ROWS, 2 * FEATURES)
    kept, sent = kernel_call(
        fold_last_body,
        [(sum_shape, f32), (sum_shape, bf16)],
        [],
        [cross, came[0], latent, came[1]],
    )
    own_shape = (ROWS, FEATURES)
    return tuple(
        kernel_call(
            last_body,
            [(own_shape, bf16), (own_shape, bf16), (own_shape, f32), (own_shape, f32)],
            [],
            [kept, swap(sent, "tp", 4), weight_terms],
        )
    )


def solution(mesh):
    placed = (
        P("ctx"),
        P(None, "tp"),
        P("ctx", "tp"),
        P(None, "tp"),
        P(None, "tp"),
        P(None, "tp"),
        P("tp", None),
        P("ctx", "tp"),
        P(),
    )
    return jax.shard_map(
        shards,
        mesh=mesh,
        in_specs=placed,
        out_specs=(P("ctx", "tp"), P("ctx", "tp"), P("ctx", "tp"), P("ctx", "tp")),
        check_vma=False,
    )
```

```python
import math

import jax
import jax.numpy as jnp
from jax import lax
from jax.experimental import pallas as pl
from jax.experimental.pallas import tpu as pltpu
from jax.sharding import PartitionSpec as P

HEAD_DIM = 128
CTX_DEVICES = 16
TP_DEVICES = 8
FEATURES = 256
HEADS_HERE = FEATURES // HEAD_DIM
ROWS = 128
LAST_PEER = 6
FIRST_PEERS = (0, 1, 2, 3, 4, 5, 7)
CHIPS = CTX_DEVICES // 2
GROUPS = 4
STORED = 120
FIRST_X, SECOND_X = (1, 3), (3, 1)
KEPT_PEERS = ((0, 3), (0, 1))
SENT_PEERS = ((1, 2), (3, 2))
ROW_ORDER = (6, 7, 5, 2, 4, 3, 1)
MIRROR = 12
LEVEL_ROWS = 16
GROUP_ROWS = 4 * ROWS
SPAN = 512

SCORE_SCALE = 1.0 / math.sqrt(HEAD_DIM)
LOG2_SCALE = SCORE_SCALE * math.log2(math.e)
MASKED = -1e30
FLOOR = -1e29

NN = (((1,), (0,)), ((), ()))
NT = (((1,), (1,)), ((), ()))
TN = (((0,), (0,)), ((), ()))

bf16 = jnp.bfloat16
f32 = jnp.float32


def mm(left, right, dims=NN):
    return lax.dot_general(left, right, dims, preferred_element_type=f32)


def swap(value, axis, bits):
    count = CTX_DEVICES if axis == "ctx" else TP_DEVICES
    return lax.ppermute(value, axis, [(i, i ^ bits) for i in range(count)])


def exchange(value, axis, groups=None):
    return lax.all_to_all(value, axis, 0, 0, axis_index_groups=groups, tiled=True)


def whole(shape):
    return pl.BlockSpec(shape, lambda i: (0,) * len(shape), pipeline_mode=pl.Buffered(1))


def kernel_call(body, outs, scalars, arrays, room=16):
    call = pl.pallas_call(
        body,
        grid=(1,),
        out_shape=[jax.ShapeDtypeStruct(shape, kind) for shape, kind in outs],
        in_specs=[pl.BlockSpec(memory_space=pltpu.SMEM)] * len(scalars)
        + [whole(a.shape) for a in arrays],
        out_specs=[whole(shape) for shape, _ in outs],
        compiler_params=pltpu.CompilerParams(vmem_limit_bytes=room * 1024 * 1024),
        cost_estimate=pl.CostEstimate(flops=0, bytes_accessed=0, transcendentals=0),
    )
    return list(call(*scalars, *arrays))


def resident_call(body, outs, scalars, arrays, far_in=(), far_out=(), scratch=(), room=16, flops=0):
    near, far = pl.BlockSpec(memory_space=pltpu.VMEM), pl.BlockSpec(memory_space=pltpu.HBM)
    call = pl.pallas_call(
        body,
        out_shape=[jax.ShapeDtypeStruct(shape, kind) for shape, kind in [*far_out, *outs]],
        in_specs=[pl.BlockSpec(memory_space=pltpu.SMEM)] * len(scalars)
        + [far] * len(far_in)
        + [near] * len(arrays),
        out_specs=[far] * len(far_out) + [near] * len(outs),
        scratch_shapes=list(scratch),
        compiler_params=pltpu.CompilerParams(vmem_limit_bytes=room * 1024 * 1024),
        cost_estimate=pl.CostEstimate(flops=flops, bytes_accessed=0, transcendentals=0),
    )
    return list(call(*scalars, *far_in, *arrays))


def far_blocks(near, back, side):
    return swap(back, "tp", 1), swap(near, "tp", 4), swap(side, "tp", 3)


def both_cores(chips):
    return jnp.concatenate(chips + [swap(pair, "ctx", 1) for pair in chips], axis=0)


def shard_start(tp_index, r):
    return pl.multiple_of((tp_index ^ r) * FEATURES, FEATURES)


def tp_place():
    return lax.axis_index("tp").astype(jnp.int32)


def ctx_place():
    return lax.axis_index("ctx").astype(jnp.int32)


def key_bases(ctx_index):
    return ctx_index * (2 * SPAN), (ctx_index ^ MIRROR) * (2 * SPAN) + SPAN


def head_of(h):
    return slice(h * HEAD_DIM, (h + 1) * HEAD_DIM)


def rows_body(w_query, w_out, *refs):
    blocks, out = refs[:-1], refs[-1]
    query = jnp.zeros((ROWS, FEATURES), f32)
    grads = [jnp.zeros((HEAD_DIM, ROWS), f32) for _ in range(HEADS_HERE)]
    for r in range(TP_DEVICES):
        part = pl.ds(shard_start(tp_place(), r), FEATURES)
        query += mm(blocks[r][:ROWS, :], w_query[part, :])
        for h in range(HEADS_HERE):
            grads[h] += mm(w_out[head_of(h), part], blocks[r][ROWS:, :], NT)
    out[:ROWS, :] = query.astype(bf16)
    for h in range(HEADS_HERE):
        out[ROWS:, head_of(h)] = grads[h].astype(bf16)


def row_block(rows, ctx_index, block):
    distance = ctx_index ^ block
    return rows.at[(distance & 1) * CHIPS + (distance >> 1)]


def group_query(rows, ctx_index, group, h):
    blocks = [row_block(rows, ctx_index, GROUPS * group + i) for i in range(GROUPS)]
    return jnp.concatenate([block[:ROWS, head_of(h)] for block in blocks], axis=0)


def group_grad(rows, ctx_index, group, h):
    blocks = [row_block(rows, ctx_index, GROUPS * group + i) for i in range(GROUPS)]
    return jnp.concatenate([block[ROWS:, head_of(h)] for block in blocks], axis=1)


def masked(scores, base, offset_row):
    if offset_row is None:
        return scores
    places = base + lax.broadcasted_iota(jnp.int32, (SPAN, GROUP_ROWS), 0)
    return jnp.where(places <= offset_row, scores, MASKED)


def visit(bounds, base, offsets, group, block):
    first, last = bounds[group * GROUP_ROWS], bounds[group * GROUP_ROWS + GROUP_ROWS - 1]
    whole_seen = first >= base + (SPAN - 1)

    @pl.when(whole_seen)
    def _():
        block(None)

    @pl.when(jnp.logical_and(last >= base, jnp.logical_not(whole_seen)))
    def _():
        lanes = [offsets[pl.ds(group * GROUPS + i, 1), :] for i in range(GROUPS)]
        block(jnp.concatenate(lanes, axis=1))


def pieces_of(level):
    pieces = []
    for _ in range(3):
        piece = level.astype(bf16).astype(f32)
        pieces.append(piece)
        level = level - piece
    return pieces


def turned(value):
    return value.astype(f32).T.astype(bf16)


def span_of(i):
    return slice(i * SPAN, (i + 1) * SPAN)


def ordered_rows(weight, tp_index, order):
    return jnp.concatenate(
        [weight[pl.ds(shard_start(tp_index, r), FEATURES), :] for r in order], axis=0
    )


def project_body(w_key, w_value, *refs):
    context = jnp.concatenate([ref[...] for ref in refs[:-1]], axis=1)
    out = refs[-1]
    out[:, :FEATURES] = mm(context, ordered_rows(w_key, tp_place(), FIRST_PEERS))
    out[:, FEATURES:] = mm(context, ordered_rows(w_value, tp_place(), FIRST_PEERS))


def forward_body(bounds, *refs):
    offsets, rows, w_key, w_value, begun, last, stored = refs[:7]
    stats, blocks, keys, values, values_t, parts, copied = refs[7:]
    ctx_index = ctx_place()
    bases = key_bases(ctx_index)
    start = shard_start(tp_place(), LAST_PEER)
    for i, (weight, out) in enumerate(((w_key, keys), (w_value, values))):
        rest = mm(last[...], weight[pl.ds(start, FEATURES), :])
        out[...] = (begun[:, i * FEATURES : (i + 1) * FEATURES] + rest).astype(bf16)
    copies = [
        pltpu.make_async_copy(keys, stored.at[0], copied.at[0]),
        pltpu.make_async_copy(values, stored.at[1], copied.at[1]),
    ]
    for copy in copies:
        copy.start()
    for h in range(HEADS_HERE):
        values_t[head_of(h), :] = turned(values[:, head_of(h)])

    def step(group, carry):
        stats[group, :2, :] = jnp.full((2, GROUP_ROWS), MASKED, f32)
        stats[group, 2:, :] = jnp.zeros((2, GROUP_ROWS), f32)
        parts[...] = jnp.zeros((FEATURES, GROUP_ROWS), f32)
        for i in range(2):
            base = bases[i]

            def block(offset_row, i=i, base=base):
                for h in range(HEADS_HERE):
                    query = group_query(rows, ctx_index, group, h)
                    scores = mm(keys[span_of(i), head_of(h)], query, NT) * LOG2_SCALE
                    scores = masked(scores, base, offset_row)
                    old = stats[group, h : h + 1, :]
                    peak = jnp.maximum(jnp.max(scores, axis=0, keepdims=True), FLOOR)
                    peak = jnp.maximum(peak, old)
                    weights = jnp.exp2(scores - peak)
                    keep = jnp.exp2(old - peak)
                    total = keep * stats[group, h + 2 : h + 3, :]
                    total += jnp.sum(weights, axis=0, keepdims=True)
                    part = mm(values_t[head_of(h), span_of(i)], weights.astype(bf16))
                    parts[head_of(h), :] = keep * parts[head_of(h), :] + part
                    stats[group, h : h + 1, :] = peak
                    stats[group, h + 2 : h + 3, :] = total

            visit(bounds, base, offsets, group, block)

        levels = []
        for h in range(HEADS_HERE):
            total = stats[group, h + 2 : h + 3, :]
            some = total > 0.0
            safe = jnp.where(some, total, 1.0)
            part = parts[head_of(h), :] * jnp.where(some, 1.0 / safe, 0.0)
            grad_t = group_grad(rows, ctx_index, group, h).astype(f32)
            level = jnp.where(some, stats[group, h : h + 1, :] + jnp.log2(safe), MASKED)
            stats[group, h : h + 1, :] = level
            stats[group, h + 2 : h + 3, :] = jnp.sum(part * grad_t, axis=0, keepdims=True)
            levels += pieces_of(level)
            for i in range(GROUPS):
                place = GROUPS * group + i
                lanes = slice(i * ROWS, (i + 1) * ROWS)
                blocks[place, head_of(h), :] = part[:, lanes].astype(bf16)
        levels.append(jnp.zeros((LEVEL_ROWS - len(levels), GROUP_ROWS), f32))
        levels = jnp.concatenate(levels, axis=0).astype(bf16)
        for i in range(GROUPS):
            place = GROUPS * group + i
            blocks[place, FEATURES:, :] = levels[:, i * ROWS : (i + 1) * ROWS]
        return carry

    lax.fori_loop(0, GROUPS, step, 0)
    for copy in copies:
        copy.wait()


def joined(refs, group):
    pieces = [ref[group] for ref in refs]
    top = pieces[0][:2]
    for piece in pieces[1:]:
        top = jnp.maximum(top, piece[:2])
    total = jnp.zeros((2, GROUP_ROWS), f32)
    delta = jnp.zeros((2, GROUP_ROWS), f32)
    for piece in pieces:
        weight = jnp.exp2(piece[:2] - top)
        total += weight
        delta += weight * piece[2:]
    return top + jnp.log2(total), delta / total


def join_body(own, one, two, three, stats):
    for group in range(GROUPS):
        level, delta = joined((own, one, two, three), group)
        stats[group, :2, :] = level
        stats[group, 2:, :] = delta


def split_parity(core, group, value, mine, other):
    for i in range(GROUPS // 2):
        low = value[:, 2 * i * ROWS : (2 * i + 1) * ROWS]
        high = value[:, (2 * i + 1) * ROWS : (2 * i + 2) * ROWS]
        chip = group * (GROUPS // 2) + i
        mine[chip] = jnp.where(core == 1, high, low)
        other[chip] = jnp.where(core == 1, low, high).astype(bf16)


def backward_body(bounds, *refs):
    stored, offsets, rows, own, one, two, three, both, mine, other = refs[:10]
    keys, values, stats, key_acc, value_acc, keys_t, query_acc, copied = refs[10:]
    copies = [
        pltpu.make_async_copy(stored.at[0], keys, copied.at[0]),
        pltpu.make_async_copy(stored.at[1], values, copied.at[1]),
    ]
    for copy in copies:
        copy.start()
    for group in range(GROUPS):
        level, delta = joined((own, one, two, three), group)
        stats[group, :2, :] = level
        stats[group, 2:, :] = delta
    ctx_index = ctx_place()
    bases = key_bases(ctx_index)
    query_acc[...] = jnp.zeros(query_acc.shape, f32)
    key_acc[...] = jnp.zeros(key_acc.shape, f32)
    value_acc[...] = jnp.zeros(value_acc.shape, f32)
    for copy in copies:
        copy.wait()
    for h in range(HEADS_HERE):
        keys_t[head_of(h), :] = turned(keys[:, head_of(h)])

    def step(group, carry):
        for i in range(2):
            base = bases[i]
            span = span_of(i)

            def block(offset_row, span=span, base=base):
                for h in range(HEADS_HERE):
                    query = group_query(rows, ctx_index, group, h)
                    grad_t = group_grad(rows, ctx_index, group, h)
                    scores = mm(keys[span, head_of(h)], query, NT) * LOG2_SCALE
                    scores = masked(scores - stats[group, h : h + 1, :], base, offset_row)
                    probs = jnp.exp2(scores)
                    prob_grad = mm(values[span, head_of(h)], grad_t)
                    delta = stats[group, h + 2 : h + 3, :]
                    score_grad = (probs * (prob_grad - delta) * SCORE_SCALE).astype(bf16)
                    value_acc[span, head_of(h)] += mm(probs.astype(bf16), grad_t, NT)
                    key_acc[span, head_of(h)] += mm(score_grad, query)
                    query_acc[group, head_of(h), :] += mm(keys_t[head_of(h), span], score_grad)

            visit(bounds, base, offsets, group, block)

        return carry

    lax.fori_loop(0, GROUPS, step, 0)
    both[:FEATURES, :] = turned(key_acc[...])
    both[FEATURES:, :] = turned(value_acc[...])
    for group in range(GROUPS):
        split_parity(ctx_index & 1, group, query_acc[group], mine, other)


def weight_body(*refs):
    both, mine, other = refs[TP_DEVICES:]
    flipped = (ctx_place() & 1) == 1
    for r in range(TP_DEVICES):
        terms = mm(both[...], refs[r][...])
        place = tp_place() ^ r
        low, high = terms[:, :ROWS], terms[:, ROWS:]
        mine[place] = jnp.where(flipped, high, low)
        other[place] = jnp.where(flipped, low, high).astype(bf16)


def add_body(own, received, out):
    out[...] = (own[...] + received[...].astype(f32)).astype(bf16)


def spread_z_body(own, received, kept, one, two, three):
    z = ctx_place() >> 2
    for y in range(2):
        place = 2 * z + y
        kept[y] = own[place] + received[place].astype(f32)
        for code, out in ((1, one), (2, two), (3, three)):
            place = 2 * (z ^ code) + y
            out[y] = (own[place] + received[place].astype(f32)).astype(bf16)


def spread_y_body(own, one, two, three, kept, sent):
    y = (ctx_place() >> 1) & 1
    for place, out in ((y, kept), (1 - y, sent)):
        total = own[place]
        for term in (one, two, three):
            total += term[place].astype(f32)
        out[...] = total.astype(out.dtype)


def weighted_sum(blocks):
    heads = []
    for h in range(HEADS_HERE):
        levels = []
        for i in range(CTX_DEVICES):
            pieces = blocks[i, FEATURES:, :].astype(f32)[3 * h : 3 * h + 3]
            levels.append(pieces[0:1] + pieces[1:2] + pieces[2:3])
        top = levels[0]
        for level in levels[1:]:
            top = jnp.maximum(top, level)
        weights = [jnp.exp2(level - top) for level in levels]
        scale = 1.0 / sum(weights)
        total = jnp.zeros((HEAD_DIM, ROWS), f32)
        for i in range(CTX_DEVICES):
            total += weights[i] * blocks[i, head_of(h), :].astype(f32)
        heads.append(total * scale)
    return jnp.concatenate(heads, axis=0)


def total_of(terms):
    total = terms[0].astype(f32)
    for i in range(1, terms.shape[0]):
        total = total + terms[i].astype(f32)
    return total


def close_body(w_out, w_query, attended_terms, query_kept, query_rest, *outs):
    attended = weighted_sum(attended_terms).T.astype(bf16)
    query_grad = (query_kept[...] + query_rest[...].astype(f32)).T.astype(bf16)
    for y in range(2):
        for x in range(4):
            part = pl.ds(shard_start(tp_place(), 4 * y + x), FEATURES)
            cross = mm(attended, w_out[:, part])
            latent = mm(query_grad, w_query[part, :], NT)
            for half, terms in ((0, cross), (1, latent)):
                stays = KEPT_PEERS[half]
                out = outs[2 * half + (x not in stays)]
                place = (stays if x in stays else SENT_PEERS[half]).index(x)
                out[place, y] = terms.astype(out.dtype)


def fold_body(*refs):
    for half in range(2):
        stays, came = refs[2 * half : 2 * half + 2]
        kept, sent = refs[4 + 2 * half : 6 + 2 * half]
        kept[...] = stays[0] + came[0].astype(f32)
        sent[...] = (stays[1] + came[1].astype(f32)).astype(bf16)


def fold_last_body(cross, cross_came, latent, latent_came, kept, sent):
    for half, (own, came) in enumerate(((cross, cross_came), (latent, latent_came))):
        columns = slice(half * FEATURES, (half + 1) * FEATURES)
        kept[:, columns] = own[0] + came[0].astype(f32)
        sent[:, columns] = (own[1] + came[1].astype(f32)).astype(bf16)


def last_body(kept, rest, terms, cross_out, latent_grad, key_grad, value_grad):
    total = (kept[...] + rest[...].astype(f32)).astype(bf16)
    cross_out[...] = total[:, :FEATURES]
    latent_grad[...] = total[:, FEATURES:]
    total = total_of(terms).T
    key_grad[...] = total[:, :FEATURES]
    value_grad[...] = total[:, FEATURES:]


def shards(token_ids, embed_table, latents, w_query, w_key, w_value, w_out, out_grad, offsets):
    mirror_ids = swap(token_ids[SPAN:], "ctx", MIRROR)
    offset_lanes = offsets.reshape(CTX_DEVICES, ROWS)

    row_part = jnp.concatenate([latents, out_grad], axis=0)
    row_part, mirror_ids = lax.optimization_barrier((row_part, mirror_ids))
    row_blocks = [swap(row_part, "tp", r) for r in ROW_ORDER]
    ids = jnp.concatenate([token_ids[:SPAN], mirror_ids])
    context_part = embed_table.at[ids].get(mode="promise_in_bounds")
    row_blocks, context_part = lax.optimization_barrier((row_blocks, context_part))
    row_blocks = [row_part] + [row_blocks[ROW_ORDER.index(r)] for r in range(1, TP_DEVICES)]
    context_first = [swap(context_part, "tp", bits) for bits in (1, 3, 4)]

    own = kernel_call(
        rows_body,
        [((2 * ROWS, FEATURES), bf16)],
        [],
        [w_query, w_out] + row_blocks,
        room=60,
    )[0]
    beside, context_first = lax.optimization_barrier((swap(own, "ctx", 2), context_first))
    near, back, side = context_first
    far, side_near, side_back = lax.optimization_barrier(far_blocks(near, back, side))
    side_far = swap(side_back, "tp", 1)
    chips = [jnp.stack([own, beside])]
    chips += [swap(chips[0], "ctx", code) for code in (4, 12, 8)]
    context = [context_part, near, far, back, side, side_near, side_far, side_back]
    begun = resident_call(
        project_body,
        [((2 * SPAN, 2 * FEATURES), f32)],
        [],
        [w_key, w_value] + [context[r] for r in FIRST_PEERS],
    )[0]
    chips, begun = lax.optimization_barrier((chips, begun))
    rows = both_cores([chips[0], chips[1], chips[3], chips[2]])

    part_shape = (CHIPS, FEATURES, ROWS)
    stats_shape = (GROUPS, 4, GROUP_ROWS)
    span_kind = ((2 * SPAN, FEATURES), bf16)
    stored, local, out_blocks = resident_call(
        forward_body,
        [
            (stats_shape, f32),
            ((CTX_DEVICES, FEATURES + LEVEL_ROWS, ROWS), bf16),
        ],
        [offsets],
        [offset_lanes, rows, w_key, w_value, begun, context[LAST_PEER]],
        far_out=[((STORED,) + span_kind[0], bf16)],
        scratch=[
            pltpu.VMEM(*span_kind),
            pltpu.VMEM(*span_kind),
            pltpu.VMEM((FEATURES, 2 * SPAN), bf16),
            pltpu.VMEM((FEATURES, GROUP_ROWS), f32),
            pltpu.SemaphoreType.DMA((2,)),
        ],
        room=24,
    )

    chip = kernel_call(
        join_body,
        [(stats_shape, f32)],
        [],
        [local] + [swap(local, "ctx", code) for code in (1, 2, 3)],
    )[0]
    chips = [chip] + [swap(chip, "ctx", code) for code in (4, 12, 8)]
    out_blocks, chips = lax.optimization_barrier((out_blocks, chips))
    attended_terms = exchange(out_blocks, "ctx")

    both, own_query, other_query = resident_call(
        backward_body,
        [((2 * FEATURES, 2 * SPAN), bf16), (part_shape, f32), (part_shape, bf16)],
        [offsets],
        [offset_lanes, rows] + chips,
        far_in=[stored],
        scratch=[
            pltpu.VMEM(*span_kind),
            pltpu.VMEM(*span_kind),
            pltpu.VMEM(stats_shape, f32),
            pltpu.VMEM((2 * SPAN, FEATURES), f32),
            pltpu.VMEM((2 * SPAN, FEATURES), f32),
            pltpu.VMEM((FEATURES, 2 * SPAN), bf16),
            pltpu.VMEM((GROUPS, FEATURES, GROUP_ROWS), f32),
            pltpu.SemaphoreType.DMA((2,)),
        ],
        room=28,
    )
    query_shape = (FEATURES, ROWS)
    kept, *sent = kernel_call(
        spread_z_body,
        [((2,) + query_shape, f32)] + [((2,) + query_shape, bf16)] * 3,
        [],
        [own_query, swap(other_query, "ctx", 1)],
    )
    both, sent = lax.optimization_barrier((both, sent))
    arriving = [swap(sent[code - 1], "ctx", 4 * code) for code in (2, 1, 3)]
    block_shape = (CHIPS, 2 * FEATURES, ROWS)
    own_weight, other_weight = resident_call(
        weight_body,
        [(block_shape, f32), (block_shape, bf16)],
        [],
        context + [both],
    )
    own_weight, other_weight, attended_terms, arriving = lax.optimization_barrier(
        (own_weight, other_weight, attended_terms, arriving)
    )
    query_kept, sent = kernel_call(
        spread_y_body,
        [(query_shape, f32), (query_shape, bf16)],
        [],
        [kept] + arriving,
        room=60,
    )
    weight_blocks = kernel_call(
        add_body,
        [(block_shape, bf16)],
        [],
        [own_weight, swap(other_weight, "ctx", 1)],
    )[0]
    query_rest, weight_blocks = lax.optimization_barrier((swap(sent, "ctx", 2), weight_blocks))
    same_core = [list(range(core, CTX_DEVICES, 2)) for core in range(2)]
    weight_terms = exchange(weight_blocks, "ctx", same_core)
    pair_shape = (2, ROWS, FEATURES)
    four_shape = (2,) + pair_shape
    terms = kernel_call(
        close_body,
        [(four_shape, f32), (four_shape, bf16)] * 2,
        [],
        [w_out, w_query, attended_terms, query_kept, query_rest],
    )
    came = [swap(terms[1], "tp", FIRST_X[0]), swap(terms[3], "tp", FIRST_X[1])]
    cross, cross_sent, latent, latent_sent = kernel_call(
        fold_body,
        [(pair_shape, f32), (pair_shape, bf16)] * 2,
        [],
        [terms[0], came[0], terms[2], came[1]],
    )
    came = [swap(cross_sent, "tp", SECOND_X[0]), swap(latent_sent, "tp", SECOND_X[1])]
    sum_shape = (ROWS, 2 * FEATURES)
    kept, sent = kernel_call(
        fold_last_body,
        [(sum_shape, f32), (sum_shape, bf16)],
        [],
        [cross, came[0], latent, came[1]],
    )
    own_shape = (ROWS, FEATURES)
    return tuple(
        kernel_call(
            last_body,
            [(own_shape, bf16), (own_shape, bf16), (own_shape, f32), (own_shape, f32)],
            [],
            [kept, swap(sent, "tp", 4), weight_terms],
        )
    )


def solution(mesh):
    placed = (
        P("ctx"),
        P(None, "tp"),
        P("ctx", "tp"),
        P(None, "tp"),
        P(None, "tp"),
        P(None, "tp"),
        P("tp", None),
        P("ctx", "tp"),
        P(),
    )
    return jax.shard_map(
        shards,
        mesh=mesh,
        in_specs=placed,
        out_specs=(P("ctx", "tp"), P("ctx", "tp"), P("ctx", "tp"), P("ctx", "tp")),
        check_vma=False,
    )
```

```python
import math

import jax
import jax.numpy as jnp
from jax import lax
from jax.experimental import pallas as pl
from jax.experimental.pallas import tpu as pltpu
from jax.sharding import PartitionSpec as P

HEAD_DIM = 128
CTX_DEVICES = 16
TP_DEVICES = 8
FEATURES = 256
HEADS_HERE = FEATURES // HEAD_DIM
ROWS = 128
LAST_PEER = 6
FIRST_PEERS = (0, 1, 2, 3, 4, 5, 7)
CHIPS = CTX_DEVICES // 2
GROUPS = 4
STORED = 120
FIRST_X, SECOND_X = (1, 3), (3, 1)
KEPT_PEERS = ((0, 3), (0, 1))
SENT_PEERS = ((1, 2), (3, 2))
ROW_ORDER = (3, 2, 4, 5, 6, 7, 1)
MIRROR = 12
LEVEL_ROWS = 16
GROUP_ROWS = 4 * ROWS
SPAN = 512

SCORE_SCALE = 1.0 / math.sqrt(HEAD_DIM)
LOG2_SCALE = SCORE_SCALE * math.log2(math.e)
MASKED = -1e30
FLOOR = -1e29

NN = (((1,), (0,)), ((), ()))
NT = (((1,), (1,)), ((), ()))
TN = (((0,), (0,)), ((), ()))

bf16 = jnp.bfloat16
f32 = jnp.float32


def mm(left, right, dims=NN):
    return lax.dot_general(left, right, dims, preferred_element_type=f32)


def swap(value, axis, bits):
    count = CTX_DEVICES if axis == "ctx" else TP_DEVICES
    return lax.ppermute(value, axis, [(i, i ^ bits) for i in range(count)])


def exchange(value, axis, groups=None):
    return lax.all_to_all(value, axis, 0, 0, axis_index_groups=groups, tiled=True)


def whole(shape):
    return pl.BlockSpec(shape, lambda i: (0,) * len(shape), pipeline_mode=pl.Buffered(1))


def kernel_call(body, outs, scalars, arrays, room=16):
    call = pl.pallas_call(
        body,
        grid=(1,),
        out_shape=[jax.ShapeDtypeStruct(shape, kind) for shape, kind in outs],
        in_specs=[pl.BlockSpec(memory_space=pltpu.SMEM)] * len(scalars)
        + [whole(a.shape) for a in arrays],
        out_specs=[whole(shape) for shape, _ in outs],
        compiler_params=pltpu.CompilerParams(vmem_limit_bytes=room * 1024 * 1024),
        cost_estimate=pl.CostEstimate(flops=0, bytes_accessed=0, transcendentals=0),
    )
    return list(call(*scalars, *arrays))


def resident_call(body, outs, scalars, arrays, far_in=(), far_out=(), scratch=(), room=16, flops=0):
    near, far = pl.BlockSpec(memory_space=pltpu.VMEM), pl.BlockSpec(memory_space=pltpu.HBM)
    call = pl.pallas_call(
        body,
        out_shape=[jax.ShapeDtypeStruct(shape, kind) for shape, kind in [*far_out, *outs]],
        in_specs=[pl.BlockSpec(memory_space=pltpu.SMEM)] * len(scalars)
        + [far] * len(far_in)
        + [near] * len(arrays),
        out_specs=[far] * len(far_out) + [near] * len(outs),
        scratch_shapes=list(scratch),
        compiler_params=pltpu.CompilerParams(vmem_limit_bytes=room * 1024 * 1024),
        cost_estimate=pl.CostEstimate(flops=flops, bytes_accessed=0, transcendentals=0),
    )
    return list(call(*scalars, *far_in, *arrays))


def far_blocks(near, back, side):
    return swap(back, "tp", 1), swap(near, "tp", 4), swap(side, "tp", 3)


def both_cores(chips):
    return jnp.concatenate(chips + [swap(pair, "ctx", 1) for pair in chips], axis=0)


def shard_start(tp_index, r):
    return pl.multiple_of((tp_index ^ r) * FEATURES, FEATURES)


def tp_place():
    return lax.axis_index("tp").astype(jnp.int32)


def ctx_place():
    return lax.axis_index("ctx").astype(jnp.int32)


def key_bases(ctx_index):
    return ctx_index * (2 * SPAN), (ctx_index ^ MIRROR) * (2 * SPAN) + SPAN


def head_of(h):
    return slice(h * HEAD_DIM, (h + 1) * HEAD_DIM)


def rows_body(w_query, w_out, *refs):
    blocks, out = refs[:-1], refs[-1]
    query = jnp.zeros((ROWS, FEATURES), f32)
    grads = [jnp.zeros((HEAD_DIM, ROWS), f32) for _ in range(HEADS_HERE)]
    for r in range(TP_DEVICES):
        part = pl.ds(shard_start(tp_place(), r), FEATURES)
        query += mm(blocks[r][:ROWS, :], w_query[part, :])
        for h in range(HEADS_HERE):
            grads[h] += mm(w_out[head_of(h), part], blocks[r][ROWS:, :], NT)
    out[:ROWS, :] = query.astype(bf16)
    for h in range(HEADS_HERE):
        out[ROWS:, head_of(h)] = grads[h].astype(bf16)


def row_block(rows, ctx_index, block):
    distance = ctx_index ^ block
    return rows.at[(distance & 1) * CHIPS + (distance >> 1)]


def group_query(rows, ctx_index, group, h):
    blocks = [row_block(rows, ctx_index, GROUPS * group + i) for i in range(GROUPS)]
    return jnp.concatenate([block[:ROWS, head_of(h)] for block in blocks], axis=0)


def group_grad(rows, ctx_index, group, h):
    blocks = [row_block(rows, ctx_index, GROUPS * group + i) for i in range(GROUPS)]
    return jnp.concatenate([block[ROWS:, head_of(h)] for block in blocks], axis=1)


def masked(scores, base, offset_row):
    if offset_row is None:
        return scores
    places = base + lax.broadcasted_iota(jnp.int32, (SPAN, GROUP_ROWS), 0)
    return jnp.where(places <= offset_row, scores, MASKED)


def visit(bounds, base, offsets, group, block):
    first, last = bounds[group * GROUP_ROWS], bounds[group * GROUP_ROWS + GROUP_ROWS - 1]
    whole_seen = first >= base + (SPAN - 1)

    @pl.when(whole_seen)
    def _():
        block(None)

    @pl.when(jnp.logical_and(last >= base, jnp.logical_not(whole_seen)))
    def _():
        lanes = [offsets[pl.ds(group * GROUPS + i, 1), :] for i in range(GROUPS)]
        block(jnp.concatenate(lanes, axis=1))


def pieces_of(level):
    pieces = []
    for _ in range(3):
        piece = level.astype(bf16).astype(f32)
        pieces.append(piece)
        level = level - piece
    return pieces


def turned(value):
    return value.astype(f32).T.astype(bf16)


def span_of(i):
    return slice(i * SPAN, (i + 1) * SPAN)


def ordered_rows(weight, tp_index, order):
    return jnp.concatenate(
        [weight[pl.ds(shard_start(tp_index, r), FEATURES), :] for r in order], axis=0
    )


def project_body(w_key, w_value, *refs):
    context = jnp.concatenate([ref[...] for ref in refs[:-1]], axis=1)
    out = refs[-1]
    out[:, :FEATURES] = mm(context, ordered_rows(w_key, tp_place(), FIRST_PEERS))
    out[:, FEATURES:] = mm(context, ordered_rows(w_value, tp_place(), FIRST_PEERS))


def forward_body(bounds, *refs):
    offsets, rows, w_key, w_value, begun, last, stored = refs[:7]
    stats, blocks, keys, values, values_t, parts, copied = refs[7:]
    ctx_index = ctx_place()
    bases = key_bases(ctx_index)
    start = shard_start(tp_place(), LAST_PEER)
    for i, (weight, out) in enumerate(((w_key, keys), (w_value, values))):
        rest = mm(last[...], weight[pl.ds(start, FEATURES), :])
        out[...] = (begun[:, i * FEATURES : (i + 1) * FEATURES] + rest).astype(bf16)
    copies = [
        pltpu.make_async_copy(keys, stored.at[0], copied.at[0]),
        pltpu.make_async_copy(values, stored.at[1], copied.at[1]),
    ]
    for copy in copies:
        copy.start()
    for h in range(HEADS_HERE):
        values_t[head_of(h), :] = turned(values[:, head_of(h)])

    def step(group, carry):
        stats[group, :2, :] = jnp.full((2, GROUP_ROWS), MASKED, f32)
        stats[group, 2:, :] = jnp.zeros((2, GROUP_ROWS), f32)
        parts[...] = jnp.zeros((FEATURES, GROUP_ROWS), f32)
        for i in range(2):
            base = bases[i]

            def block(offset_row, i=i, base=base):
                for h in range(HEADS_HERE):
                    query = group_query(rows, ctx_index, group, h)
                    scores = mm(keys[span_of(i), head_of(h)], query, NT) * LOG2_SCALE
                    scores = masked(scores, base, offset_row)
                    old = stats[group, h : h + 1, :]
                    peak = jnp.maximum(jnp.max(scores, axis=0, keepdims=True), FLOOR)
                    peak = jnp.maximum(peak, old)
                    weights = jnp.exp2(scores - peak)
                    keep = jnp.exp2(old - peak)
                    total = keep * stats[group, h + 2 : h + 3, :]
                    total += jnp.sum(weights, axis=0, keepdims=True)
                    part = mm(values_t[head_of(h), span_of(i)], weights.astype(bf16))
                    parts[head_of(h), :] = keep * parts[head_of(h), :] + part
                    stats[group, h : h + 1, :] = peak
                    stats[group, h + 2 : h + 3, :] = total

            visit(bounds, base, offsets, group, block)

        levels = []
        for h in range(HEADS_HERE):
            total = stats[group, h + 2 : h + 3, :]
            some = total > 0.0
            safe = jnp.where(some, total, 1.0)
            part = parts[head_of(h), :] * jnp.where(some, 1.0 / safe, 0.0)
            grad_t = group_grad(rows, ctx_index, group, h).astype(f32)
            level = jnp.where(some, stats[group, h : h + 1, :] + jnp.log2(safe), MASKED)
            stats[group, h : h + 1, :] = level
            stats[group, h + 2 : h + 3, :] = jnp.sum(part * grad_t, axis=0, keepdims=True)
            levels += pieces_of(level)
            for i in range(GROUPS):
                place = GROUPS * group + i
                lanes = slice(i * ROWS, (i + 1) * ROWS)
                blocks[place, head_of(h), :] = part[:, lanes].astype(bf16)
        levels.append(jnp.zeros((LEVEL_ROWS - len(levels), GROUP_ROWS), f32))
        levels = jnp.concatenate(levels, axis=0).astype(bf16)
        for i in range(GROUPS):
            place = GROUPS * group + i
            blocks[place, FEATURES:, :] = levels[:, i * ROWS : (i + 1) * ROWS]
        return carry

    lax.fori_loop(0, GROUPS, step, 0)
    for copy in copies:
        copy.wait()


def joined(refs, group):
    pieces = [ref[group] for ref in refs]
    top = pieces[0][:2]
    for piece in pieces[1:]:
        top = jnp.maximum(top, piece[:2])
    total = jnp.zeros((2, GROUP_ROWS), f32)
    delta = jnp.zeros((2, GROUP_ROWS), f32)
    for piece in pieces:
        weight = jnp.exp2(piece[:2] - top)
        total += weight
        delta += weight * piece[2:]
    return top + jnp.log2(total), delta / total


def join_body(own, one, two, three, stats):
    for group in range(GROUPS):
        level, delta = joined((own, one, two, three), group)
        stats[group, :2, :] = level
        stats[group, 2:, :] = delta


def split_parity(core, group, value, mine, other):
    for i in range(GROUPS // 2):
        low = value[:, 2 * i * ROWS : (2 * i + 1) * ROWS]
        high = value[:, (2 * i + 1) * ROWS : (2 * i + 2) * ROWS]
        chip = group * (GROUPS // 2) + i
        mine[chip] = jnp.where(core == 1, high, low)
        other[chip] = jnp.where(core == 1, low, high).astype(bf16)


def backward_body(bounds, *refs):
    stored, offsets, rows, own, one, two, three, both, mine, other = refs[:10]
    keys, values, stats, key_acc, value_acc, keys_t, query_acc, copied = refs[10:]
    copies = [
        pltpu.make_async_copy(stored.at[0], keys, copied.at[0]),
        pltpu.make_async_copy(stored.at[1], values, copied.at[1]),
    ]
    for copy in copies:
        copy.start()
    for group in range(GROUPS):
        level, delta = joined((own, one, two, three), group)
        stats[group, :2, :] = level
        stats[group, 2:, :] = delta
    ctx_index = ctx_place()
    bases = key_bases(ctx_index)
    query_acc[...] = jnp.zeros(query_acc.shape, f32)
    key_acc[...] = jnp.zeros(key_acc.shape, f32)
    value_acc[...] = jnp.zeros(value_acc.shape, f32)
    for copy in copies:
        copy.wait()
    for h in range(HEADS_HERE):
        keys_t[head_of(h), :] = turned(keys[:, head_of(h)])

    def step(group, carry):
        for i in range(2):
            base = bases[i]
            span = span_of(i)

            def block(offset_row, span=span, base=base):
                for h in range(HEADS_HERE):
                    query = group_query(rows, ctx_index, group, h)
                    grad_t = group_grad(rows, ctx_index, group, h)
                    scores = mm(keys[span, head_of(h)], query, NT) * LOG2_SCALE
                    scores = masked(scores - stats[group, h : h + 1, :], base, offset_row)
                    probs = jnp.exp2(scores)
                    prob_grad = mm(values[span, head_of(h)], grad_t)
                    delta = stats[group, h + 2 : h + 3, :]
                    score_grad = (probs * (prob_grad - delta) * SCORE_SCALE).astype(bf16)
                    value_acc[span, head_of(h)] += mm(probs.astype(bf16), grad_t, NT)
                    key_acc[span, head_of(h)] += mm(score_grad, query)
                    query_acc[group, head_of(h), :] += mm(keys_t[head_of(h), span], score_grad)

            visit(bounds, base, offsets, group, block)

        return carry

    lax.fori_loop(0, GROUPS, step, 0)
    both[:FEATURES, :] = turned(key_acc[...])
    both[FEATURES:, :] = turned(value_acc[...])
    for group in range(GROUPS):
        split_parity(ctx_index & 1, group, query_acc[group], mine, other)


def weight_body(*refs):
    both, mine, other = refs[TP_DEVICES:]
    flipped = (ctx_place() & 1) == 1
    for r in range(TP_DEVICES):
        terms = mm(both[...], refs[r][...])
        place = tp_place() ^ r
        low, high = terms[:, :ROWS], terms[:, ROWS:]
        mine[place] = jnp.where(flipped, high, low)
        other[place] = jnp.where(flipped, low, high).astype(bf16)


def add_body(own, received, out):
    out[...] = (own[...] + received[...].astype(f32)).astype(bf16)


def spread_z_body(own, received, kept, one, two, three):
    z = ctx_place() >> 2
    for y in range(2):
        place = 2 * z + y
        kept[y] = own[place] + received[place].astype(f32)
        for code, out in ((1, one), (2, two), (3, three)):
            place = 2 * (z ^ code) + y
            out[y] = (own[place] + received[place].astype(f32)).astype(bf16)


def spread_y_body(own, one, two, three, kept, sent):
    y = (ctx_place() >> 1) & 1
    for place, out in ((y, kept), (1 - y, sent)):
        total = own[place]
        for term in (one, two, three):
            total += term[place].astype(f32)
        out[...] = total.astype(out.dtype)


def weighted_sum(blocks):
    heads = []
    for h in range(HEADS_HERE):
        levels = []
        for i in range(CTX_DEVICES):
            pieces = blocks[i, FEATURES:, :].astype(f32)[3 * h : 3 * h + 3]
            levels.append(pieces[0:1] + pieces[1:2] + pieces[2:3])
        top = levels[0]
        for level in levels[1:]:
            top = jnp.maximum(top, level)
        weights = [jnp.exp2(level - top) for level in levels]
        scale = 1.0 / sum(weights)
        total = jnp.zeros((HEAD_DIM, ROWS), f32)
        for i in range(CTX_DEVICES):
            total += weights[i] * blocks[i, head_of(h), :].astype(f32)
        heads.append(total * scale)
    return jnp.concatenate(heads, axis=0)


def total_of(terms):
    total = terms[0].astype(f32)
    for i in range(1, terms.shape[0]):
        total = total + terms[i].astype(f32)
    return total


def close_body(w_out, w_query, attended_terms, query_kept, query_rest, *outs):
    attended = weighted_sum(attended_terms).T.astype(bf16)
    query_grad = (query_kept[...] + query_rest[...].astype(f32)).T.astype(bf16)
    for y in range(2):
        for x in range(4):
            part = pl.ds(shard_start(tp_place(), 4 * y + x), FEATURES)
            cross = mm(attended, w_out[:, part])
            latent = mm(query_grad, w_query[part, :], NT)
            for half, terms in ((0, cross), (1, latent)):
                stays = KEPT_PEERS[half]
                out = outs[2 * half + (x not in stays)]
                place = (stays if x in stays else SENT_PEERS[half]).index(x)
                out[place, y] = terms.astype(out.dtype)


def fold_body(*refs):
    for half in range(2):
        stays, came = refs[2 * half : 2 * half + 2]
        kept, sent = refs[4 + 2 * half : 6 + 2 * half]
        kept[...] = stays[0] + came[0].astype(f32)
        sent[...] = (stays[1] + came[1].astype(f32)).astype(bf16)


def fold_last_body(cross, cross_came, latent, latent_came, kept, sent):
    for half, (own, came) in enumerate(((cross, cross_came), (latent, latent_came))):
        columns = slice(half * FEATURES, (half + 1) * FEATURES)
        kept[:, columns] = own[0] + came[0].astype(f32)
        sent[:, columns] = (own[1] + came[1].astype(f32)).astype(bf16)


def last_body(kept, rest, terms, cross_out, latent_grad, key_grad, value_grad):
    total = (kept[...] + rest[...].astype(f32)).astype(bf16)
    cross_out[...] = total[:, :FEATURES]
    latent_grad[...] = total[:, FEATURES:]
    total = total_of(terms).T
    key_grad[...] = total[:, :FEATURES]
    value_grad[...] = total[:, FEATURES:]


def shards(token_ids, embed_table, latents, w_query, w_key, w_value, w_out, out_grad, offsets):
    mirror_ids = swap(token_ids[SPAN:], "ctx", MIRROR)
    offset_lanes = offsets.reshape(CTX_DEVICES, ROWS)

    row_part = jnp.concatenate([latents, out_grad], axis=0)
    row_part, mirror_ids = lax.optimization_barrier((row_part, mirror_ids))
    row_blocks = [swap(row_part, "tp", r) for r in ROW_ORDER]
    ids = jnp.concatenate([token_ids[:SPAN], mirror_ids])
    context_part = embed_table.at[ids].get(mode="promise_in_bounds")
    row_blocks, context_part = lax.optimization_barrier((row_blocks, context_part))
    row_blocks = [row_part] + [row_blocks[ROW_ORDER.index(r)] for r in range(1, TP_DEVICES)]
    context_first = [swap(context_part, "tp", bits) for bits in (1, 3, 4)]

    own = kernel_call(
        rows_body,
        [((2 * ROWS, FEATURES), bf16)],
        [],
        [w_query, w_out] + row_blocks,
        room=60,
    )[0]
    beside, context_first = lax.optimization_barrier((swap(own, "ctx", 2), context_first))
    near, back, side = context_first
    far, side_near, side_back = lax.optimization_barrier(far_blocks(near, back, side))
    side_far = swap(side_back, "tp", 1)
    chips = [jnp.stack([own, beside])]
    chips += [swap(chips[0], "ctx", code) for code in (4, 12, 8)]
    context = [context_part, near, far, back, side, side_near, side_far, side_back]
    begun = resident_call(
        project_body,
        [((2 * SPAN, 2 * FEATURES), f32)],
        [],
        [w_key, w_value] + [context[r] for r in FIRST_PEERS],
    )[0]
    chips, begun = lax.optimization_barrier((chips, begun))
    rows = both_cores([chips[0], chips[1], chips[3], chips[2]])

    part_shape = (CHIPS, FEATURES, ROWS)
    stats_shape = (GROUPS, 4, GROUP_ROWS)
    span_kind = ((2 * SPAN, FEATURES), bf16)
    stored, local, out_blocks = resident_call(
        forward_body,
        [
            (stats_shape, f32),
            ((CTX_DEVICES, FEATURES + LEVEL_ROWS, ROWS), bf16),
        ],
        [offsets],
        [offset_lanes, rows, w_key, w_value, begun, context[LAST_PEER]],
        far_out=[((STORED,) + span_kind[0], bf16)],
        scratch=[
            pltpu.VMEM(*span_kind),
            pltpu.VMEM(*span_kind),
            pltpu.VMEM((FEATURES, 2 * SPAN), bf16),
            pltpu.VMEM((FEATURES, GROUP_ROWS), f32),
            pltpu.SemaphoreType.DMA((2,)),
        ],
        room=24,
    )

    chip = kernel_call(
        join_body,
        [(stats_shape, f32)],
        [],
        [local] + [swap(local, "ctx", code) for code in (1, 2, 3)],
    )[0]
    chips = [chip] + [swap(chip, "ctx", code) for code in (4, 12, 8)]
    out_blocks, chips = lax.optimization_barrier((out_blocks, chips))
    attended_terms = exchange(out_blocks, "ctx")

    both, own_query, other_query = resident_call(
        backward_body,
        [((2 * FEATURES, 2 * SPAN), bf16), (part_shape, f32), (part_shape, bf16)],
        [offsets],
        [offset_lanes, rows] + chips,
        far_in=[stored],
        scratch=[
            pltpu.VMEM(*span_kind),
            pltpu.VMEM(*span_kind),
            pltpu.VMEM(stats_shape, f32),
            pltpu.VMEM((2 * SPAN, FEATURES), f32),
            pltpu.VMEM((2 * SPAN, FEATURES), f32),
            pltpu.VMEM((FEATURES, 2 * SPAN), bf16),
            pltpu.VMEM((GROUPS, FEATURES, GROUP_ROWS), f32),
            pltpu.SemaphoreType.DMA((2,)),
        ],
        room=28,
    )
    query_shape = (FEATURES, ROWS)
    kept, *sent = kernel_call(
        spread_z_body,
        [((2,) + query_shape, f32)] + [((2,) + query_shape, bf16)] * 3,
        [],
        [own_query, swap(other_query, "ctx", 1)],
    )
    both, sent = lax.optimization_barrier((both, sent))
    arriving = [swap(sent[code - 1], "ctx", 4 * code) for code in (2, 1, 3)]
    block_shape = (CHIPS, 2 * FEATURES, ROWS)
    own_weight, other_weight = resident_call(
        weight_body,
        [(block_shape, f32), (block_shape, bf16)],
        [],
        context + [both],
    )
    own_weight, other_weight, attended_terms, arriving = lax.optimization_barrier(
        (own_weight, other_weight, attended_terms, arriving)
    )
    query_kept, sent = kernel_call(
        spread_y_body,
        [(query_shape, f32), (query_shape, bf16)],
        [],
        [kept] + arriving,
        room=60,
    )
    weight_blocks = kernel_call(
        add_body,
        [(block_shape, bf16)],
        [],
        [own_weight, swap(other_weight, "ctx", 1)],
    )[0]
    query_rest, weight_blocks = lax.optimization_barrier((swap(sent, "ctx", 2), weight_blocks))
    same_core = [list(range(core, CTX_DEVICES, 2)) for core in range(2)]
    weight_terms = exchange(weight_blocks, "ctx", same_core)
    pair_shape = (2, ROWS, FEATURES)
    four_shape = (2,) + pair_shape
    terms = kernel_call(
        close_body,
        [(four_shape, f32), (four_shape, bf16)] * 2,
        [],
        [w_out, w_query, attended_terms, query_kept, query_rest],
    )
    came = [swap(terms[1], "tp", FIRST_X[0]), swap(terms[3], "tp", FIRST_X[1])]
    cross, cross_sent, latent, latent_sent = kernel_call(
        fold_body,
        [(pair_shape, f32), (pair_shape, bf16)] * 2,
        [],
        [terms[0], came[0], terms[2], came[1]],
    )
    came = [swap(cross_sent, "tp", SECOND_X[0]), swap(latent_sent, "tp", SECOND_X[1])]
    sum_shape = (ROWS, 2 * FEATURES)
    kept, sent = kernel_call(
        fold_last_body,
        [(sum_shape, f32), (sum_shape, bf16)],
        [],
        [cross, came[0], latent, came[1]],
    )
    own_shape = (ROWS, FEATURES)
    return tuple(
        kernel_call(
            last_body,
            [(own_shape, bf16), (own_shape, bf16), (own_shape, f32), (own_shape, f32)],
            [],
            [kept, swap(sent, "tp", 4), weight_terms],
        )
    )


def solution(mesh):
    placed = (
        P("ctx"),
        P(None, "tp"),
        P("ctx", "tp"),
        P(None, "tp"),
        P(None, "tp"),
        P(None, "tp"),
        P("tp", None),
        P("ctx", "tp"),
        P(),
    )
    return jax.shard_map(
        shards,
        mesh=mesh,
        in_specs=placed,
        out_specs=(P("ctx", "tp"), P("ctx", "tp"), P("ctx", "tp"), P("ctx", "tp")),
        check_vma=False,
    )
```
